32 devices in a mesh: groups: 2 (over y), inst: 4 (over x, core), space: 4 (over z).
Axes of the slice: x: 2, y: 2, z: 4, core: 2. Of those that a mesh axis runs over, the one named last changes fastest.
Arguments:
- flow_state: float32 [8, 6, 256, 256], P(('groups', 'inst'), None, 'space'), parts along dimension 0, may hold values from -0.8 to 3.2, as said below
- cell_volume: float32 [512, 256], P(('groups', 'space')), parts along dimension 0, may hold values from 0.5 to 2
- frequency: float32 [1], replicated, may hold values from 0.5 to 1.5
- block_count: int32 [8], P('groups'), parts along dimension 0, may hold values from 1 to 4, 8 in all
- block_place: int32 [16], P('groups'), parts along dimension 0, may hold values from 0 to 7, each once
- face_links: int32 [16, 2], P('groups'), parts along dimension 0, may hold values from -1 to 7
- face_offset: int32 [16, 2], P('groups'), parts along dimension 0, may hold values from 0 to 255
- face_flip: int32 [16, 2], P('groups'), parts along dimension 0, may hold values from 0 to 1
Outputs:
- new_state: float32 [8, 6, 256, 256], P(('groups', 'inst'), None, 'space'), parts along dimension 0
- last_residual: float32 [8, 6, 256, 256], P(('groups', 'inst'), None, 'space'), parts along dimension 0
The draws below stay inside these ranges and needn't reach their ends.
There are 2 independent parts, one for each index of `groups`. The reference program is written for one: setup_inputs(seed, part) draws one part's arguments, and reference() takes and returns one part's arrays. A program takes and returns all parts, laid end to end along the dimension named above; an argument that names none is the same for every part. Nothing has to cross between parts.
Inputs may be any that keep to these rules, and one draw needn't show every extreme that they name: `block_count`: 8 live blocks in all; some device holds exactly 4. `face_links`: a face link of -1 marks a boundary face. `flow_state`: density lies within 0.75 to 1.25 and energy within 2 to 3.2.
All inputs are finite; a program needn't handle non-finite values.
Results may differ from the reference program's by a relative error of at most 0.00016.
Values sent between devices are 32-bit elements; how exact they have to be, the bound alone decides.
No kernel may reach another device: no remote copies, remote signals or barrier semaphores. Data moves between devices by JAX's collectives and lax.ppermute only.
A program may use at most 64 MiB of HBM per device.

```python
import math
import jax
import jax.numpy as jnp
import numpy as np
from jax import lax

CELLS_J = 256
BLOCKS_MAX = 4
BLOCKS = 8
ROWS = 256
INSTANCES = 4
PSEUDO_STEPS = 2
N_SPACE = 4


def draw_flow_state(key, part):
    key = jax.random.fold_in(key, 11)
    keys = jax.random.split(key, 4)
    shape = (INSTANCES, ROWS, CELLS_J)
    density = 1.0 + 0.1 * jax.random.truncated_normal(keys[0], -2.0, 2.0, shape, jnp.float32)
    momentum = 0.4 * jax.random.truncated_normal(keys[1], -2.0, 2.0, (3,) + shape, jnp.float32)
    energy = 2.6 + 0.3 * jax.random.truncated_normal(keys[2], -2.0, 2.0, shape, jnp.float32)
    turbulence = jnp.exp(jax.random.uniform(keys[3], shape, jnp.float32, -3.0, 0.0))
    stacked = jnp.concatenate([density[None], momentum, energy[None], turbulence[None]], axis=0)
    return jnp.transpose(stacked, (1, 0, 2, 3))


def with_ends(entries, stream_key, low, high):
    dims = entries.shape
    spot = [jax.random.randint(jax.random.fold_in(stream_key, axis), (), 0, dims[axis]) for axis in range(len(dims))]
    entries = entries.at[tuple(spot)].set(low)
    longest = dims.index(max(dims))
    spot[longest] = (spot[longest] + 1) % dims[longest]
    return entries.at[tuple(spot)].set(high)


def block_scale(own_key, shape, cuts, least, largest):
    def one(dim, shards_of):
        steps = jax.random.uniform(jax.random.fold_in(jax.random.fold_in(own_key, 6), dim), (shards_of,), jnp.float32, least / len(cuts), largest / len(cuts))
        return jnp.repeat(jnp.exp(steps), shape[dim] // shards_of).reshape((-1,) + (1,) * (len(shape) - dim - 1))

    level = one(*cuts[0])
    for cut in cuts[1:]:
        level = level * one(*cut)
    return level


def profile(number_of, total, limit, slope):
    loads = [(1 << 20) // math.isqrt(standing ** slope) + 1 for standing in range(2, number_of + 1)]
    surplus, counts = total - limit - (number_of - 1), [1] * (number_of - 1)
    while surplus > 0:
        movable = [i for i in range(number_of - 1) if counts[i] < limit]
        pool, budget = sum([loads[i] for i in movable]), surplus
        for i in movable:
            more = min(limit - counts[i], max(1, budget * loads[i] // pool), surplus)
            counts[i] = counts[i] + more
            surplus = surplus - more
    return np.array([limit] + counts)


def uneven_parts(stream_key, count, total, bound, lean):
    if count == 2:
        one = jax.random.randint(stream_key, (), max(1, total - bound), min(bound, total - 1) + 1)
        return jnp.stack([one, total - one])
    tallies = jnp.asarray(profile(count, total, bound, lean), jnp.int32)
    couples = (count - 1) // 2
    source_of, taker = tallies[1:1 + 2 * couples:2], tallies[2:2 + 2 * couples:2]
    margin = jnp.minimum(source_of - 1, bound - taker)
    shifted = jax.random.randint(jax.random.fold_in(stream_key, 1), (couples,), 0, 1 << 20) % (margin + 1)
    tallies = tallies.at[1:1 + 2 * couples:2].set(source_of - shifted).at[2:2 + 2 * couples:2].set(taker + shifted)
    return tallies[jax.random.permutation(jax.random.fold_in(stream_key, 2), count)]


def setup_inputs(seed: int = 0, part: int = 0) -> dict:
    arg_keys = jax.random.split(jax.random.key(seed), 9)
    part_keys = jax.random.split(jax.random.fold_in(arg_keys[8], part), 9)
    return {
        "flow_state": draw_flow_state(jax.random.fold_in(jax.random.fold_in(arg_keys[8], part), 71), part),
        "cell_volume": jnp.clip(jnp.exp(math.log(2.0) - 1.3862944 * jax.random.uniform(part_keys[1], (ROWS, CELLS_J), jnp.float32) ** block_scale(part_keys[1], (ROWS, CELLS_J), ((0, 4),), -0.2, 0.2)), 0.5, 2.0),
        "frequency": jnp.clip(jax.random.uniform(arg_keys[2], (1,), jnp.float32, 0.5, 1.5), 0.5, 1.5),
        "block_count": uneven_parts(part_keys[3], N_SPACE, BLOCKS, BLOCKS_MAX, 2).astype(jnp.int32),
        "block_place": jax.random.permutation(part_keys[4], BLOCKS).astype(jnp.int32),
        "face_links": with_ends(jax.random.randint(part_keys[5], (BLOCKS, 2), -1, BLOCKS), jax.random.fold_in(part_keys[5], 1), -1, BLOCKS - 1).astype(jnp.int32),
        "face_offset": with_ends(jax.random.randint(part_keys[6], (BLOCKS, 2), 0, CELLS_J), jax.random.fold_in(part_keys[6], 1), 0, CELLS_J - 1).astype(jnp.int32),
        "face_flip": with_ends(jax.random.randint(part_keys[7], (BLOCKS, 2), 0, 2), jax.random.fold_in(part_keys[7], 1), 0, 1).astype(jnp.int32),
    }


HEAT_RATIO = 1.4
SECOND_DISSIPATION = 0.05
FOURTH_DISSIPATION = 0.02
SOUND_SPEED = 1.0
COURANT = 0.5
TIME_VISCOSITY = 0.25


def spectral_matrix(instance_total, omega_value):
    position = jnp.arange(instance_total, dtype=jnp.int32)
    distance = (position[:, None] - position[None, :]) % instance_total
    parity = (1 - 2 * (distance % 2)).astype(jnp.float32)
    phase_angle = jnp.pi * distance.astype(jnp.float32) / instance_total
    safe_angle = jnp.where(distance == 0, 0.5 * jnp.pi, phase_angle)
    first_derivative = jnp.where(distance == 0, 0.0, 0.5 * parity * jnp.cos(safe_angle) / jnp.sin(safe_angle))
    second_derivative = jnp.where(distance == 0, -(instance_total * instance_total + 2) / 12.0,
                                  -parity / (2.0 * jnp.sin(safe_angle) ** 2))
    return omega_value * (first_derivative - TIME_VISCOSITY * second_derivative)


def block_tables(block_count, block_place, face_links, face_offset, face_flip, targets, slot_count, width):
    block_total = block_place.shape[0]
    first_position = (jnp.cumsum(block_count) - block_count).astype(jnp.int32)
    block_at_position = jnp.zeros((block_total,), jnp.int32).at[block_place].set(
        jnp.arange(block_total, dtype=jnp.int32))
    owner_device = jnp.sum((block_place[:, None] >= first_position[None, 1:]).astype(jnp.int32), axis=1).astype(jnp.int32)
    flat_slot = (owner_device * slot_count + block_place - first_position[owner_device]).astype(jnp.int32)
    target_device = targets // slot_count
    target_slot = targets % slot_count
    is_live = target_slot < block_count[target_device]
    block_index = block_at_position[jnp.clip(first_position[target_device] + target_slot, 0, block_total - 1)]
    neighbour = face_links[block_index]
    source_slot = jnp.where(neighbour >= 0, flat_slot[jnp.clip(neighbour, 0, block_total - 1)], -1).astype(jnp.int32)
    column = jnp.arange(width, dtype=jnp.int32)
    flipped = face_flip[block_index][:, :, None]
    ordered = jnp.where(flipped == 1, width - 1 - column, column)
    column_index = ((face_offset[block_index][:, :, None] + ordered) % width).astype(jnp.int32)
    return is_live, source_slot, column_index


def with_halos(blocks, faces, source_slot, column_index):
    comps, slot_count, cells_i, width = blocks.shape
    picked = jnp.take(faces, jnp.clip(source_slot, 0, faces.shape[1] - 1).reshape(-1), axis=1)
    picked = picked.reshape(comps, slot_count, 2, 2, 2, width)
    lower = picked[:, :, 0, 1]
    upper = picked[:, :, 1, 0]
    lower = jnp.take_along_axis(lower, jnp.broadcast_to(column_index[None, :, 0, None, :], lower.shape), axis=3)
    upper = jnp.take_along_axis(upper, jnp.broadcast_to(column_index[None, :, 1, None, :], upper.shape), axis=3)
    lower = jnp.where((source_slot[:, 0] >= 0)[None, :, None, None], lower,
                      jnp.repeat(blocks[:, :, 0:1], 2, axis=2))
    upper = jnp.where((source_slot[:, 1] >= 0)[None, :, None, None], upper,
                      jnp.repeat(blocks[:, :, cells_i - 1:cells_i], 2, axis=2))
    return jnp.concatenate([lower, blocks, upper], axis=2)


def fluxes(conserved):
    inverse_rho = 1.0 / conserved[0]
    velocity_i = conserved[1] * inverse_rho
    velocity_j = conserved[2] * inverse_rho
    pressure = (HEAT_RATIO - 1.0) * (conserved[4] - 0.5 * (conserved[1] * conserved[1] + conserved[2] * conserved[2]
                                                         + conserved[3] * conserved[3]) * inverse_rho)
    flux_i = jnp.stack([conserved[1], conserved[1] * velocity_i + pressure, conserved[2] * velocity_i,
                        conserved[3] * velocity_i, (conserved[4] + pressure) * velocity_i, conserved[5] * velocity_i])
    flux_j = jnp.stack([conserved[2], conserved[1] * velocity_j, conserved[2] * velocity_j + pressure,
                        conserved[3] * velocity_j, (conserved[4] + pressure) * velocity_j, conserved[5] * velocity_j])
    return flux_i, flux_j, jnp.abs(velocity_i), jnp.abs(velocity_j)


def advance(extended, volumes, spectral, omega_value, instance_total):
    cells_i = extended.shape[2] - 4
    flux_i, flux_j, speed_i, speed_j = fluxes(extended)
    left_cell = extended[:, :, 1:cells_i + 2]
    right_cell = extended[:, :, 2:cells_i + 3]
    back_cell = extended[:, :, 0:cells_i + 1]
    ahead_cell = extended[:, :, 3:cells_i + 4]
    radius_i = 0.5 * (speed_i[:, 1:cells_i + 2] + speed_i[:, 2:cells_i + 3]) + SOUND_SPEED
    face_i = 0.5 * (flux_i[:, :, 1:cells_i + 2] + flux_i[:, :, 2:cells_i + 3]) - radius_i * (
        SECOND_DISSIPATION * (right_cell - left_cell)
        - FOURTH_DISSIPATION * (ahead_cell - 3.0 * right_cell + 3.0 * left_cell - back_cell))
    centre = extended[:, :, 2:cells_i + 2]
    centre_flux = flux_j[:, :, 2:cells_i + 2]
    centre_speed = speed_j[:, 2:cells_i + 2]
    next_cell = jnp.roll(centre, -1, axis=-1)
    prior_cell = jnp.roll(centre, 1, axis=-1)
    far_cell = jnp.roll(centre, -2, axis=-1)
    radius_j = 0.5 * (centre_speed + jnp.roll(centre_speed, -1, axis=-1)) + SOUND_SPEED
    face_j = 0.5 * (centre_flux + jnp.roll(centre_flux, -1, axis=-1)) - radius_j * (
        SECOND_DISSIPATION * (next_cell - centre)
        - FOURTH_DISSIPATION * (far_cell - 3.0 * next_cell + 3.0 * centre - prior_cell))
    residual_sum = (face_i[:, :, 1:] - face_i[:, :, :-1]) + (face_j - jnp.roll(face_j, 1, axis=-1)) + volumes * spectral
    step_rate = COURANT / (speed_i[:, 2:cells_i + 2] + centre_speed + 2.0 * SOUND_SPEED
                           + volumes * omega_value * 0.5 * instance_total)
    return centre - step_rate * residual_sum, residual_sum / volumes


def reference(flow_state, cell_volume, frequency, block_count, block_place, face_links, face_offset, face_flip):
    instance_total, comps, row_total, width = flow_state.shape
    slot_total = N_SPACE * BLOCKS_MAX
    cells_i = row_total // slot_total
    is_live, source_slot, column_index = block_tables(block_count, block_place, face_links, face_offset, face_flip,
                                                      jnp.arange(slot_total, dtype=jnp.int32), BLOCKS_MAX, width)
    volumes = cell_volume.reshape(slot_total, cells_i, width)
    matrix = spectral_matrix(instance_total, frequency[0])
    current = flow_state
    last_residual = jnp.zeros_like(flow_state)
    for iteration in range(PSEUDO_STEPS):
        spectral_all = jnp.einsum('nm,mcrb->ncrb', matrix, current, precision=lax.Precision.HIGHEST)

        def one_instance(pair):
            blocks = pair[0].reshape(comps, slot_total, cells_i, width)
            faces = jnp.stack([blocks[:, :, 0:2], blocks[:, :, cells_i - 2:cells_i]], axis=2)
            extended = with_halos(blocks, faces, source_slot, column_index)
            updated, residual_now = advance(extended, volumes, pair[1].reshape(comps, slot_total, cells_i, width),
                                            frequency[0], instance_total)
            return updated.reshape(comps, row_total, width), residual_now.reshape(comps, row_total, width)

        current, last_residual = lax.map(one_instance, (current, spectral_all))
    row_live = jnp.repeat(is_live, cells_i)[None, None, :, None]
    return jnp.where(row_live, current, 0.0), jnp.where(row_live, last_residual, 0.0)
```

```python
import functools
import math

import jax
import jax.numpy as jnp
from jax import lax
from jax.experimental import pallas as pl
from jax.experimental.pallas import tpu as pltpu
from jax.sharding import PartitionSpec as P

BLOCKS_MAX = 4
PSEUDO_STEPS = 2


HEAT_RATIO = 1.4
SECOND_DISSIPATION = 0.05
FOURTH_DISSIPATION = 0.02
SOUND_SPEED = 1.0
COURANT = 0.5
TIME_VISCOSITY = 0.25

COMPS = 6
FACES = 2 * BLOCKS_MAX
F32 = jnp.float32
VMEM = pl.BlockSpec(memory_space=pltpu.VMEM)
SMEM = pl.BlockSpec(memory_space=pltpu.SMEM)


def spectral_weights(total):
    weights = [TIME_VISCOSITY * (total * total + 2) / 12.0]
    for k in range(1, total):
        sign = 1.0 - 2.0 * (k % 2)
        angle = math.pi * k / total
        first = 0.5 * sign * math.cos(angle) / math.sin(angle)
        second = -sign / (2.0 * math.sin(angle) ** 2)
        weights.append(first - TIME_VISCOSITY * second)
    return weights


def pair_cap(space_total, block_total):
    second_most = min(BLOCKS_MAX, block_total - BLOCKS_MAX - (space_total - 2))
    return 2 * max(1, second_most)


def primitives(q):
    inverse = 1.0 / q[0]
    u = q[1] * inverse
    v = q[2] * inverse
    p = (HEAT_RATIO - 1.0) * (
        q[4] - 0.5 * (q[1] * q[1] + q[2] * q[2] + q[3] * q[3]) * inverse
    )
    return u, v, p


def flux_along_i(q, u, p):
    return [q[1], q[1] * u + p, q[2] * u, q[3] * u, (q[4] + p) * u, q[5] * u]


def flux_along_j(q, v, p):
    return [q[2], q[1] * v, q[2] * v + p, q[3] * v, (q[4] + p) * v, q[5] * v]


def ahead(x):
    return pltpu.roll(x, x.shape[1] - 1, axis=1)


def behind(x):
    return pltpu.roll(x, 1, axis=1)


DIFF_ONE = SECOND_DISSIPATION + 2.0 * FOURTH_DISSIPATION


def residual_j(q, v, p):
    speed = jnp.abs(v)
    radius = 0.5 * (speed + ahead(speed)) + SOUND_SPEED
    out = []
    for q_c, g_c in zip(q, flux_along_j(q, v, p)):
        step = ahead(q_c) - q_c
        damping = DIFF_ONE * step - FOURTH_DISSIPATION * (ahead(step) + behind(step))
        face = 0.5 * (g_c + ahead(g_c)) - radius * damping
        out.append(face - behind(face))
    return out


class Rows:
    def __init__(self, load):
        self.load = load
        self.state, self.prim, self.flux, self.steps, self.faces = {}, {}, {}, {}, {}

    def q(self, r):
        if r not in self.state:
            self.state[r] = self.load(r)
        return self.state[r]

    def uvp(self, r):
        if r not in self.prim:
            self.prim[r] = primitives(self.q(r))
        return self.prim[r]

    def f(self, r):
        if r not in self.flux:
            u, _, p = self.uvp(r)
            self.flux[r] = flux_along_i(self.q(r), u, p)
        return self.flux[r]

    def step(self, r):
        if r not in self.steps:
            self.steps[r] = [b - a for a, b in zip(self.q(r), self.q(r + 1))]
        return self.steps[r]

    def face(self, r):
        if r not in self.faces:
            radius = 0.5 * (jnp.abs(self.uvp(r)[0]) + jnp.abs(self.uvp(r + 1)[0])) + SOUND_SPEED
            out = []
            for c in range(COMPS):
                damping = DIFF_ONE * self.step(r)[c] - FOURTH_DISSIPATION * (
                    self.step(r + 1)[c] + self.step(r - 1)[c]
                )
                out.append(0.5 * (self.f(r)[c] + self.f(r + 1)[c]) - radius * damping)
            self.faces[r] = out
        return self.faces[r]

    def residual(self, r):
        u, v, p = self.uvp(r)
        lower, upper = self.face(r - 1), self.face(r)
        across = residual_j(self.q(r), v, p)
        total = [(b - a) + j for a, b, j in zip(lower, upper, across)]
        return total, jnp.abs(u) + jnp.abs(v)


def even_tiles(shape):
    return lax.broadcasted_iota(jnp.int32, shape, 0) % 2 == 0


def row_loader(load, halo_ref):
    def extended(r):
        out = []
        for c in range(COMPS):
            if r < 0:
                inner = pltpu.roll(load(c, r + 8), 1, axis=0)
                out.append(jnp.where(even_tiles(inner.shape), halo_ref[c, r + 2], inner))
            elif r > 7:
                inner = pltpu.roll(load(c, r - 8), 7, axis=0)
                out.append(jnp.where(even_tiles(inner.shape), inner, halo_ref[c, r - 8]))
            else:
                out.append(load(c, r))
        return out

    return extended


def split_parts(parts_ref, rest_ref):
    def load(c, r):
        if 2 <= r <= 5:
            return rest_ref[c, r]
        layer = r % 2
        outer, other = parts_ref[c, layer], rest_ref[c, layer]
        even = even_tiles(outer.shape)
        if r < 2:
            return jnp.where(even, outer, other)
        return jnp.where(even, other, outer)

    return load


def coefficients(frequency_ref):
    weights = spectral_weights(4)
    omega = frequency_ref[0]
    even = lax.axis_index("inst") % 2 == 0
    near = omega * jnp.where(even, F32(weights[3]), F32(weights[1]))
    far = omega * jnp.where(even, F32(weights[1]), F32(weights[3]))
    return omega, omega * F32(weights[0]), omega * F32(weights[2]), near, far


def own_instance_rate(speeds, volume, omega):
    return COURANT / (speeds + 2.0 * SOUND_SPEED + volume * (omega * (0.5 * 4)))


def pack_kernel(
    space_total, block_total, cap,
    state_ref, volume_ref, counts_ref, place_ref, links_ref, offset_ref, flip_ref,
    rows_ref, vrows_ref, outer_ref, rest_ref, table_ref, index_ref, *more
):
    sends = more[: space_total - 1]
    half_ref, first_ref, inverse_ref = more[space_total - 1 :]
    width = state_ref.shape[2]
    for c in range(COMPS + 1):
        for h in range(2):
            lanes = pl.ds(128 * h, 128)
            half_ref[c, h] = state_ref[c, :, lanes] if c < COMPS else volume_ref[:, lanes]
    for c in range(COMPS + 1):
        for r in range(8):
            for h in range(2):
                row = half_ref[c, h, pl.ds(r, 8, stride=8), :]
                if c < COMPS:
                    rows_ref[c, r, :, pl.ds(128 * h, 128)] = row
                else:
                    vrows_ref[r, :, pl.ds(128 * h, 128)] = row
    even = even_tiles((8, width))
    for c in range(COMPS):
        for l in range(2):
            low, high = rows_ref[c, l], rows_ref[c, 6 + l]
            outer_ref[c, l] = jnp.where(even, low, high)
            rest_ref[c, l] = jnp.where(even, high, low)
        for r in range(2, 6):
            rest_ref[c, r] = rows_ref[c, r]
    me = lax.axis_index("space")
    total = jnp.int32(0)
    firsts = []
    for d in range(space_total):
        firsts.append(total)
        first_ref[d] = total
        total = total + counts_ref[d]
    for b in range(block_total):
        inverse_ref[place_ref[b]] = jnp.int32(b)

    def block_in(device, slot):
        return inverse_ref[jnp.minimum(first_ref[device] + slot, block_total - 1)]

    def source_of(block, side):
        link = links_ref[block, side]
        place = place_ref[jnp.maximum(link, 0)]
        owner = jnp.int32(0)
        first = jnp.int32(0)
        for d in range(1, space_total):
            past = place >= firsts[d]
            owner = jnp.where(past, d, owner)
            first = jnp.where(past, firsts[d], first)
        return link, owner, 2 * (place - first) + (1 - side)

    own_base = (space_total - 1) * COMPS * 2 * cap
    few = 2 * counts_ref[me] <= cap
    tile = lax.broadcasted_iota(jnp.int32, (FACES, width), 0)
    start = jnp.zeros((FACES, width), jnp.int32)
    turned = jnp.zeros((FACES, width), jnp.int32)
    for f in range(FACES):
        slot, side = f // 2, f % 2
        block = block_in(me, slot)
        link, owner, source = source_of(block, side)
        shift = lax.rem(me - owner + space_total, space_total)
        listed = 2 * counts_ref[owner] <= cap
        place = jnp.where(listed, jnp.minimum(source, cap - 1), min(f, cap - 1))
        outside = link < 0
        mine = owner == me
        base = jnp.where(mine, own_base + source, (shift - 1) * (COMPS * 2 * cap) + place)
        base = jnp.where(outside, own_base + 8 * side + f, base)
        table_ref[f] = base
        table_ref[FACES + f] = jnp.where(outside | mine, 2 * FACES, 2 * cap)
        table_ref[2 * FACES + f] = jnp.where(outside, 0, jnp.where(mine, FACES, cap))
        start = jnp.where(tile == f, jnp.where(outside, 0, offset_ref[block, side]), start)
        turned = jnp.where(tile == f, jnp.where(outside, 0, flip_ref[block, side]), turned)
    column = lax.broadcasted_iota(jnp.int32, (FACES, width), 1)
    index_ref[...] = (start + jnp.where(turned == 1, width - 1 - column, column)) % width
    for k in range(1, space_total):
        target = lax.rem(me + k, space_total)
        for i in range(cap):
            _, owner, source = source_of(block_in(target, i // 2), i % 2)
            wanted = jnp.where(owner == me, source, 0)
            table_ref[3 * FACES + (k - 1) * cap + i] = jnp.where(few, i, wanted)
    pack_sends(cap, outer_ref, table_ref, sends)


def pack_sends(cap, outer_ref, table_ref, sends):
    for k, send_ref in enumerate(sends):
        for i in range(cap):
            f = table_ref[3 * FACES + k * cap + i]
            for c in range(COMPS):
                for l in range(2):
                    send_ref[pl.ds((2 * c + l) * cap + i, 1), :] = outer_ref[c, l, pl.ds(f, 1), :]


def halo_kernel(space_total, cap, table_ref, index_ref, outer_ref, *more):
    received = more[: space_total - 1]
    halo_ref, pool_ref, raw_ref = more[space_total - 1 :]
    size = COMPS * 2 * cap
    for k, part in enumerate(received):
        pool_ref[pl.ds(k * size, size), :] = part[...]
    own_base = (space_total - 1) * size
    for c in range(COMPS):
        for l in range(2):
            pool_ref[pl.ds(own_base + (2 * c + l) * FACES, FACES), :] = outer_ref[c, l]
    for f in range(FACES):
        base, per_comp, per_layer = table_ref[f], table_ref[FACES + f], table_ref[2 * FACES + f]
        for c in range(COMPS):
            for l in range(2):
                row = base + c * per_comp + l * per_layer
                raw_ref[c, l, pl.ds(f, 1), :] = pool_ref[pl.ds(row, 1), :]
    width = index_ref.shape[1]
    masks, lanes = [], []
    for h in range(width // 128):
        index = index_ref[:, pl.ds(128 * h, 128)]
        lanes.append(index & 127)
        masks.append(index < 128)
    for c in range(COMPS):
        for l in range(2):
            low, high = raw_ref[c, l, :, pl.ds(0, 128)], raw_ref[c, l, :, pl.ds(128, 128)]
            for h in range(2):
                a = jnp.take_along_axis(low, lanes[h], axis=1)
                b = jnp.take_along_axis(high, lanes[h], axis=1)
                halo_ref[c, l, :, pl.ds(128 * h, 128)] = jnp.where(masks[h], a, b)


def outer_kernel(
    cap, table_ref, frequency_ref, rows_ref, vrows_ref, halo_ref, across_ref, sibling_ref,
    sibling_across_ref, outer_ref, *sends
):
    omega, w_own, w_across, w_near, w_far = coefficients(frequency_ref)
    load = row_loader(lambda c, r: rows_ref[c, r], halo_ref)
    even = even_tiles(vrows_ref.shape[1:])
    low = {r: load(r) for r in range(-2, 4)}
    high = {r: load(r) for r in range(4, 10)}
    picked = {
        k: [jnp.where(even, a, b) for a, b in zip(low[k - 2], high[k + 4])] for k in range(6)
    }
    rows = Rows(lambda k: picked[k])
    for l in range(2):
        flux, speeds = rows.residual(l + 2)
        volume = jnp.where(even, vrows_ref[l], vrows_ref[l + 6])
        rate = own_instance_rate(speeds, volume, omega)
        for c in range(COMPS):
            own = picked[l + 2][c]
            sibling = jnp.where(even, sibling_ref[c, l], sibling_ref[c, l + 6])
            spectral = (
                w_own * own + w_across * across_ref[c, l]
                + w_near * sibling + w_far * sibling_across_ref[c, l]
            )
            outer_ref[c, l] = own - rate * (flux[c] + volume * spectral)
    pack_sends(cap, outer_ref, table_ref, sends)


def first_kernel(
    frequency_ref, rows_ref, vrows_ref, halo_ref, across_halo_ref, across_outer_ref,
    across_rest_ref, sibling_ref, sib_across_outer_ref, sib_across_rest_ref,
    next_ref, partial_ref, send_ref
):
    omega, w_own, w_across, w_near, w_far = coefficients(frequency_ref)
    own_load = lambda c, r: rows_ref[c, r]
    across_load = split_parts(across_outer_ref, across_rest_ref)
    far_load = split_parts(sib_across_outer_ref, sib_across_rest_ref)
    own = Rows(row_loader(own_load, halo_ref))
    across = Rows(row_loader(across_load, across_halo_ref))
    for r in range(8):
        volume = vrows_ref[r]
        own_flux, own_speeds = own.residual(r)
        own_rate = own_instance_rate(own_speeds, volume, omega)
        across_flux, across_speeds = across.residual(r)
        across_rate = own_instance_rate(across_speeds, volume, omega)
        for c in range(COMPS):
            mine, other = own.q(r)[c], across.q(r)[c]
            near, far = sibling_ref[c, r], far_load(c, r)
            spectral = w_own * mine + w_across * other + w_near * near + w_far * far
            mine_next = mine - own_rate * (own_flux[c] + volume * spectral)
            spectral = w_own * other + w_across * mine + w_far * near + w_near * far
            other_next = other - across_rate * (across_flux[c] + volume * spectral)
            next_ref[c, r] = mine_next
            partial_ref[c, r] = w_own * mine_next + w_across * other_next
            send_ref[c, r] = w_far * mine_next + w_near * other_next


def last_kernel(
    frequency_ref, counts_ref, rows_ref, vrows_ref, halo_ref, partial_ref, received_ref,
    new_ref, residual_ref, new_half_ref, residual_half_ref
):
    omega = frequency_ref[0]
    own = Rows(row_loader(lambda c, r: rows_ref[c, r], halo_ref))
    live = (lax.broadcasted_iota(jnp.int32, vrows_ref.shape[1:], 0) // 2) < counts_ref[
        lax.axis_index("space")
    ]
    for r in range(8):
        volume = vrows_ref[r]
        flux, speeds = own.residual(r)
        rate = own_instance_rate(speeds, volume, omega)
        inverse = 1.0 / volume
        for c in range(COMPS):
            residual = flux[c] + volume * (partial_ref[c, r] + received_ref[c, r])
            new = jnp.where(live, own.q(r)[c] - rate * residual, 0.0)
            scaled = jnp.where(live, residual * inverse, 0.0)
            for h in range(2):
                lanes = slice(128 * h, 128 * h + 128)
                new_half_ref[c, h, pl.ds(r, 8, stride=8), :] = new[:, lanes]
                residual_half_ref[c, h, pl.ds(r, 8, stride=8), :] = scaled[:, lanes]
    for c in range(COMPS):
        for h in range(2):
            new_ref[c, :, pl.ds(128 * h, 128)] = new_half_ref[c, h]
            residual_ref[c, :, pl.ds(128 * h, 128)] = residual_half_ref[c, h]


def hold(x):
    return pltpu.with_memory_space_constraint(x, pltpu.VMEM)


def four_instances(
    flow_state, cell_volume, frequency, block_count, block_place, face_links, face_offset, face_flip
):
    _, comps, row_count, width = flow_state.shape
    space_total = lax.axis_size("space")
    block_total = block_place.shape[0]
    cap = pair_cap(space_total, block_total)
    state = flow_state[0]

    def over_inst(x, flip):
        return lax.ppermute(x, "inst", [(i, i ^ flip) for i in range(4)])

    def over_space(parts):
        return [
            lax.ppermute(x, "space", [(i, (i + k + 1) % space_total) for i in range(space_total)])
            for k, x in enumerate(parts)
        ]

    full = (comps, 8, 8, width)
    outer = (comps, 2, 8, width)
    pair = (comps * 2 * cap, width)
    entries = 3 * FACES + (space_total - 1) * cap
    on_chip = lambda shape, dtype=F32: pltpu.VMEM(shape, dtype)
    sends_shape = [on_chip(pair) for _ in range(space_total - 1)]

    packed = pl.pallas_call(
        functools.partial(pack_kernel, space_total, block_total, cap),
        out_shape=[
            on_chip(full), on_chip((8, 8, width)), on_chip(outer), on_chip((comps, 6, 8, width)),
            pltpu.SMEM((entries,), jnp.int32), on_chip((FACES, width), jnp.int32), *sends_shape,
        ],
        in_specs=[VMEM, VMEM] + [SMEM] * 5,
        out_specs=[VMEM] * 4 + [SMEM, VMEM] + [VMEM] * (space_total - 1),
        scratch_shapes=[
            pltpu.VMEM((comps + 1, 2, row_count, 128), F32),
            pltpu.SMEM((space_total,), jnp.int32),
            pltpu.SMEM((block_total,), jnp.int32),
        ],
    )(hold(state), hold(cell_volume), block_count, block_place, face_links, face_offset, face_flip)
    rows, vrows, outer_rows, rest, table, index = packed[:6]
    sends = packed[6:]
    in_smem = lambda x: pltpu.with_memory_space_constraint(x, pltpu.SMEM)
    table = in_smem(table)

    def halos(outer_own, received):
        return pl.pallas_call(
            functools.partial(halo_kernel, space_total, cap),
            out_shape=on_chip(outer),
            in_specs=[SMEM] + [VMEM] * (2 + len(received)),
            out_specs=VMEM,
            scratch_shapes=[
                pltpu.VMEM(((space_total - 1) * pair[0] + comps * 2 * FACES, width), F32),
                pltpu.VMEM(outer, F32),
            ],
        )(table, hold(index), hold(outer_own), *[hold(x) for x in received])

    across_outer = over_inst(outer_rows, 2)
    across_rest = over_inst(rest, 2)
    sibling = over_inst(rows, 1)
    halo = halos(outer_rows, over_space(sends))
    sib_across_outer = over_inst(across_outer, 1)
    across_halo = over_inst(halo, 2)

    produced = pl.pallas_call(
        functools.partial(outer_kernel, cap),
        out_shape=[on_chip(outer), *sends_shape],
        in_specs=[SMEM, SMEM] + [VMEM] * 6,
        out_specs=[VMEM] * space_total,
    )(
        table, frequency, hold(rows), hold(vrows), hold(halo), hold(across_outer), hold(sibling),
        hold(sib_across_outer),
    )
    next_outer, next_sends = produced[0], produced[1:]
    sib_across_rest = over_inst(across_rest, 1)
    next_halo = halos(next_outer, over_space(next_sends))

    next_rows, partial, to_sibling = pl.pallas_call(
        first_kernel,
        out_shape=[on_chip(full)] * 3,
        in_specs=[SMEM] + [VMEM] * 9,
        out_specs=[VMEM] * 3,
    )(
        frequency, hold(rows), hold(vrows), hold(halo), hold(across_halo), hold(across_outer),
        hold(across_rest), hold(sibling), hold(sib_across_outer), hold(sib_across_rest),
    )
    from_sibling = over_inst(to_sibling, 1)

    new, residual = pl.pallas_call(
        last_kernel,
        out_shape=[jax.ShapeDtypeStruct(state.shape, F32)] * 2,
        in_specs=[SMEM, SMEM] + [VMEM] * 5,
        out_specs=[VMEM] * 2,
        scratch_shapes=[pltpu.VMEM((comps, 2, row_count, 128), F32)] * 2,
    )(
        frequency, block_count, hold(next_rows), hold(vrows), hold(next_halo), hold(partial),
        hold(from_sibling),
    )
    return new[None], residual[None]


def spectral_matrix(instance_total, omega_value):
    position = jnp.arange(instance_total, dtype=jnp.int32)
    distance = (position[:, None] - position[None, :]) % instance_total
    parity = (1 - 2 * (distance % 2)).astype(jnp.float32)
    phase_angle = jnp.pi * distance.astype(jnp.float32) / instance_total
    safe_angle = jnp.where(distance == 0, 0.5 * jnp.pi, phase_angle)
    first_derivative = jnp.where(
        distance == 0, 0.0, 0.5 * parity * jnp.cos(safe_angle) / jnp.sin(safe_angle)
    )
    second_derivative = jnp.where(
        distance == 0,
        -(instance_total * instance_total + 2) / 12.0,
        -parity / (2.0 * jnp.sin(safe_angle) ** 2),
    )
    return omega_value * (first_derivative - TIME_VISCOSITY * second_derivative)


def block_tables(
    block_count, block_place, face_links, face_offset, face_flip, targets, slot_count, width
):
    block_total = block_place.shape[0]
    first_position = jnp.cumsum(block_count) - block_count
    block_at_position = (
        jnp.zeros((block_total,), jnp.int32)
        .at[block_place]
        .set(jnp.arange(block_total, dtype=jnp.int32))
    )
    owner_device = jnp.sum(
        (block_place[:, None] >= first_position[None, 1:]).astype(jnp.int32), axis=1
    )
    flat_slot = owner_device * slot_count + block_place - first_position[owner_device]
    target_device = targets // slot_count
    target_slot = targets % slot_count
    is_live = target_slot < block_count[target_device]
    block_index = block_at_position[
        jnp.clip(first_position[target_device] + target_slot, 0, block_total - 1)
    ]
    neighbour = face_links[block_index]
    source_slot = jnp.where(neighbour >= 0, flat_slot[jnp.clip(neighbour, 0, block_total - 1)], -1)
    column = jnp.arange(width, dtype=jnp.int32)
    flipped = face_flip[block_index][:, :, None]
    ordered = jnp.where(flipped == 1, width - 1 - column, column)
    column_index = (face_offset[block_index][:, :, None] + ordered) % width
    return (is_live, source_slot, column_index)


def attach_halos(blocks, lower, upper, source_slot):
    cells_i = blocks.shape[2]
    lower = jnp.where(
        (source_slot[:, 0] >= 0)[None, :, None, None],
        lower,
        jnp.repeat(blocks[:, :, 0:1], 2, axis=2),
    )
    upper = jnp.where(
        (source_slot[:, 1] >= 0)[None, :, None, None],
        upper,
        jnp.repeat(blocks[:, :, cells_i - 1 : cells_i], 2, axis=2),
    )
    return jnp.concatenate([lower, blocks, upper], axis=2)


def fluxes(conserved):
    inverse_rho = 1.0 / conserved[0]
    velocity_i = conserved[1] * inverse_rho
    velocity_j = conserved[2] * inverse_rho
    pressure = (HEAT_RATIO - 1.0) * (
        conserved[4]
        - 0.5
        * (conserved[1] * conserved[1] + conserved[2] * conserved[2] + conserved[3] * conserved[3])
        * inverse_rho
    )
    flux_i = jnp.stack(
        [
            conserved[1],
            conserved[1] * velocity_i + pressure,
            conserved[2] * velocity_i,
            conserved[3] * velocity_i,
            (conserved[4] + pressure) * velocity_i,
            conserved[5] * velocity_i,
        ]
    )
    flux_j = jnp.stack(
        [
            conserved[2],
            conserved[1] * velocity_j,
            conserved[2] * velocity_j + pressure,
            conserved[3] * velocity_j,
            (conserved[4] + pressure) * velocity_j,
            conserved[5] * velocity_j,
        ]
    )
    return (flux_i, flux_j, jnp.abs(velocity_i), jnp.abs(velocity_j))


def advance(extended, volumes, spectral, omega_value, instance_total):
    cells_i = extended.shape[2] - 4
    flux_i, flux_j, speed_i, speed_j = fluxes(extended)
    left_cell = extended[:, :, 1 : cells_i + 2]
    right_cell = extended[:, :, 2 : cells_i + 3]
    back_cell = extended[:, :, 0 : cells_i + 1]
    ahead_cell = extended[:, :, 3 : cells_i + 4]
    radius_i = 0.5 * (speed_i[:, 1 : cells_i + 2] + speed_i[:, 2 : cells_i + 3]) + SOUND_SPEED
    face_i = 0.5 * (flux_i[:, :, 1 : cells_i + 2] + flux_i[:, :, 2 : cells_i + 3]) - radius_i * (
        SECOND_DISSIPATION * (right_cell - left_cell)
        - FOURTH_DISSIPATION * (ahead_cell - 3.0 * right_cell + 3.0 * left_cell - back_cell)
    )
    centre = extended[:, :, 2 : cells_i + 2]
    centre_flux = flux_j[:, :, 2 : cells_i + 2]
    centre_speed = speed_j[:, 2 : cells_i + 2]
    next_cell = jnp.roll(centre, -1, axis=-1)
    prior_cell = jnp.roll(centre, 1, axis=-1)
    far_cell = jnp.roll(centre, -2, axis=-1)
    radius_j = 0.5 * (centre_speed + jnp.roll(centre_speed, -1, axis=-1)) + SOUND_SPEED
    face_j = 0.5 * (centre_flux + jnp.roll(centre_flux, -1, axis=-1)) - radius_j * (
        SECOND_DISSIPATION * (next_cell - centre)
        - FOURTH_DISSIPATION * (far_cell - 3.0 * next_cell + 3.0 * centre - prior_cell)
    )
    residual_sum = (
        face_i[:, :, 1:]
        - face_i[:, :, :-1]
        + (face_j - jnp.roll(face_j, 1, axis=-1))
        + volumes * spectral
    )
    step_rate = COURANT / (
        speed_i[:, 2 : cells_i + 2]
        + centre_speed
        + 2.0 * SOUND_SPEED
        + volumes * omega_value * 0.5 * instance_total
    )
    return (centre - step_rate * residual_sum, residual_sum / volumes)


def select_faces(selector, slabs):
    return jnp.einsum("tf,lcfxw->lctxw", selector, slabs, precision=lax.Precision.HIGHEST)


def orient_faces(slabs, permuter):
    return jnp.einsum("lctxw,tvw->lctxv", slabs, permuter, precision=lax.Precision.HIGHEST)


def on_device(
    flow_state, cell_volume, frequency, block_count, block_place, face_links, face_offset, face_flip
):
    local_count, comps, row_count, width = flow_state.shape
    slot_count = BLOCKS_MAX
    cells_i = row_count // slot_count
    space_total = lax.axis_size("space")
    space_index = lax.axis_index("space")
    targets = space_index * slot_count + jnp.arange(slot_count, dtype=jnp.int32)
    is_live, source_slot, column_index = block_tables(
        block_count, block_place, face_links, face_offset, face_flip, targets, slot_count, width
    )
    column = jnp.arange(width, dtype=jnp.int32)
    permuter = (
        column_index.reshape(slot_count * 2, width)[:, :, None] == column[None, None, :]
    ).astype(jnp.float32)
    side_index = jnp.arange(2, dtype=jnp.int32)[None, :]
    volumes = cell_volume.reshape(slot_count, cells_i, width)
    instance_total = local_count * lax.axis_size("inst")
    matrix = spectral_matrix(instance_total, frequency[0])
    row_offset = lax.axis_index("inst") * local_count
    own_rows = lax.dynamic_slice_in_dim(matrix, row_offset, local_count, 0)
    wanted_face = (source_slot * 2 + (1 - side_index)).reshape(-1)
    face_range = jnp.arange(space_total * slot_count * 2, dtype=jnp.int32)
    selector = (
        (wanted_face[:, None] == face_range[None, :]) & (source_slot.reshape(-1)[:, None] >= 0)
    ).astype(jnp.float32)
    current = flow_state
    last_residual = jnp.zeros_like(flow_state)
    for iteration in range(PSEUDO_STEPS):
        spectral_all = jnp.einsum(
            "nm,mcrb->ncrb",
            own_rows,
            lax.all_gather(current, "inst", axis=0, tiled=True),
            precision=lax.Precision.HIGHEST,
        )
        blocks = current.reshape(local_count, comps, slot_count, cells_i, width)
        faces = jnp.stack([blocks[:, :, :, 0:2], blocks[:, :, :, cells_i - 2 : cells_i]], axis=3)
        gathered = lax.all_gather(faces, "space", axis=2, tiled=True)
        gathered = gathered.reshape(local_count, comps, space_total * slot_count * 2, 2, width)
        arrived = select_faces(selector, gathered)
        oriented = orient_faces(arrived, permuter).reshape(
            local_count, comps, slot_count, 2, 2, width
        )

        def one_instance(own_blocks, slabs, spectral):
            extended = attach_halos(own_blocks, slabs[:, :, 0], slabs[:, :, 1], source_slot)
            return advance(
                extended,
                volumes,
                spectral.reshape(comps, slot_count, cells_i, width),
                frequency[0],
                instance_total,
            )

        updated, residual_now = jax.vmap(one_instance)(blocks, oriented, spectral_all)
        current = updated.reshape(flow_state.shape)
        last_residual = residual_now.reshape(flow_state.shape)
    row_live = jnp.repeat(is_live, cells_i)[None, None, :, None]
    return (jnp.where(row_live, current, 0.0), jnp.where(row_live, last_residual, 0.0))


def solution(mesh):
    return jax.shard_map(
        four_instances if mesh.shape["inst"] == 4 else on_device,
        mesh=mesh,
        in_specs=(
            P(("groups", "inst"), None, "space", None),
            P(("groups", "space"), None),
            P(),
            P("groups"),
            P("groups"),
            P("groups", None),
            P("groups", None),
            P("groups", None),
        ),
        out_specs=(
            P(("groups", "inst"), None, "space", None),
            P(("groups", "inst"), None, "space", None),
        ),
        check_vma=False,
    )
```

```python
import functools
import math

import jax
import jax.numpy as jnp
from jax import lax
from jax.experimental import pallas as pl
from jax.experimental.pallas import tpu as pltpu
from jax.sharding import PartitionSpec as P

BLOCKS_MAX = 4
PSEUDO_STEPS = 2


HEAT_RATIO = 1.4
SECOND_DISSIPATION = 0.05
FOURTH_DISSIPATION = 0.02
SOUND_SPEED = 1.0
COURANT = 0.5
TIME_VISCOSITY = 0.25

COMPS = 6
FACES = 2 * BLOCKS_MAX
POOLED = COMPS + 1
F32 = jnp.float32
VMEM = pl.BlockSpec(memory_space=pltpu.VMEM)
SMEM = pl.BlockSpec(memory_space=pltpu.SMEM)


def spectral_weights(total):
    weights = [TIME_VISCOSITY * (total * total + 2) / 12.0]
    for k in range(1, total):
        sign = 1.0 - 2.0 * (k % 2)
        angle = math.pi * k / total
        first = 0.5 * sign * math.cos(angle) / math.sin(angle)
        second = -sign / (2.0 * math.sin(angle) ** 2)
        weights.append(first - TIME_VISCOSITY * second)
    return weights


def pair_cap(space_total, block_total):
    second_most = min(BLOCKS_MAX, block_total - BLOCKS_MAX - (space_total - 2))
    return 2 * max(1, second_most)


def primitives(q):
    inverse = 1.0 / q[0]
    u = q[1] * inverse
    v = q[2] * inverse
    p = (HEAT_RATIO - 1.0) * (
        q[4] - 0.5 * (q[1] * q[1] + q[2] * q[2] + q[3] * q[3]) * inverse
    )
    return u, v, p


def flux_along_i(q, u, p):
    return [q[1], q[1] * u + p, q[2] * u, q[3] * u, (q[4] + p) * u, q[5] * u]


def flux_along_j(q, v, p):
    return [q[2], q[1] * v, q[2] * v + p, q[3] * v, (q[4] + p) * v, q[5] * v]


def ahead(x):
    return pltpu.roll(x, x.shape[1] - 1, axis=1)


def behind(x):
    return pltpu.roll(x, 1, axis=1)


DIFF_ONE = SECOND_DISSIPATION + 2.0 * FOURTH_DISSIPATION


def turn(x, shift):
    return pltpu.roll(x, shift % x.shape[1], axis=1)


def pitchwise_shifts(load, near_ref):
    for c in range(COMPS):
        for r in range(8):
            q = load(c, r)
            near_ref[0, c, r] = turn(q, -1)
            near_ref[1, c, r] = turn(q, -2)
            near_ref[2, c, r] = turn(q, 1)


def pitchwise_faces(q, v, p, near_ref, r):
    after = [near_ref[0, c, r] for c in range(COMPS)]
    _, v_after, p_after = primitives(after)
    radius = 0.5 * (jnp.abs(v) + jnp.abs(v_after)) + SOUND_SPEED
    here, there = flux_along_j(q, v, p), flux_along_j(after, v_after, p_after)
    upper, lower = [], []
    for c in range(COMPS):
        step = after[c] - q[c]
        others = (near_ref[1, c, r] - after[c]) + (q[c] - near_ref[2, c, r])
        damping = radius * (DIFF_ONE * step - FOURTH_DISSIPATION * others)
        upper.append(0.5 * there[c] - damping)
        lower.append(0.5 * here[c] - damping)
    return upper, lower


class Rows:
    def __init__(self, load):
        self.load = load
        self.state, self.prim, self.flux, self.steps, self.faces = {}, {}, {}, {}, {}

    def q(self, r):
        if r not in self.state:
            self.state[r] = self.load(r)
        return self.state[r]

    def uvp(self, r):
        if r not in self.prim:
            self.prim[r] = primitives(self.q(r))
        return self.prim[r]

    def f(self, r):
        if r not in self.flux:
            u, _, p = self.uvp(r)
            self.flux[r] = flux_along_i(self.q(r), u, p)
        return self.flux[r]

    def step(self, r):
        if r not in self.steps:
            self.steps[r] = [b - a for a, b in zip(self.q(r), self.q(r + 1))]
        return self.steps[r]

    def face(self, r):
        if r not in self.faces:
            radius = 0.5 * (jnp.abs(self.uvp(r)[0]) + jnp.abs(self.uvp(r + 1)[0])) + SOUND_SPEED
            out = []
            for c in range(COMPS):
                damping = DIFF_ONE * self.step(r)[c] - FOURTH_DISSIPATION * (
                    self.step(r + 1)[c] + self.step(r - 1)[c]
                )
                out.append(0.5 * (self.f(r)[c] + self.f(r + 1)[c]) - radius * damping)
            self.faces[r] = out
        return self.faces[r]

    def along(self, r):
        return [b - a for a, b in zip(self.face(r - 1), self.face(r))]


def even_tiles(shape):
    return lax.broadcasted_iota(jnp.int32, shape, 0) % 2 == 0


def row_loader(load, halo_ref):
    def extended(r):
        out = []
        for c in range(COMPS):
            if r < 0:
                inner = pltpu.roll(load(c, r + 8), 1, axis=0)
                out.append(jnp.where(even_tiles(inner.shape), halo_ref[c, r + 2], inner))
            elif r > 7:
                inner = pltpu.roll(load(c, r - 8), 7, axis=0)
                out.append(jnp.where(even_tiles(inner.shape), inner, halo_ref[c, r - 8]))
            else:
                out.append(load(c, r))
        return out

    return extended


def rows_from(raw_ref, half_ref, rows_ref):
    for c in range(COMPS):
        for h in range(2):
            half_ref[c, h] = raw_ref[c, :, pl.ds(128 * h, 128)]
    for c in range(COMPS):
        for r in range(8):
            for h in range(2):
                rows_ref[c, r, :, pl.ds(128 * h, 128)] = half_ref[c, h, pl.ds(r, 8, stride=8), :]


def put_coefficients(frequency_ref, weight_ref):
    weights = spectral_weights(4)
    omega = frequency_ref[0]
    even = lax.axis_index("inst") % 2 == 0
    weight_ref[0] = omega
    weight_ref[1] = omega * F32(weights[0])
    weight_ref[2] = omega * F32(weights[2])
    weight_ref[3] = omega * jnp.where(even, F32(weights[3]), F32(weights[1]))
    weight_ref[4] = omega * jnp.where(even, F32(weights[1]), F32(weights[3]))


def coefficients(weight_ref):
    return [weight_ref[k] for k in range(5)]


def own_instance_rate(speeds, volume, omega):
    return COURANT / (speeds + 2.0 * SOUND_SPEED + volume * (omega * (0.5 * 4)))


def pack_kernel(
    space_total, block_total, cap,
    state_ref, volume_ref, frequency_ref, counts_ref, place_ref, links_ref, offset_ref, flip_ref,
    rows_ref, vrows_ref, outer_ref, table_ref, weight_ref, index_ref, *more
):
    sends = more[: space_total - 1]
    half_ref, arrival, first_ref, inverse_ref = more[space_total - 1 :]
    width = state_ref.shape[2]
    copies = []
    for h in range(2):
        lanes = pl.ds(128 * h, 128)
        for n, (source, target) in enumerate(
            [
                (state_ref.at[:, :, lanes], half_ref.at[h, pl.ds(0, COMPS)]),
                (volume_ref.at[:, lanes], half_ref.at[h, COMPS]),
            ]
        ):
            copies.append(pltpu.make_async_copy(source, target, arrival.at[2 * h + n]))
            copies[-1].start()
    put_coefficients(frequency_ref, weight_ref)
    me = lax.axis_index("space")
    total = jnp.int32(0)
    firsts = []
    for d in range(space_total):
        firsts.append(total)
        first_ref[d] = total
        total = total + counts_ref[d]
    for b in range(block_total):
        inverse_ref[place_ref[b]] = jnp.int32(b)

    def block_in(device, slot):
        return inverse_ref[jnp.minimum(first_ref[device] + slot, block_total - 1)]

    def source_of(block, side):
        link = links_ref[side, block]
        place = place_ref[jnp.maximum(link, 0)]
        owner = jnp.int32(0)
        first = jnp.int32(0)
        for d in range(1, space_total):
            past = place >= firsts[d]
            owner = jnp.where(past, d, owner)
            first = jnp.where(past, firsts[d], first)
        return link, owner, 2 * (place - first) + (1 - side)

    own_base = (space_total - 1) * POOLED * 2 * cap
    few = 2 * counts_ref[me] <= cap
    table_ref[3 * FACES + (space_total - 1) * cap] = counts_ref[me]
    tile = lax.broadcasted_iota(jnp.int32, (FACES, width), 0)
    start = jnp.zeros((FACES, width), jnp.int32)
    turned = jnp.zeros((FACES, width), jnp.int32)
    for f in range(FACES):
        slot, side = f // 2, f % 2
        block = block_in(me, slot)
        link, owner, source = source_of(block, side)
        shift = lax.rem(me - owner + space_total, space_total)
        listed = 2 * counts_ref[owner] <= cap
        place = jnp.where(listed, jnp.minimum(source, cap - 1), min(f, cap - 1))
        outside = link < 0
        mine = owner == me
        base = jnp.where(mine, own_base + source, (shift - 1) * (POOLED * 2 * cap) + place)
        base = jnp.where(outside, own_base + 8 * side + f, base)
        table_ref[f] = base
        table_ref[FACES + f] = jnp.where(outside | mine, 2 * FACES, 2 * cap)
        table_ref[2 * FACES + f] = jnp.where(outside, 0, jnp.where(mine, FACES, cap))
        start = jnp.where(tile == f, jnp.where(outside, 0, offset_ref[side, block]), start)
        turned = jnp.where(tile == f, jnp.where(outside, 0, flip_ref[side, block]), turned)
    column = lax.broadcasted_iota(jnp.int32, (FACES, width), 1)
    index_ref[...] = (start + jnp.where(turned == 1, width - 1 - column, column)) % width
    for k in range(1, space_total):
        target = lax.rem(me + k, space_total)
        for i in range(cap):
            _, owner, source = source_of(block_in(target, i // 2), i % 2)
            wanted = jnp.where(owner == me, source, 0)
            table_ref[3 * FACES + (k - 1) * cap + i] = jnp.where(few, i, wanted)
    for copy in copies:
        copy.wait()
    for c in range(COMPS + 1):
        for r in range(8):
            for h in range(2):
                row = half_ref[h, c, pl.ds(r, 8, stride=8), :]
                if c < COMPS:
                    rows_ref[c, r, :, pl.ds(128 * h, 128)] = row
                else:
                    vrows_ref[r, :, pl.ds(128 * h, 128)] = row
    even = even_tiles((8, width))
    for c in range(COMPS):
        for l in range(2):
            low, high = rows_ref[c, l], rows_ref[c, 6 + l]
            outer_ref[c, l] = jnp.where(even, low, high)
    pack_sends(cap, outer_ref, table_ref, sends)


def pack_sends(cap, outer_ref, table_ref, sends):
    for k, send_ref in enumerate(sends):
        for i in range(cap):
            f = table_ref[3 * FACES + k * cap + i]
            for c in range(outer_ref.shape[0]):
                for l in range(2):
                    send_ref[pl.ds((2 * c + l) * cap + i, 1), :] = outer_ref[c, l, pl.ds(f, 1), :]


def permuted_halos(space_total, cap, table_ref, index_ref, outer_ref, received, pool_ref, raw_ref):
    comps = outer_ref.shape[0]
    for k, part in enumerate(received):
        pool_ref[pl.ds(k * POOLED * 2 * cap, comps * 2 * cap), :] = part[...]
    own_base = (space_total - 1) * POOLED * 2 * cap
    for c in range(comps):
        for l in range(2):
            pool_ref[pl.ds(own_base + (2 * c + l) * FACES, FACES), :] = outer_ref[c, l]
    for f in range(FACES):
        base, per_comp, per_layer = table_ref[f], table_ref[FACES + f], table_ref[2 * FACES + f]
        for c in range(comps):
            for l in range(2):
                row = base + c * per_comp + l * per_layer
                raw_ref[c, l, pl.ds(f, 1), :] = pool_ref[pl.ds(row, 1), :]
    masks, lanes = [], []
    for h in range(2):
        index = index_ref[:, pl.ds(128 * h, 128)]
        lanes.append(index & 127)
        masks.append(index < 128)
    for c in reversed(range(comps)):
        for l in range(2):
            low, high = raw_ref[c, l, :, pl.ds(0, 128)], raw_ref[c, l, :, pl.ds(128, 128)]
            for h in range(2):
                a = jnp.take_along_axis(low, lanes[h], axis=1)
                b = jnp.take_along_axis(high, lanes[h], axis=1)
                yield c, l, h, jnp.where(masks[h], a, b)


def halo_kernel(space_total, cap, table_ref, index_ref, outer_ref, *more):
    received, (halo_ref, pool_ref, raw_ref) = more[: space_total - 1], more[space_total - 1 :]
    for c, l, h, halo in permuted_halos(
        space_total, cap, table_ref, index_ref, outer_ref, received, pool_ref, raw_ref
    ):
        halo_ref[c, l, :, pl.ds(128 * h, 128)] = halo


def next_halo_kernel(
    space_total, cap, table_ref, index_ref, weight_ref, outer_ref, across_ref, far_ref, *more
):
    received, (halo_ref, pool_ref, raw_ref) = more[: space_total - 1], more[space_total - 1 :]
    omega, w_own, w_across, w_near, w_far = coefficients(weight_ref)
    gain = {}
    for c, l, h, halo in permuted_halos(
        space_total, cap, table_ref, index_ref, outer_ref, received, pool_ref, raw_ref
    ):
        if c == COMPS:
            gain[l, h] = halo
            continue
        lanes = pl.ds(128 * h, 128)
        lacking = w_across * across_ref[c, l, :, lanes] + w_far * far_ref[c, l, :, lanes]
        halo_ref[c, l, :, lanes] = halo - gain[l, h] * lacking


def outer_kernel(
    cap, table_ref, weight_ref, rows_ref, vrows_ref, halo_ref, sibling_ref, outer_ref, *more
):
    sends, near_ref, lower_ref = more[:-2], more[-2], more[-1]
    omega, w_own, w_across, w_near, w_far = coefficients(weight_ref)
    load = row_loader(lambda c, r: rows_ref[c, r], halo_ref)
    even = even_tiles(vrows_ref.shape[1:])
    low = {r: load(r) for r in range(-2, 4)}
    high = {r: load(r) for r in range(4, 10)}
    picked = {
        k: [jnp.where(even, a, b) for a, b in zip(low[k - 2], high[k + 4])] for k in range(6)
    }
    rows = Rows(lambda k: picked[k])
    for c in range(COMPS):
        for l in range(2):
            q = picked[l + 2][c]
            near_ref[0, c, l] = turn(q, -1)
            near_ref[1, c, l] = turn(q, -2)
            near_ref[2, c, l] = turn(q, 1)
    rates = []
    for l in range(2):
        q = picked[l + 2]
        u, v, p = rows.uvp(l + 2)
        upper, lower = pitchwise_faces(q, v, p, near_ref, l)
        along = rows.along(l + 2)
        volume = jnp.where(even, vrows_ref[l], vrows_ref[l + 6])
        rate = own_instance_rate(jnp.abs(u) + jnp.abs(v), volume, omega)
        rates.append(rate)
        outer_ref[COMPS, l] = rate * volume
        for c in range(COMPS):
            sibling = jnp.where(even, sibling_ref[c, l], sibling_ref[c, l + 6])
            spectral = w_own * q[c] + w_near * sibling
            outer_ref[c, l] = q[c] - rate * (along[c] + upper[c] + volume * spectral)
            lower_ref[c, l] = lower[c]
    for l in range(2):
        for c in range(COMPS):
            outer_ref[c, l] = outer_ref[c, l] + rates[l] * turn(lower_ref[c, l], 1)
    pack_sends(cap, outer_ref, table_ref, sends)


def sweep(load, halo_ref, vrows_ref, omega, term, next_ref, near_ref, lower_ref, rate_ref):
    pitchwise_shifts(load, near_ref)
    rows = Rows(row_loader(load, halo_ref))
    for r in range(8):
        q = rows.q(r)
        u, v, p = rows.uvp(r)
        upper, lower = pitchwise_faces(q, v, p, near_ref, r)
        along = rows.along(r)
        volume = vrows_ref[r]
        rate = own_instance_rate(jnp.abs(u) + jnp.abs(v), volume, omega)
        rate_ref[r] = rate
        for c in range(COMPS):
            next_ref[c, r] = q[c] - rate * (along[c] + upper[c] + volume * term(c, r, q[c]))
            lower_ref[c, r] = lower[c]
    for r in range(8):
        rate = rate_ref[r]
        for c in range(COMPS):
            next_ref[c, r] = next_ref[c, r] + rate * turn(lower_ref[c, r], 1)


def own_kernel(
    weight_ref, rows_ref, vrows_ref, halo_ref, sibling_ref,
    next_ref, gain_ref, near_ref, lower_ref
):
    omega, w_own, w_across, w_near, w_far = coefficients(weight_ref)
    sweep(
        lambda c, r: rows_ref[c, r], halo_ref, vrows_ref, omega,
        lambda c, r, q: w_own * q + w_near * sibling_ref[c, r],
        next_ref, near_ref, lower_ref, gain_ref,
    )
    for r in range(8):
        gain_ref[r] = gain_ref[r] * vrows_ref[r]


def across_kernel(
    weight_ref, rows_ref, vrows_ref, halo_ref, across_ref, sibling_ref, own_ref, own_gain_ref,
    next_ref, gain_ref, own_next_ref, near_ref, lower_ref, half_ref, state_ref
):
    omega, w_own, w_across, w_near, w_far = coefficients(weight_ref)
    rows_from(across_ref, half_ref, state_ref)
    sweep(
        lambda c, r: state_ref[c, r], halo_ref, vrows_ref, omega,
        lambda c, r, q: w_own * q + w_across * rows_ref[c, r] + w_far * sibling_ref[c, r],
        next_ref, near_ref, lower_ref, gain_ref,
    )
    for r in range(8):
        gain_ref[r] = gain_ref[r] * vrows_ref[r]
        gain = own_gain_ref[r] * w_across
        for c in range(COMPS):
            own_next_ref[c, r] = own_ref[c, r] - gain * state_ref[c, r]


def finish_kernel(
    weight_ref, own_ref, own_gain_ref, across_ref, across_gain_ref, far_ref,
    next_ref, partial_ref, send_ref, half_ref, state_ref
):
    omega, w_own, w_across, w_near, w_far = coefficients(weight_ref)
    rows_from(far_ref, half_ref, state_ref)
    for r in range(8):
        own_gain, across_gain = own_gain_ref[r] * w_far, across_gain_ref[r] * w_near
        for c in range(COMPS):
            far = state_ref[c, r]
            mine = own_ref[c, r] - own_gain * far
            other = across_ref[c, r] - across_gain * far
            next_ref[c, r] = mine
            partial_ref[c, r] = w_own * mine + w_across * other
            send_ref[c, r] = w_far * mine + w_near * other


def pitchwise_kernel(
    rows_ref, vrows_ref, partial_ref, weight_ref, sum_ref, rate_ref, near_ref, lower_ref
):
    load = lambda c, r: rows_ref[c, r]
    pitchwise_shifts(load, near_ref)
    for r in range(8):
        q = [load(c, r) for c in range(COMPS)]
        u, v, p = primitives(q)
        upper, lower = pitchwise_faces(q, v, p, near_ref, r)
        volume = vrows_ref[r]
        rate_ref[r] = own_instance_rate(jnp.abs(u) + jnp.abs(v), volume, weight_ref[0])
        for c in range(COMPS):
            sum_ref[c, r] = upper[c] + volume * partial_ref[c, r]
            lower_ref[c, r] = lower[c]
    for r in range(8):
        for c in range(COMPS):
            sum_ref[c, r] = sum_ref[c, r] - turn(lower_ref[c, r], 1)


def last_kernel(
    space_total, cap, table_ref, rows_ref, vrows_ref, halo_ref, sum_ref, rate_ref, received_ref,
    new_ref, residual_ref, new_half_ref, residual_half_ref
):
    own = Rows(row_loader(lambda c, r: rows_ref[c, r], halo_ref))
    live_slots = table_ref[3 * FACES + (space_total - 1) * cap]
    live = (lax.broadcasted_iota(jnp.int32, vrows_ref.shape[1:], 0) // 2) < live_slots
    for r in range(8):
        volume = vrows_ref[r]
        along = own.along(r)
        rate = rate_ref[r]
        inverse = 1.0 / volume
        for c in range(COMPS):
            residual = sum_ref[c, r] + along[c] + volume * received_ref[c, r]
            new = jnp.where(live, own.q(r)[c] - rate * residual, 0.0)
            scaled = jnp.where(live, residual * inverse, 0.0)
            for h in range(2):
                lanes = slice(128 * h, 128 * h + 128)
                new_half_ref[c, h, pl.ds(r, 8, stride=8), :] = new[:, lanes]
                residual_half_ref[c, h, pl.ds(r, 8, stride=8), :] = scaled[:, lanes]
    for c in range(COMPS):
        for h in range(2):
            new_ref[c, :, pl.ds(128 * h, 128)] = new_half_ref[c, h]
            residual_ref[c, :, pl.ds(128 * h, 128)] = residual_half_ref[c, h]


def after_kernel(value_ref, first_ref, out_ref):
    pass


def hold(x):
    return pltpu.with_memory_space_constraint(x, pltpu.VMEM)


def four_instances(
    flow_state, cell_volume, frequency, block_count, block_place, face_links, face_offset, face_flip
):
    _, comps, row_count, width = flow_state.shape
    space_total = lax.axis_size("space")
    block_total = block_place.shape[0]
    cap = pair_cap(space_total, block_total)
    state = flow_state[0]

    def over_inst(x, flip):
        return lax.ppermute(x, "inst", [(i, i ^ flip) for i in range(4)])

    def over_space(parts):
        return [
            lax.ppermute(x, "space", [(i, (i + k + 1) % space_total) for i in range(space_total)])
            for k, x in enumerate(parts)
        ]

    full = (comps, 8, 8, width)
    outer = (comps, 2, 8, width)
    plane = (8, 8, width)
    pooled = (POOLED, 2, 8, width)
    entries = 3 * FACES + (space_total - 1) * cap + 1
    on_chip = lambda shape, dtype=F32: pltpu.VMEM(shape, dtype)
    sends_shape = lambda n: [on_chip((n * 2 * cap, width)) for _ in range(space_total - 1)]
    shifts = [pltpu.VMEM((3,) + full, F32), pltpu.VMEM(full, F32)]

    def call(kernel, out, specs, args, scratch=(), micros=0.3, out_specs=None, aliases={}):
        args = [hold(x) if spec is VMEM else x for spec, x in zip(specs, args)]
        return pl.pallas_call(
            kernel,
            out_shape=out,
            in_specs=specs,
            out_specs=out_specs or jax.tree.map(lambda _: VMEM, out),
            scratch_shapes=list(scratch),
            input_output_aliases=aliases,
            compiler_params=pltpu.CompilerParams(vmem_limit_bytes=8 << 20),
            cost_estimate=pl.CostEstimate(
                flops=0, bytes_accessed=1, transcendentals=0
            ),
        )(*args)

    in_smem = lambda x: pltpu.with_memory_space_constraint(x, pltpu.SMEM)
    far_off = pl.BlockSpec(memory_space=pltpu.HBM)
    packed = call(
        functools.partial(pack_kernel, space_total, block_total, cap),
        [
            on_chip(full), on_chip(plane), on_chip(outer),
            pltpu.SMEM((entries,), jnp.int32), pltpu.SMEM((8,), F32),
            on_chip((FACES, width), jnp.int32), *sends_shape(comps),
        ],
        [far_off] * 2 + [SMEM] * 6,
        (state, cell_volume, frequency, block_count, block_place, face_links.T, face_offset.T, face_flip.T),
        scratch=[
            pltpu.VMEM((2, comps + 1, row_count, 128), F32),
            pltpu.SemaphoreType.DMA((4,)),
            pltpu.SMEM((space_total,), jnp.int32),
            pltpu.SMEM((block_total,), jnp.int32),
        ],
        micros=2.0,
        out_specs=[VMEM] * 3 + [SMEM] * 2 + [VMEM] * space_total,
    )
    rows, vrows, outer_rows, table, weights, index = packed[:6]
    sends = packed[6:]
    table, weights = in_smem(table), in_smem(weights)
    halves = [pltpu.VMEM((comps, 2, row_count, 128), F32), pltpu.VMEM(full, F32)]
    pool = [
        pltpu.VMEM(((space_total - 1) * POOLED * 2 * cap + POOLED * 2 * FACES, width), F32),
        pltpu.VMEM(pooled, F32),
    ]

    across = over_inst(state, 2)
    sibling = over_inst(rows, 1)
    received = over_space(sends)
    halo = call(
        functools.partial(halo_kernel, space_total, cap),
        on_chip(outer),
        [SMEM] + [VMEM] * (1 + space_total),
        (table, index, outer_rows, *received),
        scratch=pool,
    )
    across_halo = over_inst(halo, 2)
    next_outer, *next_sends = call(
        functools.partial(outer_kernel, cap),
        [on_chip(pooled), *sends_shape(POOLED)],
        [SMEM, SMEM] + [VMEM] * 4,
        (table, weights, rows, vrows, halo, sibling),
        scratch=[pltpu.VMEM((3,) + outer, F32), pltpu.VMEM(outer, F32)],
        micros=0.4,
    )
    next_received = over_space(next_sends)
    far_halo = over_inst(across_halo, 1)
    own, own_gain = call(
        own_kernel,
        [on_chip(full), on_chip(plane)],
        [SMEM] + [VMEM] * 4,
        (weights, rows, vrows, halo, sibling),
        scratch=shifts,
        micros=0.8,
    )
    across = call(
        after_kernel, on_chip(state.shape), [VMEM] * 2, (across, next_outer), aliases={0: 0}, micros=0.05
    )
    far = over_inst(across, 1)
    across_next, across_gain, own = call(
        across_kernel,
        [on_chip(full), on_chip(plane), on_chip(full)],
        [SMEM] + [VMEM] * 7,
        (weights, rows, vrows, across_halo, across, sibling, own, own_gain),
        scratch=shifts + halves,
        micros=0.9,
    )
    next_rows, partial, to_sibling = call(
        finish_kernel,
        [on_chip(full)] * 3,
        [SMEM] + [VMEM] * 5,
        (weights, own, own_gain, across_next, across_gain, far),
        scratch=halves,
    )
    from_sibling = over_inst(to_sibling, 1)
    total, rate = call(
        pitchwise_kernel,
        [on_chip(full), on_chip(plane)],
        [VMEM] * 3 + [SMEM],
        (next_rows, vrows, partial, weights),
        scratch=shifts,
        micros=0.6,
    )
    next_halo = call(
        functools.partial(next_halo_kernel, space_total, cap),
        on_chip(outer),
        [SMEM, VMEM, SMEM] + [VMEM] * (2 + space_total),
        (table, index, weights, next_outer, across_halo, far_halo, *next_received),
        scratch=pool,
    )
    new, residual = call(
        functools.partial(last_kernel, space_total, cap),
        [jax.ShapeDtypeStruct(state.shape, F32)] * 2,
        [SMEM] + [VMEM] * 6,
        (table, next_rows, vrows, next_halo, total, rate, from_sibling),
        scratch=[pltpu.VMEM((comps, 2, row_count, 128), F32)] * 2,
        micros=1.5,
    )
    return new[None], residual[None]


def spectral_matrix(instance_total, omega_value):
    position = jnp.arange(instance_total, dtype=jnp.int32)
    distance = (position[:, None] - position[None, :]) % instance_total
    parity = (1 - 2 * (distance % 2)).astype(jnp.float32)
    phase_angle = jnp.pi * distance.astype(jnp.float32) / instance_total
    safe_angle = jnp.where(distance == 0, 0.5 * jnp.pi, phase_angle)
    first_derivative = jnp.where(
        distance == 0, 0.0, 0.5 * parity * jnp.cos(safe_angle) / jnp.sin(safe_angle)
    )
    second_derivative = jnp.where(
        distance == 0,
        -(instance_total * instance_total + 2) / 12.0,
        -parity / (2.0 * jnp.sin(safe_angle) ** 2),
    )
    return omega_value * (first_derivative - TIME_VISCOSITY * second_derivative)


def block_tables(
    block_count, block_place, face_links, face_offset, face_flip, targets, slot_count, width
):
    block_total = block_place.shape[0]
    first_position = jnp.cumsum(block_count) - block_count
    block_at_position = (
        jnp.zeros((block_total,), jnp.int32)
        .at[block_place]
        .set(jnp.arange(block_total, dtype=jnp.int32))
    )
    owner_device = jnp.sum(
        (block_place[:, None] >= first_position[None, 1:]).astype(jnp.int32), axis=1
    )
    flat_slot = owner_device * slot_count + block_place - first_position[owner_device]
    target_device = targets // slot_count
    target_slot = targets % slot_count
    is_live = target_slot < block_count[target_device]
    block_index = block_at_position[
        jnp.clip(first_position[target_device] + target_slot, 0, block_total - 1)
    ]
    neighbour = face_links[block_index]
    source_slot = jnp.where(neighbour >= 0, flat_slot[jnp.clip(neighbour, 0, block_total - 1)], -1)
    column = jnp.arange(width, dtype=jnp.int32)
    flipped = face_flip[block_index][:, :, None]
    ordered = jnp.where(flipped == 1, width - 1 - column, column)
    column_index = (face_offset[block_index][:, :, None] + ordered) % width
    return (is_live, source_slot, column_index)


def attach_halos(blocks, lower, upper, source_slot):
    cells_i = blocks.shape[2]
    lower = jnp.where(
        (source_slot[:, 0] >= 0)[None, :, None, None],
        lower,
        jnp.repeat(blocks[:, :, 0:1], 2, axis=2),
    )
    upper = jnp.where(
        (source_slot[:, 1] >= 0)[None, :, None, None],
        upper,
        jnp.repeat(blocks[:, :, cells_i - 1 : cells_i], 2, axis=2),
    )
    return jnp.concatenate([lower, blocks, upper], axis=2)


def fluxes(conserved):
    inverse_rho = 1.0 / conserved[0]
    velocity_i = conserved[1] * inverse_rho
    velocity_j = conserved[2] * inverse_rho
    pressure = (HEAT_RATIO - 1.0) * (
        conserved[4]
        - 0.5
        * (conserved[1] * conserved[1] + conserved[2] * conserved[2] + conserved[3] * conserved[3])
        * inverse_rho
    )
    flux_i = jnp.stack(
        [
            conserved[1],
            conserved[1] * velocity_i + pressure,
            conserved[2] * velocity_i,
            conserved[3] * velocity_i,
            (conserved[4] + pressure) * velocity_i,
            conserved[5] * velocity_i,
        ]
    )
    flux_j = jnp.stack(
        [
            conserved[2],
            conserved[1] * velocity_j,
            conserved[2] * velocity_j + pressure,
            conserved[3] * velocity_j,
            (conserved[4] + pressure) * velocity_j,
            conserved[5] * velocity_j,
        ]
    )
    return (flux_i, flux_j, jnp.abs(velocity_i), jnp.abs(velocity_j))


def advance(extended, volumes, spectral, omega_value, instance_total):
    cells_i = extended.shape[2] - 4
    flux_i, flux_j, speed_i, speed_j = fluxes(extended)
    left_cell = extended[:, :, 1 : cells_i + 2]
    right_cell = extended[:, :, 2 : cells_i + 3]
    back_cell = extended[:, :, 0 : cells_i + 1]
    ahead_cell = extended[:, :, 3 : cells_i + 4]
    radius_i = 0.5 * (speed_i[:, 1 : cells_i + 2] + speed_i[:, 2 : cells_i + 3]) + SOUND_SPEED
    face_i = 0.5 * (flux_i[:, :, 1 : cells_i + 2] + flux_i[:, :, 2 : cells_i + 3]) - radius_i * (
        SECOND_DISSIPATION * (right_cell - left_cell)
        - FOURTH_DISSIPATION * (ahead_cell - 3.0 * right_cell + 3.0 * left_cell - back_cell)
    )
    centre = extended[:, :, 2 : cells_i + 2]
    centre_flux = flux_j[:, :, 2 : cells_i + 2]
    centre_speed = speed_j[:, 2 : cells_i + 2]
    next_cell = jnp.roll(centre, -1, axis=-1)
    prior_cell = jnp.roll(centre, 1, axis=-1)
    far_cell = jnp.roll(centre, -2, axis=-1)
    radius_j = 0.5 * (centre_speed + jnp.roll(centre_speed, -1, axis=-1)) + SOUND_SPEED
    face_j = 0.5 * (centre_flux + jnp.roll(centre_flux, -1, axis=-1)) - radius_j * (
        SECOND_DISSIPATION * (next_cell - centre)
        - FOURTH_DISSIPATION * (far_cell - 3.0 * next_cell + 3.0 * centre - prior_cell)
    )
    residual_sum = (
        face_i[:, :, 1:]
        - face_i[:, :, :-1]
        + (face_j - jnp.roll(face_j, 1, axis=-1))
        + volumes * spectral
    )
    step_rate = COURANT / (
        speed_i[:, 2 : cells_i + 2]
        + centre_speed
        + 2.0 * SOUND_SPEED
        + volumes * omega_value * 0.5 * instance_total
    )
    return (centre - step_rate * residual_sum, residual_sum / volumes)


def select_faces(selector, slabs):
    return jnp.einsum("tf,lcfxw->lctxw", selector, slabs, precision=lax.Precision.HIGHEST)


def orient_faces(slabs, permuter):
    return jnp.einsum("lctxw,tvw->lctxv", slabs, permuter, precision=lax.Precision.HIGHEST)


def on_device(
    flow_state, cell_volume, frequency, block_count, block_place, face_links, face_offset, face_flip
):
    local_count, comps, row_count, width = flow_state.shape
    slot_count = BLOCKS_MAX
    cells_i = row_count // slot_count
    space_total = lax.axis_size("space")
    space_index = lax.axis_index("space")
    targets = space_index * slot_count + jnp.arange(slot_count, dtype=jnp.int32)
    is_live, source_slot, column_index = block_tables(
        block_count, block_place, face_links, face_offset, face_flip, targets, slot_count, width
    )
    column = jnp.arange(width, dtype=jnp.int32)
    permuter = (
        column_index.reshape(slot_count * 2, width)[:, :, None] == column[None, None, :]
    ).astype(jnp.float32)
    side_index = jnp.arange(2, dtype=jnp.int32)[None, :]
    volumes = cell_volume.reshape(slot_count, cells_i, width)
    instance_total = local_count * lax.axis_size("inst")
    matrix = spectral_matrix(instance_total, frequency[0])
    row_offset = lax.axis_index("inst") * local_count
    own_rows = lax.dynamic_slice_in_dim(matrix, row_offset, local_count, 0)
    wanted_face = (source_slot * 2 + (1 - side_index)).reshape(-1)
    face_range = jnp.arange(space_total * slot_count * 2, dtype=jnp.int32)
    selector = (
        (wanted_face[:, None] == face_range[None, :]) & (source_slot.reshape(-1)[:, None] >= 0)
    ).astype(jnp.float32)
    current = flow_state
    last_residual = jnp.zeros_like(flow_state)
    for iteration in range(PSEUDO_STEPS):
        spectral_all = jnp.einsum(
            "nm,mcrb->ncrb",
            own_rows,
            lax.all_gather(current, "inst", axis=0, tiled=True),
            precision=lax.Precision.HIGHEST,
        )
        blocks = current.reshape(local_count, comps, slot_count, cells_i, width)
        faces = jnp.stack([blocks[:, :, :, 0:2], blocks[:, :, :, cells_i - 2 : cells_i]], axis=3)
        gathered = lax.all_gather(faces, "space", axis=2, tiled=True)
        gathered = gathered.reshape(local_count, comps, space_total * slot_count * 2, 2, width)
        arrived = select_faces(selector, gathered)
        oriented = orient_faces(arrived, permuter).reshape(
            local_count, comps, slot_count, 2, 2, width
        )

        def one_instance(own_blocks, slabs, spectral):
            extended = attach_halos(own_blocks, slabs[:, :, 0], slabs[:, :, 1], source_slot)
            return advance(
                extended,
                volumes,
                spectral.reshape(comps, slot_count, cells_i, width),
                frequency[0],
                instance_total,
            )

        updated, residual_now = jax.vmap(one_instance)(blocks, oriented, spectral_all)
        current = updated.reshape(flow_state.shape)
        last_residual = residual_now.reshape(flow_state.shape)
    row_live = jnp.repeat(is_live, cells_i)[None, None, :, None]
    return (jnp.where(row_live, current, 0.0), jnp.where(row_live, last_residual, 0.0))


def solution(mesh):
    return jax.shard_map(
        four_instances if mesh.shape["inst"] == 4 else on_device,
        mesh=mesh,
        in_specs=(
            P(("groups", "inst"), None, "space", None),
            P(("groups", "space"), None),
            P(),
            P("groups"),
            P("groups"),
            P("groups", None),
            P("groups", None),
            P("groups", None),
        ),
        out_specs=(
            P(("groups", "inst"), None, "space", None),
            P(("groups", "inst"), None, "space", None),
        ),
        check_vma=False,
    )
```

```python
import functools
import math

import jax
import jax.numpy as jnp
from jax import lax
from jax.experimental import pallas as pl
from jax.experimental.pallas import tpu as pltpu
from jax.sharding import PartitionSpec as P

BLOCKS_MAX = 4
PSEUDO_STEPS = 2


HEAT_RATIO = 1.4
SECOND_DISSIPATION = 0.05
FOURTH_DISSIPATION = 0.02
SOUND_SPEED = 1.0
COURANT = 0.5
TIME_VISCOSITY = 0.25

COMPS = 6
FACES = 2 * BLOCKS_MAX
POOLED = COMPS + 1
F32 = jnp.float32
VMEM = pl.BlockSpec(memory_space=pltpu.VMEM)
SMEM = pl.BlockSpec(memory_space=pltpu.SMEM)
HBM = pl.BlockSpec(memory_space=pltpu.HBM)


def spectral_weights(total):
    weights = [TIME_VISCOSITY * (total * total + 2) / 12.0]
    for k in range(1, total):
        sign = 1.0 - 2.0 * (k % 2)
        angle = math.pi * k / total
        first = 0.5 * sign * math.cos(angle) / math.sin(angle)
        second = -sign / (2.0 * math.sin(angle) ** 2)
        weights.append(first - TIME_VISCOSITY * second)
    return weights


def exchanges(total):
    return [2, 3, 1] if total == 4 else list(range(1, total))


def partner(device, k, total):
    return device ^ k if total & (total - 1) == 0 else (device + k) % total


def apart(device, source, total):
    return device ^ source if total & (total - 1) == 0 else (device - source + total) % total


def pair_cap(space_total, block_total):
    second_most = min(BLOCKS_MAX, block_total - BLOCKS_MAX - (space_total - 2))
    return 2 * max(1, second_most)


def primitives(q):
    inverse = 1.0 / q[0]
    u = q[1] * inverse
    v = q[2] * inverse
    p = (HEAT_RATIO - 1.0) * (
        q[4] - 0.5 * (q[1] * q[1] + q[2] * q[2] + q[3] * q[3]) * inverse
    )
    return u, v, p


def flux_along_i(q, u, p):
    return [q[1], q[1] * u + p, q[2] * u, q[3] * u, (q[4] + p) * u, q[5] * u]


def flux_along_j(q, v, p):
    return [q[2], q[1] * v, q[2] * v + p, q[3] * v, (q[4] + p) * v, q[5] * v]


def ahead(x):
    return pltpu.roll(x, x.shape[1] - 1, axis=1)


def behind(x):
    return pltpu.roll(x, 1, axis=1)


DIFF_ONE = SECOND_DISSIPATION + 2.0 * FOURTH_DISSIPATION


def turn(x, shift):
    return pltpu.roll(x, shift % x.shape[1], axis=1)


def pitchwise_shifts(load, near_ref):
    for c in range(COMPS):
        for r in range(8):
            q = load(c, r)
            near_ref[0, c, r] = turn(q, -1)
            near_ref[1, c, r] = turn(q, -2)
            near_ref[2, c, r] = turn(q, 1)


def pitchwise_faces(q, v, p, near_ref, r):
    after = [near_ref[0, c, r] for c in range(COMPS)]
    _, v_after, p_after = primitives(after)
    radius = 0.5 * (jnp.abs(v) + jnp.abs(v_after)) + SOUND_SPEED
    here, there = flux_along_j(q, v, p), flux_along_j(after, v_after, p_after)
    upper, lower = [], []
    for c in range(COMPS):
        step = after[c] - q[c]
        others = (near_ref[1, c, r] - after[c]) + (q[c] - near_ref[2, c, r])
        damping = radius * (DIFF_ONE * step - FOURTH_DISSIPATION * others)
        upper.append(0.5 * there[c] - damping)
        lower.append(0.5 * here[c] - damping)
    return upper, lower


class Rows:
    def __init__(self, load):
        self.load = load
        self.state, self.prim, self.flux, self.steps, self.faces = {}, {}, {}, {}, {}

    def q(self, r):
        if r not in self.state:
            self.state[r] = self.load(r)
        return self.state[r]

    def uvp(self, r):
        if r not in self.prim:
            self.prim[r] = primitives(self.q(r))
        return self.prim[r]

    def f(self, r):
        if r not in self.flux:
            u, _, p = self.uvp(r)
            self.flux[r] = flux_along_i(self.q(r), u, p)
        return self.flux[r]

    def step(self, r):
        if r not in self.steps:
            self.steps[r] = [b - a for a, b in zip(self.q(r), self.q(r + 1))]
        return self.steps[r]

    def face(self, r):
        if r not in self.faces:
            radius = 0.5 * (jnp.abs(self.uvp(r)[0]) + jnp.abs(self.uvp(r + 1)[0])) + SOUND_SPEED
            out = []
            for c in range(COMPS):
                damping = DIFF_ONE * self.step(r)[c] - FOURTH_DISSIPATION * (
                    self.step(r + 1)[c] + self.step(r - 1)[c]
                )
                out.append(0.5 * (self.f(r)[c] + self.f(r + 1)[c]) - radius * damping)
            self.faces[r] = out
        return self.faces[r]

    def along(self, r):
        return [b - a for a, b in zip(self.face(r - 1), self.face(r))]


def even_tiles(shape):
    return lax.broadcasted_iota(jnp.int32, shape, 0) % 2 == 0


def row_loader(load, halo_ref):
    def extended(r):
        out = []
        for c in range(COMPS):
            if r < 0:
                inner = pltpu.roll(load(c, r + 8), 1, axis=0)
                out.append(jnp.where(even_tiles(inner.shape), halo_ref[c, r + 2], inner))
            elif r > 7:
                inner = pltpu.roll(load(c, r - 8), 7, axis=0)
                out.append(jnp.where(even_tiles(inner.shape), inner, halo_ref[c, r - 8]))
            else:
                out.append(load(c, r))
        return out

    return extended


def rows_from(raw_ref, half_ref, rows_ref):
    for c in range(COMPS):
        for h in range(2):
            half_ref[c, h] = raw_ref[c, :, pl.ds(128 * h, 128)]
    for c in range(COMPS):
        for r in range(8):
            for h in range(2):
                rows_ref[c, r, :, pl.ds(128 * h, 128)] = half_ref[c, h, pl.ds(r, 8, stride=8), :]


def weight_kernel(frequency_ref, weight_ref):
    weights = spectral_weights(4)
    omega = frequency_ref[0]
    even = lax.axis_index("inst") % 2 == 0
    weight_ref[0] = omega
    weight_ref[1] = omega * F32(weights[0])
    weight_ref[2] = omega * F32(weights[2])
    weight_ref[3] = omega * jnp.where(even, F32(weights[3]), F32(weights[1]))
    weight_ref[4] = omega * jnp.where(even, F32(weights[1]), F32(weights[3]))


def coefficients(weight_ref):
    return [weight_ref[k] for k in range(5)]


def own_instance_rate(speeds, volume, omega):
    return COURANT / (speeds + 2.0 * SOUND_SPEED + volume * (omega * (0.5 * 4)))


def pack_kernel(
    space_total, block_total, cap,
    state_ref, volume_ref, counts_in, place_in, links_in, offset_in, flip_in,
    rows_ref, vrows_ref, outer_ref, table_ref, index_ref, *more
):
    sends = more[: space_total - 1]
    half_ref, arrival, first_ref, inverse_ref, *small = more[space_total - 1 :]
    counts_ref, place_ref, links_ref, offset_ref, flip_ref = small
    width = state_ref.shape[2]
    moves = list(zip([counts_in, place_in, links_in, offset_in, flip_in], small))
    for h in range(2):
        lanes = pl.ds(128 * h, 128)
        moves.append((state_ref.at[:, :, lanes], half_ref.at[h, pl.ds(0, COMPS)]))
        moves.append((volume_ref.at[:, lanes], half_ref.at[h, COMPS]))
    copies = [
        pltpu.make_async_copy(source, target, arrival.at[n])
        for n, (source, target) in enumerate(moves)
    ]
    for copy in copies:
        copy.start()
    for copy in copies[: len(small)]:
        copy.wait()
    me = lax.axis_index("space")
    total = jnp.int32(0)
    firsts = []
    for d in range(space_total):
        firsts.append(total)
        first_ref[d] = total
        total = total + counts_ref[d]
    for b in range(block_total):
        inverse_ref[place_ref[b]] = jnp.int32(b)

    def block_in(device, slot):
        return inverse_ref[jnp.minimum(first_ref[device] + slot, block_total - 1)]

    def source_of(block, side):
        link = links_ref[side, block]
        place = place_ref[jnp.maximum(link, 0)]
        owner = jnp.int32(0)
        first = jnp.int32(0)
        for d in range(1, space_total):
            past = place >= firsts[d]
            owner = jnp.where(past, d, owner)
            first = jnp.where(past, firsts[d], first)
        return link, owner, 2 * (place - first) + (1 - side)

    own_base = (space_total - 1) * POOLED * 2 * cap
    few = 2 * counts_ref[me] <= cap
    table_ref[3 * FACES + (space_total - 1) * cap] = counts_ref[me]
    tile = lax.broadcasted_iota(jnp.int32, (FACES, width), 0)
    start = jnp.zeros((FACES, width), jnp.int32)
    turned = jnp.zeros((FACES, width), jnp.int32)
    for f in range(FACES):
        slot, side = f // 2, f % 2
        block = block_in(me, slot)
        link, owner, source = source_of(block, side)
        shift = apart(me, owner, space_total)
        listed = 2 * counts_ref[owner] <= cap
        place = jnp.where(listed, jnp.minimum(source, cap - 1), min(f, cap - 1))
        outside = link < 0
        mine = owner == me
        base = jnp.where(mine, own_base + source, (shift - 1) * (POOLED * 2 * cap) + place)
        base = jnp.where(outside, own_base + 8 * side + f, base)
        table_ref[f] = base
        table_ref[FACES + f] = jnp.where(outside | mine, 2 * FACES, 2 * cap)
        table_ref[2 * FACES + f] = jnp.where(outside, 0, jnp.where(mine, FACES, cap))
        start = jnp.where(tile == f, jnp.where(outside, 0, offset_ref[side, block]), start)
        turned = jnp.where(tile == f, jnp.where(outside, 0, flip_ref[side, block]), turned)
    column = lax.broadcasted_iota(jnp.int32, (FACES, width), 1)
    index_ref[...] = (start + jnp.where(turned == 1, width - 1 - column, column)) % width
    for k in range(1, space_total):
        target = partner(me, k, space_total)
        for i in range(cap):
            _, owner, source = source_of(block_in(target, i // 2), i % 2)
            wanted = jnp.where(owner == me, source, 0)
            table_ref[3 * FACES + (k - 1) * cap + i] = jnp.where(few, i, wanted)
    for copy in copies[len(small) :]:
        copy.wait()
    for c in range(COMPS + 1):
        for r in range(8):
            for h in range(2):
                row = half_ref[h, c, pl.ds(r, 8, stride=8), :]
                if c < COMPS:
                    rows_ref[c, r, :, pl.ds(128 * h, 128)] = row
                else:
                    vrows_ref[r, :, pl.ds(128 * h, 128)] = row
    even = even_tiles((8, width))
    for c in range(COMPS):
        for l in range(2):
            low, high = rows_ref[c, l], rows_ref[c, 6 + l]
            outer_ref[c, l] = jnp.where(even, low, high)
    pack_sends(cap, outer_ref, table_ref, sends)


def pack_sends(cap, outer_ref, table_ref, sends):
    for k, send_ref in enumerate(sends):
        for i in range(cap):
            f = table_ref[3 * FACES + k * cap + i]
            for c in range(outer_ref.shape[0]):
                for l in range(2):
                    send_ref[pl.ds((2 * c + l) * cap + i, 1), :] = outer_ref[c, l, pl.ds(f, 1), :]


def permuted_halos(space_total, cap, table_ref, index_ref, outer_ref, received, pool_ref, raw_ref):
    comps = outer_ref.shape[0]
    for k, part in zip(exchanges(len(received) + 1), received):
        pool_ref[pl.ds((k - 1) * POOLED * 2 * cap, comps * 2 * cap), :] = part[...]
    own_base = (space_total - 1) * POOLED * 2 * cap
    for c in range(comps):
        for l in range(2):
            pool_ref[pl.ds(own_base + (2 * c + l) * FACES, FACES), :] = outer_ref[c, l]
    for f in range(FACES):
        base, per_comp, per_layer = table_ref[f], table_ref[FACES + f], table_ref[2 * FACES + f]
        for c in range(comps):
            for l in range(2):
                row = base + c * per_comp + l * per_layer
                raw_ref[c, l, pl.ds(f, 1), :] = pool_ref[pl.ds(row, 1), :]
    masks, lanes = [], []
    for h in range(2):
        index = index_ref[:, pl.ds(128 * h, 128)]
        lanes.append(index & 127)
        masks.append(index < 128)
    for c in reversed(range(comps)):
        for l in range(2):
            low, high = raw_ref[c, l, :, pl.ds(0, 128)], raw_ref[c, l, :, pl.ds(128, 128)]
            for h in range(2):
                a = jnp.take_along_axis(low, lanes[h], axis=1)
                b = jnp.take_along_axis(high, lanes[h], axis=1)
                yield c, l, h, jnp.where(masks[h], a, b)


def halo_kernel(space_total, cap, table_ref, index_ref, outer_ref, _, __, *more):
    received, (halo_ref, pool_ref, raw_ref) = more[: space_total - 1], more[space_total - 1 :]
    for c, l, h, halo in permuted_halos(
        space_total, cap, table_ref, index_ref, outer_ref, received, pool_ref, raw_ref
    ):
        halo_ref[c, l, :, pl.ds(128 * h, 128)] = halo


def next_halo_kernel(
    space_total, cap, table_ref, index_ref, weight_ref, outer_ref, across_ref, _, *more
):
    received, halos = more[: space_total - 1], more[space_total - 1 : -4]
    halo_ref, pool_ref, raw_ref, far_ref = more[-4:]
    join_halos(halos, far_ref)
    omega, w_own, w_across, w_near, w_far = coefficients(weight_ref)
    gain = {}
    for c, l, h, halo in permuted_halos(
        space_total, cap, table_ref, index_ref, outer_ref, received, pool_ref, raw_ref
    ):
        if c == COMPS:
            gain[l, h] = halo
            continue
        lanes = pl.ds(128 * h, 128)
        lacking = w_across * across_ref[c, l, :, lanes] + w_far * far_ref[c, l, :, lanes]
        halo_ref[c, l, :, lanes] = halo - gain[l, h] * lacking


def pitchwise_kernel(weight_ref, rows_ref, vrows_ref, *more):
    part_ref, rate_ref, near_ref, lower_ref = more[-4:]
    pitchwise(lambda c, r: rows_ref[c, r], vrows_ref, weight_ref[0], part_ref, rate_ref, near_ref, lower_ref)


def pitchwise(load, vrows_ref, omega, part_ref, rate_ref, near_ref, lower_ref):
    pitchwise_shifts(load, near_ref)
    for r in range(8):
        q = [load(c, r) for c in range(COMPS)]
        u, v, p = primitives(q)
        upper, lower = pitchwise_faces(q, v, p, near_ref, r)
        rate_ref[r] = own_instance_rate(jnp.abs(u) + jnp.abs(v), vrows_ref[r], omega)
        for c in range(COMPS):
            part_ref[c, r] = upper[c]
            lower_ref[c, r] = lower[c]
    for r in range(8):
        for c in range(COMPS):
            part_ref[c, r] = part_ref[c, r] - turn(lower_ref[c, r], 1)


def outer_kernel(
    cap, table_ref, weight_ref, rows_ref, vrows_ref, part_ref, rate_ref, halo_ref, sibling_ref,
    outer_ref, *sends
):
    omega, w_own, w_across, w_near, w_far = coefficients(weight_ref)
    load = row_loader(lambda c, r: rows_ref[c, r], halo_ref)
    even = even_tiles(vrows_ref.shape[1:])
    low = {r: load(r) for r in range(-2, 4)}
    high = {r: load(r) for r in range(4, 10)}
    picked = {
        k: [jnp.where(even, a, b) for a, b in zip(low[k - 2], high[k + 4])] for k in range(6)
    }
    rows = Rows(lambda k: picked[k])
    for l in range(2):
        along = rows.along(l + 2)
        volume = jnp.where(even, vrows_ref[l], vrows_ref[l + 6])
        rate = jnp.where(even, rate_ref[l], rate_ref[l + 6])
        outer_ref[COMPS, l] = rate * volume
        for c in range(COMPS):
            q = picked[l + 2][c]
            part = jnp.where(even, part_ref[c, l], part_ref[c, l + 6])
            sibling = jnp.where(even, sibling_ref[c, l], sibling_ref[c, l + 6])
            spectral = w_own * q + w_near * sibling
            outer_ref[c, l] = q - rate * (along[c] + part + volume * spectral)
    pack_sends(cap, outer_ref, table_ref, sends)


def near_kernel(
    weight_ref, vrows_ref,
    rows_ref, part_ref, rate_ref, halo_ref,
    sibling_ref, sibling_part_ref, sibling_rate_ref, sibling_halo_ref, _,
    next_ref, sibling_next_ref, gain_ref, sibling_gain_ref
):
    omega, w_own, w_across, w_near, w_far = coefficients(weight_ref)
    for one, other, weight, part, rate_of, halo, out, gain in (
        (rows_ref, sibling_ref, w_near, part_ref, rate_ref, halo_ref, next_ref, gain_ref),
        (sibling_ref, rows_ref, w_far, sibling_part_ref, sibling_rate_ref, sibling_halo_ref,
         sibling_next_ref, sibling_gain_ref),
    ):
        rows = Rows(row_loader(lambda c, r: one[c, r], halo))
        for r in range(8):
            along, volume, rate = rows.along(r), vrows_ref[r], rate_of[r]
            gain[r] = rate * volume
            for c in range(COMPS):
                spectral = w_own * one[c, r] + weight * other[c, r]
                out[c, r] = one[c, r] - rate * (along[c] + part[c, r] + volume * spectral)


def across_kernel(
    weight_ref, vrows_ref, rows_ref, sibling_ref, own_ref, own_gain_ref, sibling_next_ref,
    sibling_gain_ref, raw_ref, halo_ref,
    next_ref, term_ref, across_ref, lacking_ref, gain_ref,
    near_ref, lower_ref, half_ref, part_ref, rate_ref
):
    omega, w_own, w_across, w_near, w_far = coefficients(weight_ref)
    rows_from(raw_ref, half_ref, across_ref)
    load = lambda c, r: across_ref[c, r]
    pitchwise(load, vrows_ref, omega, part_ref, rate_ref, near_ref, lower_ref)
    rows = Rows(row_loader(load, halo_ref))
    for r in range(8):
        along, volume, rate = rows.along(r), vrows_ref[r], rate_ref[r]
        own_gain, sibling_gain, gain = own_gain_ref[r], sibling_gain_ref[r], rate * volume
        gain_ref[r] = (
            (w_own * w_far) * own_gain + (w_near * w_across) * sibling_gain + (w_across * w_near) * gain
        )
        lacking_ref[r] = w_far * own_gain
        for c in range(COMPS):
            q = across_ref[c, r]
            spectral = w_own * q + w_across * rows_ref[c, r] + w_far * sibling_ref[c, r]
            new = q - rate * (along[c] + part_ref[c, r] + volume * spectral)
            mine = own_ref[c, r] - (w_across * own_gain) * q
            sibling = sibling_next_ref[c, r] - (w_near * sibling_gain) * q
            next_ref[c, r] = mine
            term_ref[c, r] = w_own * mine + w_near * sibling + w_across * new


def far_pitchwise_kernel(
    weight_ref, vrows_ref, raw_ref, rows_ref, part_ref, rate_ref, near_ref, lower_ref, half_ref
):
    rows_from(raw_ref, half_ref, rows_ref)
    load = lambda c, r: rows_ref[c, r]
    pitchwise(load, vrows_ref, weight_ref[0], part_ref, rate_ref, near_ref, lower_ref)


def far_kernel(
    weight_ref, vrows_ref, rows_ref, sibling_ref, across_ref, own_ref, partial_ref,
    lacking_ref, lacking_term_ref, far_ref, part_ref, rate_ref, *more
):
    halos, (next_ref, term_ref, halo_ref) = more[:-3], more[-3:]
    omega, w_own, w_across, w_near, w_far = coefficients(weight_ref)
    join_halos(halos, halo_ref)
    rows = Rows(row_loader(lambda c, r: far_ref[c, r], halo_ref))
    for r in range(8):
        along, volume, rate = rows.along(r), vrows_ref[r], rate_ref[r]
        lacking, lacking_term = lacking_ref[r], lacking_term_ref[r]
        for c in range(COMPS):
            q = far_ref[c, r]
            spectral = (
                w_own * q + w_across * sibling_ref[c, r] + w_near * rows_ref[c, r]
                + w_far * across_ref[c, r]
            )
            new = q - rate * (along[c] + part_ref[c, r] + volume * spectral)
            next_ref[c, r] = own_ref[c, r] - lacking * q
            term_ref[c, r] = partial_ref[c, r] - lacking_term * q + w_far * new


def join_halos(parts, halo_ref):
    size = COMPS // len(parts)
    for n, part in enumerate(parts):
        for c in range(size):
            for l in range(2):
                halo_ref[n * size + c, l] = part[c, l]


def last_kernel(
    space_total, cap, table_ref, rows_ref, vrows_ref, halo_ref, part_ref, rate_ref, term_ref,
    new_ref, residual_ref, new_half_ref, residual_half_ref
):
    own = Rows(row_loader(lambda c, r: rows_ref[c, r], halo_ref))
    live_slots = table_ref[3 * FACES + (space_total - 1) * cap]
    live = (lax.broadcasted_iota(jnp.int32, vrows_ref.shape[1:], 0) // 2) < live_slots
    for r in range(8):
        volume = vrows_ref[r]
        along = own.along(r)
        rate = rate_ref[r]
        inverse = 1.0 / volume
        for c in range(COMPS):
            residual = part_ref[c, r] + along[c] + volume * term_ref[c, r]
            new = jnp.where(live, own.q(r)[c] - rate * residual, 0.0)
            scaled = jnp.where(live, residual * inverse, 0.0)
            for h in range(2):
                lanes = slice(128 * h, 128 * h + 128)
                new_half_ref[c, h, pl.ds(r, 8, stride=8), :] = new[:, lanes]
                residual_half_ref[c, h, pl.ds(r, 8, stride=8), :] = scaled[:, lanes]
    for c in range(COMPS):
        for h in range(2):
            new_ref[c, :, pl.ds(128 * h, 128)] = new_half_ref[c, h]
            residual_ref[c, :, pl.ds(128 * h, 128)] = residual_half_ref[c, h]


def after_kernel(value_ref, *more):
    pass


def four_instances(
    flow_state, cell_volume, frequency, block_count, block_place, face_links, face_offset, face_flip
):
    _, comps, row_count, width = flow_state.shape
    space_total = lax.axis_size("space")
    block_total = block_place.shape[0]
    cap = pair_cap(space_total, block_total)
    state = flow_state[0]

    def over_inst(x, flip):
        return lax.ppermute(x, "inst", [(i, i ^ flip) for i in range(4)])

    def over_space(parts):
        arrived = {
            k: lax.ppermute(
                parts[k - 1], "space", [(i, partner(i, k, space_total)) for i in range(space_total)]
            )
            for k in exchanges(space_total)
        }
        return [arrived[k] for k in exchanges(space_total)]

    full = (comps, 8, 8, width)
    outer = (comps, 2, 8, width)
    plane = (8, 8, width)
    pooled = (POOLED, 2, 8, width)
    entries = 3 * FACES + (space_total - 1) * cap + 1
    on_chip = lambda shape, dtype=F32: pltpu.VMEM(shape, dtype)
    sends_shape = lambda n: [on_chip((n * 2 * cap, width)) for _ in range(space_total - 1)]
    shifts = [pltpu.VMEM((3,) + full, F32), pltpu.VMEM(full, F32)]

    def call(kernel, out, specs, args, scratch=(), micros=0.3, out_specs=None, aliases={}):
        args = [
            pltpu.with_memory_space_constraint(x, spec.memory_space) for spec, x in zip(specs, args)
        ]
        return pl.pallas_call(
            kernel,
            out_shape=out,
            in_specs=specs,
            out_specs=out_specs or jax.tree.map(lambda _: VMEM, out),
            scratch_shapes=list(scratch),
            input_output_aliases=aliases,
            compiler_params=pltpu.CompilerParams(vmem_limit_bytes=12 << 20),
            cost_estimate=pl.CostEstimate(
                flops=0, bytes_accessed=int(micros * 3.69e6), transcendentals=0
            ),
        )(*args)

    packed = call(
        functools.partial(pack_kernel, space_total, block_total, cap),
        [
            on_chip(full), on_chip(plane), on_chip(outer),
            pltpu.SMEM((entries,), jnp.int32),
            on_chip((FACES, width), jnp.int32), *sends_shape(comps),
        ],
        [HBM] * 7,
        (state, cell_volume, block_count, block_place, face_links.T, face_offset.T, face_flip.T),
        scratch=[
            pltpu.VMEM((2, comps + 1, row_count, 128), F32),
            pltpu.SemaphoreType.DMA((9,)),
            pltpu.SMEM((space_total,), jnp.int32),
            pltpu.SMEM((block_total,), jnp.int32),
            pltpu.SMEM((space_total,), jnp.int32),
            pltpu.SMEM((block_total,), jnp.int32),
            *[pltpu.SMEM((2, block_total), jnp.int32)] * 3,
        ],
        micros=2.0,
        out_specs=[VMEM] * 3 + [SMEM] + [VMEM] * space_total,
    )
    rows, vrows, outer_rows, table, index = packed[:5]
    sends = packed[5:]
    weights = pl.pallas_call(
        weight_kernel, out_shape=pltpu.SMEM((8,), F32), in_specs=[SMEM], out_specs=SMEM
    )(frequency)
    halves = [pltpu.VMEM((comps, 2, row_count, 128), F32), pltpu.VMEM(full, F32)]
    pool = [
        pltpu.VMEM(((space_total - 1) * POOLED * 2 * cap + POOLED * 2 * FACES, width), F32),
        pltpu.VMEM(pooled, F32),
    ]

    def pitch(x, *first):
        return call(
            pitchwise_kernel,
            [on_chip(full), on_chip(plane)],
            [SMEM] + [VMEM] * (2 + len(first)),
            (weights, x, vrows, *first),
            scratch=shifts,
            micros=0.5,
        )

    across = over_inst(state, 2)
    sibling = over_inst(rows, 1)
    received = over_space(sends)
    part, rate = pitch(rows)
    sibling_part, sibling_rate = pitch(sibling, across)
    halo = call(
        functools.partial(halo_kernel, space_total, cap),
        on_chip(outer),
        [SMEM] + [VMEM] * (3 + space_total),
        (table, index, outer_rows, rate, sibling_rate, *received),
        scratch=pool,
    )
    across_halo = over_inst(halo, 2)
    sibling_halo = over_inst(halo, 1)
    next_outer, *next_sends = call(
        functools.partial(outer_kernel, cap),
        [on_chip(pooled), *sends_shape(POOLED)],
        [SMEM, SMEM] + [VMEM] * 6,
        (table, weights, rows, vrows, part, rate, halo, sibling),
        micros=0.3,
    )
    next_received = over_space(next_sends)
    def after(x, *first):
        return call(
            after_kernel, on_chip(x.shape), [VMEM] * (1 + len(first)), (x, *first), aliases={0: 0}, micros=0.05
        )

    far = over_inst(after(across, next_outer), 1)
    pieces = 2
    size = comps // pieces
    hx = across_halo
    far_halo = [over_inst(hx[n * size : n * size + size], 1) for n in range(pieces)]
    far_rows, far_part, far_rate = call(
        far_pitchwise_kernel,
        [on_chip(full)] * 2 + [on_chip(plane)],
        [SMEM] + [VMEM] * 2,
        (weights, vrows, far),
        scratch=shifts + halves[:1],
        micros=0.6,
    )
    own, sibling_next, own_gain, sibling_gain = call(
        near_kernel,
        [on_chip(full)] * 2 + [on_chip(plane)] * 2,
        [SMEM] + [VMEM] * 10,
        (weights, vrows, rows, part, rate, halo, sibling, sibling_part, sibling_rate, sibling_halo,
         far_rate),
        micros=0.7,
    )
    own, partial, across_rows, lacking, lacking_term = call(
        across_kernel,
        [on_chip(full)] * 3 + [on_chip(plane)] * 2,
        [SMEM] + [VMEM] * 9,
        (weights, vrows, rows, sibling, own, own_gain, sibling_next, sibling_gain, across, across_halo),
        scratch=shifts + halves[:1] + [halves[1], pltpu.VMEM(plane, F32)],
        micros=1.0,
    )
    next_rows, term = call(
        far_kernel,
        [on_chip(full)] * 2,
        [SMEM] + [VMEM] * (11 + len(far_halo)),
        (weights, vrows, rows, sibling, across_rows, own, partial, lacking, lacking_term,
         far_rows, far_part, far_rate, *far_halo),
        scratch=[pltpu.VMEM(outer, F32)],
        micros=0.5,
    )
    next_part, next_rate = pitch(next_rows)
    next_halo = call(
        functools.partial(next_halo_kernel, space_total, cap),
        on_chip(outer),
        [SMEM, VMEM, SMEM] + [VMEM] * (2 + space_total + len(far_halo)),
        (table, index, weights, next_outer, across_halo, next_rate, *next_received, *far_halo),
        scratch=pool + [pltpu.VMEM(outer, F32)],
    )
    new, residual = call(
        functools.partial(last_kernel, space_total, cap),
        [jax.ShapeDtypeStruct(state.shape, F32)] * 2,
        [SMEM] + [VMEM] * 6,
        (table, next_rows, vrows, next_halo, next_part, next_rate, term),
        scratch=[pltpu.VMEM((comps, 2, row_count, 128), F32)] * 2,
        micros=1.5,
    )
    return new[None], residual[None]


def spectral_matrix(instance_total, omega_value):
    position = jnp.arange(instance_total, dtype=jnp.int32)
    distance = (position[:, None] - position[None, :]) % instance_total
    parity = (1 - 2 * (distance % 2)).astype(jnp.float32)
    phase_angle = jnp.pi * distance.astype(jnp.float32) / instance_total
    safe_angle = jnp.where(distance == 0, 0.5 * jnp.pi, phase_angle)
    first_derivative = jnp.where(
        distance == 0, 0.0, 0.5 * parity * jnp.cos(safe_angle) / jnp.sin(safe_angle)
    )
    second_derivative = jnp.where(
        distance == 0,
        -(instance_total * instance_total + 2) / 12.0,
        -parity / (2.0 * jnp.sin(safe_angle) ** 2),
    )
    return omega_value * (first_derivative - TIME_VISCOSITY * second_derivative)


def block_tables(
    block_count, block_place, face_links, face_offset, face_flip, targets, slot_count, width
):
    block_total = block_place.shape[0]
    first_position = jnp.cumsum(block_count) - block_count
    block_at_position = (
        jnp.zeros((block_total,), jnp.int32)
        .at[block_place]
        .set(jnp.arange(block_total, dtype=jnp.int32))
    )
    owner_device = jnp.sum(
        (block_place[:, None] >= first_position[None, 1:]).astype(jnp.int32), axis=1
    )
    flat_slot = owner_device * slot_count + block_place - first_position[owner_device]
    target_device = targets // slot_count
    target_slot = targets % slot_count
    is_live = target_slot < block_count[target_device]
    block_index = block_at_position[
        jnp.clip(first_position[target_device] + target_slot, 0, block_total - 1)
    ]
    neighbour = face_links[block_index]
    source_slot = jnp.where(neighbour >= 0, flat_slot[jnp.clip(neighbour, 0, block_total - 1)], -1)
    column = jnp.arange(width, dtype=jnp.int32)
    flipped = face_flip[block_index][:, :, None]
    ordered = jnp.where(flipped == 1, width - 1 - column, column)
    column_index = (face_offset[block_index][:, :, None] + ordered) % width
    return (is_live, source_slot, column_index)


def attach_halos(blocks, lower, upper, source_slot):
    cells_i = blocks.shape[2]
    lower = jnp.where(
        (source_slot[:, 0] >= 0)[None, :, None, None],
        lower,
        jnp.repeat(blocks[:, :, 0:1], 2, axis=2),
    )
    upper = jnp.where(
        (source_slot[:, 1] >= 0)[None, :, None, None],
        upper,
        jnp.repeat(blocks[:, :, cells_i - 1 : cells_i], 2, axis=2),
    )
    return jnp.concatenate([lower, blocks, upper], axis=2)


def fluxes(conserved):
    inverse_rho = 1.0 / conserved[0]
    velocity_i = conserved[1] * inverse_rho
    velocity_j = conserved[2] * inverse_rho
    pressure = (HEAT_RATIO - 1.0) * (
        conserved[4]
        - 0.5
        * (conserved[1] * conserved[1] + conserved[2] * conserved[2] + conserved[3] * conserved[3])
        * inverse_rho
    )
    flux_i = jnp.stack(
        [
            conserved[1],
            conserved[1] * velocity_i + pressure,
            conserved[2] * velocity_i,
            conserved[3] * velocity_i,
            (conserved[4] + pressure) * velocity_i,
            conserved[5] * velocity_i,
        ]
    )
    flux_j = jnp.stack(
        [
            conserved[2],
            conserved[1] * velocity_j,
            conserved[2] * velocity_j + pressure,
            conserved[3] * velocity_j,
            (conserved[4] + pressure) * velocity_j,
            conserved[5] * velocity_j,
        ]
    )
    return (flux_i, flux_j, jnp.abs(velocity_i), jnp.abs(velocity_j))


def advance(extended, volumes, spectral, omega_value, instance_total):
    cells_i = extended.shape[2] - 4
    flux_i, flux_j, speed_i, speed_j = fluxes(extended)
    left_cell = extended[:, :, 1 : cells_i + 2]
    right_cell = extended[:, :, 2 : cells_i + 3]
    back_cell = extended[:, :, 0 : cells_i + 1]
    ahead_cell = extended[:, :, 3 : cells_i + 4]
    radius_i = 0.5 * (speed_i[:, 1 : cells_i + 2] + speed_i[:, 2 : cells_i + 3]) + SOUND_SPEED
    face_i = 0.5 * (flux_i[:, :, 1 : cells_i + 2] + flux_i[:, :, 2 : cells_i + 3]) - radius_i * (
        SECOND_DISSIPATION * (right_cell - left_cell)
        - FOURTH_DISSIPATION * (ahead_cell - 3.0 * right_cell + 3.0 * left_cell - back_cell)
    )
    centre = extended[:, :, 2 : cells_i + 2]
    centre_flux = flux_j[:, :, 2 : cells_i + 2]
    centre_speed = speed_j[:, 2 : cells_i + 2]
    next_cell = jnp.roll(centre, -1, axis=-1)
    prior_cell = jnp.roll(centre, 1, axis=-1)
    far_cell = jnp.roll(centre, -2, axis=-1)
    radius_j = 0.5 * (centre_speed + jnp.roll(centre_speed, -1, axis=-1)) + SOUND_SPEED
    face_j = 0.5 * (centre_flux + jnp.roll(centre_flux, -1, axis=-1)) - radius_j * (
        SECOND_DISSIPATION * (next_cell - centre)
        - FOURTH_DISSIPATION * (far_cell - 3.0 * next_cell + 3.0 * centre - prior_cell)
    )
    residual_sum = (
        face_i[:, :, 1:]
        - face_i[:, :, :-1]
        + (face_j - jnp.roll(face_j, 1, axis=-1))
        + volumes * spectral
    )
    step_rate = COURANT / (
        speed_i[:, 2 : cells_i + 2]
        + centre_speed
        + 2.0 * SOUND_SPEED
        + volumes * omega_value * 0.5 * instance_total
    )
    return (centre - step_rate * residual_sum, residual_sum / volumes)


def select_faces(selector, slabs):
    return jnp.einsum("tf,lcfxw->lctxw", selector, slabs, precision=lax.Precision.HIGHEST)


def orient_faces(slabs, permuter):
    return jnp.einsum("lctxw,tvw->lctxv", slabs, permuter, precision=lax.Precision.HIGHEST)


def on_device(
    flow_state, cell_volume, frequency, block_count, block_place, face_links, face_offset, face_flip
):
    local_count, comps, row_count, width = flow_state.shape
    slot_count = BLOCKS_MAX
    cells_i = row_count // slot_count
    space_total = lax.axis_size("space")
    space_index = lax.axis_index("space")
    targets = space_index * slot_count + jnp.arange(slot_count, dtype=jnp.int32)
    is_live, source_slot, column_index = block_tables(
        block_count, block_place, face_links, face_offset, face_flip, targets, slot_count, width
    )
    column = jnp.arange(width, dtype=jnp.int32)
    permuter = (
        column_index.reshape(slot_count * 2, width)[:, :, None] == column[None, None, :]
    ).astype(jnp.float32)
    side_index = jnp.arange(2, dtype=jnp.int32)[None, :]
    volumes = cell_volume.reshape(slot_count, cells_i, width)
    instance_total = local_count * lax.axis_size("inst")
    matrix = spectral_matrix(instance_total, frequency[0])
    row_offset = lax.axis_index("inst") * local_count
    own_rows = lax.dynamic_slice_in_dim(matrix, row_offset, local_count, 0)
    wanted_face = (source_slot * 2 + (1 - side_index)).reshape(-1)
    face_range = jnp.arange(space_total * slot_count * 2, dtype=jnp.int32)
    selector = (
        (wanted_face[:, None] == face_range[None, :]) & (source_slot.reshape(-1)[:, None] >= 0)
    ).astype(jnp.float32)
    current = flow_state
    last_residual = jnp.zeros_like(flow_state)
    for iteration in range(PSEUDO_STEPS):
        spectral_all = jnp.einsum(
            "nm,mcrb->ncrb",
            own_rows,
            lax.all_gather(current, "inst", axis=0, tiled=True),
            precision=lax.Precision.HIGHEST,
        )
        blocks = current.reshape(local_count, comps, slot_count, cells_i, width)
        faces = jnp.stack([blocks[:, :, :, 0:2], blocks[:, :, :, cells_i - 2 : cells_i]], axis=3)
        gathered = lax.all_gather(faces, "space", axis=2, tiled=True)
        gathered = gathered.reshape(local_count, comps, space_total * slot_count * 2, 2, width)
        arrived = select_faces(selector, gathered)
        oriented = orient_faces(arrived, permuter).reshape(
            local_count, comps, slot_count, 2, 2, width
        )

        def one_instance(own_blocks, slabs, spectral):
            extended = attach_halos(own_blocks, slabs[:, :, 0], slabs[:, :, 1], source_slot)
            return advance(
                extended,
                volumes,
                spectral.reshape(comps, slot_count, cells_i, width),
                frequency[0],
                instance_total,
            )

        updated, residual_now = jax.vmap(one_instance)(blocks, oriented, spectral_all)
        current = updated.reshape(flow_state.shape)
        last_residual = residual_now.reshape(flow_state.shape)
    row_live = jnp.repeat(is_live, cells_i)[None, None, :, None]
    return (jnp.where(row_live, current, 0.0), jnp.where(row_live, last_residual, 0.0))


def solution(mesh):
    return jax.shard_map(
        four_instances if mesh.shape["inst"] == 4 else on_device,
        mesh=mesh,
        in_specs=(
            P(("groups", "inst"), None, "space", None),
            P(("groups", "space"), None),
            P(),
            P("groups"),
            P("groups"),
            P("groups", None),
            P("groups", None),
            P("groups", None),
        ),
        out_specs=(
            P(("groups", "inst"), None, "space", None),
            P(("groups", "inst"), None, "space", None),
        ),
        check_vma=False,
    )
```

```python
import functools
import math

import jax
import jax.numpy as jnp
from jax import lax
from jax.experimental import pallas as pl
from jax.experimental.pallas import tpu as pltpu
from jax.sharding import PartitionSpec as P

BLOCKS_MAX = 4
PSEUDO_STEPS = 2


HEAT_RATIO = 1.4
SECOND_DISSIPATION = 0.05
FOURTH_DISSIPATION = 0.02
SOUND_SPEED = 1.0
COURANT = 0.5
TIME_VISCOSITY = 0.25

COMPS = 6
FACES = 2 * BLOCKS_MAX
POOLED = COMPS + 1
F32 = jnp.float32
VMEM = pl.BlockSpec(memory_space=pltpu.VMEM)
SMEM = pl.BlockSpec(memory_space=pltpu.SMEM)
HBM = pl.BlockSpec(memory_space=pltpu.HBM)


def spectral_weights(total):
    weights = [TIME_VISCOSITY * (total * total + 2) / 12.0]
    for k in range(1, total):
        sign = 1.0 - 2.0 * (k % 2)
        angle = math.pi * k / total
        first = 0.5 * sign * math.cos(angle) / math.sin(angle)
        second = -sign / (2.0 * math.sin(angle) ** 2)
        weights.append(first - TIME_VISCOSITY * second)
    return weights


def exchanges(total):
    return [2, 3, 1] if total == 4 else list(range(1, total))


def partner(device, k, total):
    return device ^ k if total & (total - 1) == 0 else (device + k) % total


def apart(device, source, total):
    return device ^ source if total & (total - 1) == 0 else (device - source + total) % total


def pair_cap(space_total, block_total):
    second_most = min(BLOCKS_MAX, block_total - BLOCKS_MAX - (space_total - 2))
    return 2 * max(1, second_most)


def primitives(q):
    inverse = 1.0 / q[0]
    u = q[1] * inverse
    v = q[2] * inverse
    p = (HEAT_RATIO - 1.0) * (
        q[4] - 0.5 * (q[1] * q[1] + q[2] * q[2] + q[3] * q[3]) * inverse
    )
    return u, v, p


def flux_along_i(q, u, p, c):
    if c == 0:
        return q[1]
    if c == 1:
        return q[1] * u + p
    return ((q[4] + p) if c == 4 else q[c]) * u


def flux_along_j(q, v, p):
    return [q[2], q[1] * v, q[2] * v + p, q[3] * v, (q[4] + p) * v, q[5] * v]


def ahead(x):
    return pltpu.roll(x, x.shape[1] - 1, axis=1)


def behind(x):
    return pltpu.roll(x, 1, axis=1)


DIFF_ONE = SECOND_DISSIPATION + 2.0 * FOURTH_DISSIPATION


def turn(x, shift):
    return pltpu.roll(x, shift % x.shape[1], axis=1)


def pitchwise_shifts(load, near_ref):
    for c in range(COMPS):
        for r in range(8):
            q = load(c, r)
            near_ref[0, c, r] = turn(q, -1)
            near_ref[1, c, r] = turn(q, -2)
            near_ref[2, c, r] = turn(q, 1)


def pitchwise_faces(q, v, p, near_ref, r):
    after = [near_ref[0, c, r] for c in range(COMPS)]
    _, v_after, p_after = primitives(after)
    radius = 0.5 * (jnp.abs(v) + jnp.abs(v_after)) + SOUND_SPEED
    here, there = flux_along_j(q, v, p), flux_along_j(after, v_after, p_after)
    upper, lower = [], []
    for c in range(COMPS):
        step = after[c] - q[c]
        others = (near_ref[1, c, r] - after[c]) + (q[c] - near_ref[2, c, r])
        damping = radius * (DIFF_ONE * step - FOURTH_DISSIPATION * others)
        upper.append(0.5 * there[c] - damping)
        lower.append(0.5 * here[c] - damping)
    return upper, lower


class Rows:
    def __init__(self, load):
        self.load = load
        self.state, self.prim, self.flux = {}, {}, {}
        self.steps, self.radii, self.faces = {}, {}, {}

    def q(self, r):
        if r not in self.state:
            self.state[r] = self.load(r)
        return self.state[r]

    def uvp(self, r):
        if r not in self.prim:
            self.prim[r] = primitives(self.q(r))
        return self.prim[r]

    def f(self, c, r):
        if (c, r) not in self.flux:
            u, _, p = self.uvp(r)
            self.flux[c, r] = flux_along_i(self.q(r), u, p, c)
        return self.flux[c, r]

    def step(self, c, r):
        if (c, r) not in self.steps:
            self.steps[c, r] = self.q(r + 1)[c] - self.q(r)[c]
        return self.steps[c, r]

    def radius(self, r):
        if r not in self.radii:
            speeds = jnp.abs(self.uvp(r)[0]) + jnp.abs(self.uvp(r + 1)[0])
            self.radii[r] = 0.5 * speeds + SOUND_SPEED
        return self.radii[r]

    def face(self, c, r):
        if (c, r) not in self.faces:
            damping = DIFF_ONE * self.step(c, r) - FOURTH_DISSIPATION * (
                self.step(c, r + 1) + self.step(c, r - 1)
            )
            average = 0.5 * (self.f(c, r) + self.f(c, r + 1))
            self.faces[c, r] = average - self.radius(r) * damping
        return self.faces[c, r]

    def along_one(self, c, r):
        return self.face(c, r) - self.face(c, r - 1)

    def along(self, r):
        return [self.along_one(c, r) for c in range(COMPS)]


def even_tiles(shape):
    return lax.broadcasted_iota(jnp.int32, shape, 0) % 2 == 0


def row_loader(load, halo_ref):
    def extended(r):
        out = []
        for c in range(COMPS):
            if r < 0:
                inner = pltpu.roll(load(c, r + 8), 1, axis=0)
                out.append(jnp.where(even_tiles(inner.shape), halo_ref[c, r + 2], inner))
            elif r > 7:
                inner = pltpu.roll(load(c, r - 8), 7, axis=0)
                out.append(jnp.where(even_tiles(inner.shape), inner, halo_ref[c, r - 8]))
            else:
                out.append(load(c, r))
        return out

    return extended


def rows_from(raw_ref, half_ref, rows_ref):
    for c in range(COMPS):
        for h in range(2):
            half_ref[c, h] = raw_ref[c, :, pl.ds(128 * h, 128)]
    for c in range(COMPS):
        for r in range(8):
            for h in range(2):
                rows_ref[c, r, :, pl.ds(128 * h, 128)] = half_ref[c, h, pl.ds(r, 8, stride=8), :]


def weight_kernel(frequency_ref, weight_ref):
    weights = spectral_weights(4)
    omega = frequency_ref[0]
    even = lax.axis_index("inst") % 2 == 0
    weight_ref[0] = omega
    weight_ref[1] = omega * F32(weights[0])
    weight_ref[2] = omega * F32(weights[2])
    weight_ref[3] = omega * jnp.where(even, F32(weights[3]), F32(weights[1]))
    weight_ref[4] = omega * jnp.where(even, F32(weights[1]), F32(weights[3]))


def coefficients(weight_ref):
    return [weight_ref[k] for k in range(5)]


def own_instance_rate(speeds, volume, omega):
    return COURANT / (speeds + 2.0 * SOUND_SPEED + volume * (omega * (0.5 * 4)))


def pack_kernel(
    space_total, block_total, cap,
    state_ref, volume_ref, counts_in, place_in, links_in, offset_in, flip_in,
    rows_ref, vrows_ref, outer_ref, table_ref, index_ref, *more
):
    sends = more[: space_total - 1]
    half_ref, arrival, first_ref, inverse_ref, *small = more[space_total - 1 :]
    counts_ref, place_ref, links_ref, offset_ref, flip_ref = small
    width = state_ref.shape[2]
    moves = list(zip([counts_in, place_in, links_in, offset_in, flip_in], small))
    for h in range(2):
        lanes = pl.ds(128 * h, 128)
        moves.append((state_ref.at[:, :, lanes], half_ref.at[h, pl.ds(0, COMPS)]))
        moves.append((volume_ref.at[:, lanes], half_ref.at[h, COMPS]))
    copies = [
        pltpu.make_async_copy(source, target, arrival.at[n])
        for n, (source, target) in enumerate(moves)
    ]
    for copy in copies:
        copy.start()
    for copy in copies[: len(small)]:
        copy.wait()
    me = lax.axis_index("space")
    total = jnp.int32(0)
    firsts = []
    for d in range(space_total):
        firsts.append(total)
        first_ref[d] = total
        total = total + counts_ref[d]
    for b in range(block_total):
        inverse_ref[place_ref[b]] = jnp.int32(b)

    def block_in(device, slot):
        return inverse_ref[jnp.minimum(first_ref[device] + slot, block_total - 1)]

    def source_of(block, side):
        link = links_ref[side, block]
        place = place_ref[jnp.maximum(link, 0)]
        owner = jnp.int32(0)
        first = jnp.int32(0)
        for d in range(1, space_total):
            past = place >= firsts[d]
            owner = jnp.where(past, d, owner)
            first = jnp.where(past, firsts[d], first)
        return link, owner, 2 * (place - first) + (1 - side)

    own_base = (space_total - 1) * POOLED * 2 * cap
    few = 2 * counts_ref[me] <= cap
    table_ref[3 * FACES + (space_total - 1) * cap] = counts_ref[me]
    tile = lax.broadcasted_iota(jnp.int32, (FACES, width), 0)
    start = jnp.zeros((FACES, width), jnp.int32)
    turned = jnp.zeros((FACES, width), jnp.int32)
    for f in range(FACES):
        slot, side = f // 2, f % 2
        block = block_in(me, slot)
        link, owner, source = source_of(block, side)
        shift = apart(me, owner, space_total)
        listed = 2 * counts_ref[owner] <= cap
        place = jnp.where(listed, jnp.minimum(source, cap - 1), min(f, cap - 1))
        outside = link < 0
        mine = owner == me
        base = jnp.where(mine, own_base + source, (shift - 1) * (POOLED * 2 * cap) + place)
        base = jnp.where(outside, own_base + 8 * side + f, base)
        table_ref[f] = base
        table_ref[FACES + f] = jnp.where(outside | mine, 2 * FACES, 2 * cap)
        table_ref[2 * FACES + f] = jnp.where(outside, 0, jnp.where(mine, FACES, cap))
        start = jnp.where(tile == f, jnp.where(outside, 0, offset_ref[side, block]), start)
        turned = jnp.where(tile == f, jnp.where(outside, 0, flip_ref[side, block]), turned)
    column = lax.broadcasted_iota(jnp.int32, (FACES, width), 1)
    index_ref[...] = (start + jnp.where(turned == 1, width - 1 - column, column)) % width
    for k in range(1, space_total):
        target = partner(me, k, space_total)
        for i in range(cap):
            _, owner, source = source_of(block_in(target, i // 2), i % 2)
            wanted = jnp.where(owner == me, source, 0)
            table_ref[3 * FACES + (k - 1) * cap + i] = jnp.where(few, i, wanted)
    for copy in copies[len(small) :]:
        copy.wait()
    for c in range(COMPS + 1):
        for r in range(8):
            for h in range(2):
                row = half_ref[h, c, pl.ds(r, 8, stride=8), :]
                if c < COMPS:
                    rows_ref[c, r, :, pl.ds(128 * h, 128)] = row
                else:
                    vrows_ref[r, :, pl.ds(128 * h, 128)] = row
    even = even_tiles((8, width))
    for c in range(COMPS):
        for l in range(2):
            low, high = rows_ref[c, l], rows_ref[c, 6 + l]
            outer_ref[c, l] = jnp.where(even, low, high)
    pack_sends(cap, outer_ref, table_ref, sends)


def pack_sends(cap, outer_ref, table_ref, sends):
    for k, send_ref in enumerate(sends):
        for i in range(cap):
            f = table_ref[3 * FACES + k * cap + i]
            for c in range(outer_ref.shape[0]):
                for l in range(2):
                    send_ref[pl.ds((2 * c + l) * cap + i, 1), :] = outer_ref[c, l, pl.ds(f, 1), :]


def permuted_halos(space_total, cap, table_ref, index_ref, outer_ref, received, pool_ref, raw_ref):
    comps = outer_ref.shape[0]
    for k, part in zip(exchanges(len(received) + 1), received):
        pool_ref[pl.ds((k - 1) * POOLED * 2 * cap, comps * 2 * cap), :] = part[...]
    own_base = (space_total - 1) * POOLED * 2 * cap
    for c in range(comps):
        for l in range(2):
            pool_ref[pl.ds(own_base + (2 * c + l) * FACES, FACES), :] = outer_ref[c, l]
    for f in range(FACES):
        base, per_comp, per_layer = table_ref[f], table_ref[FACES + f], table_ref[2 * FACES + f]
        for c in range(comps):
            for l in range(2):
                row = base + c * per_comp + l * per_layer
                raw_ref[c, l, pl.ds(f, 1), :] = pool_ref[pl.ds(row, 1), :]
    masks, lanes = [], []
    for h in range(2):
        index = index_ref[:, pl.ds(128 * h, 128)]
        lanes.append(index & 127)
        masks.append(index < 128)
    for c in reversed(range(comps)):
        for l in range(2):
            low, high = raw_ref[c, l, :, pl.ds(0, 128)], raw_ref[c, l, :, pl.ds(128, 128)]
            for h in range(2):
                a = jnp.take_along_axis(low, lanes[h], axis=1)
                b = jnp.take_along_axis(high, lanes[h], axis=1)
                yield c, l, h, jnp.where(masks[h], a, b)


def halo_kernel(space_total, cap, table_ref, index_ref, outer_ref, _, __, *more):
    received, (halo_ref, pool_ref, raw_ref) = more[: space_total - 1], more[space_total - 1 :]
    for c, l, h, halo in permuted_halos(
        space_total, cap, table_ref, index_ref, outer_ref, received, pool_ref, raw_ref
    ):
        halo_ref[c, l, :, pl.ds(128 * h, 128)] = halo


def next_halo_kernel(
    space_total, cap, table_ref, index_ref, weight_ref, outer_ref, across_ref, _, *more
):
    received, halos = more[: space_total - 1], more[space_total - 1 : -4]
    halo_ref, pool_ref, raw_ref, far_ref = more[-4:]
    join_halos(halos, far_ref)
    omega, w_own, w_across, w_near, w_far = coefficients(weight_ref)
    gain = {}
    for c, l, h, halo in permuted_halos(
        space_total, cap, table_ref, index_ref, outer_ref, received, pool_ref, raw_ref
    ):
        if c == COMPS:
            gain[l, h] = halo
            continue
        lanes = pl.ds(128 * h, 128)
        lacking = w_across * across_ref[c, l, :, lanes] + w_far * far_ref[c, l, :, lanes]
        halo_ref[c, l, :, lanes] = halo - gain[l, h] * lacking


def pitchwise_kernel(weight_ref, rows_ref, vrows_ref, *more):
    part_ref, rate_ref, near_ref, lower_ref = more[-4:]
    pitchwise(lambda c, r: rows_ref[c, r], vrows_ref, weight_ref[0], part_ref, rate_ref, near_ref, lower_ref)


def sibling_pitchwise_kernel(
    weight_ref, vrows_ref, first_ref, second_ref, rows_ref, part_ref, rate_ref, near_ref, lower_ref
):
    for c in range(COMPS):
        rows_ref[c] = first_ref[c] if c < 3 else second_ref[c - 3]
    load = lambda c, r: rows_ref[c, r]
    pitchwise(load, vrows_ref, weight_ref[0], part_ref, rate_ref, near_ref, lower_ref)


def pitchwise(load, vrows_ref, omega, part_ref, rate_ref, near_ref, lower_ref):
    pitchwise_shifts(load, near_ref)
    for r in range(8):
        q = [load(c, r) for c in range(COMPS)]
        u, v, p = primitives(q)
        upper, lower = pitchwise_faces(q, v, p, near_ref, r)
        rate_ref[r] = own_instance_rate(jnp.abs(u) + jnp.abs(v), vrows_ref[r], omega)
        for c in range(COMPS):
            part_ref[c, r] = upper[c]
            lower_ref[c, r] = lower[c]
    for r in range(8):
        for c in range(COMPS):
            part_ref[c, r] = part_ref[c, r] - turn(lower_ref[c, r], 1)


def outer_kernel(
    cap, table_ref, weight_ref, rows_ref, vrows_ref, part_ref, rate_ref, halo_ref, sibling_ref,
    outer_ref, *sends
):
    omega, w_own, w_across, w_near, w_far = coefficients(weight_ref)
    load = row_loader(lambda c, r: rows_ref[c, r], halo_ref)
    even = even_tiles(vrows_ref.shape[1:])
    low = {r: load(r) for r in range(-2, 4)}
    high = {r: load(r) for r in range(4, 10)}
    picked = {
        k: [jnp.where(even, a, b) for a, b in zip(low[k - 2], high[k + 4])] for k in range(6)
    }
    rows = Rows(lambda k: picked[k])
    for l in range(2):
        along = rows.along(l + 2)
        volume = jnp.where(even, vrows_ref[l], vrows_ref[l + 6])
        rate = jnp.where(even, rate_ref[l], rate_ref[l + 6])
        outer_ref[COMPS, l] = rate * volume
        for c in range(COMPS):
            q = picked[l + 2][c]
            part = jnp.where(even, part_ref[c, l], part_ref[c, l + 6])
            sibling = jnp.where(even, sibling_ref[c, l], sibling_ref[c, l + 6])
            spectral = w_own * q + w_near * sibling
            outer_ref[c, l] = q - rate * (along[c] + part + volume * spectral)
    pack_sends(cap, outer_ref, table_ref, sends)


def near_kernel(
    weight_ref, vrows_ref,
    rows_ref, part_ref, rate_ref, halo_ref,
    sibling_ref, sibling_part_ref, sibling_rate_ref, sibling_halo_ref, _,
    next_ref, sibling_next_ref, gain_ref, sibling_gain_ref
):
    omega, w_own, w_across, w_near, w_far = coefficients(weight_ref)
    for one, other, weight, part, rate_of, halo, out, gain in (
        (rows_ref, sibling_ref, w_near, part_ref, rate_ref, halo_ref, next_ref, gain_ref),
        (sibling_ref, rows_ref, w_far, sibling_part_ref, sibling_rate_ref, sibling_halo_ref,
         sibling_next_ref, sibling_gain_ref),
    ):
        rows = Rows(row_loader(lambda c, r: one[c, r], halo))
        for r in range(8):
            along, volume, rate = rows.along(r), vrows_ref[r], rate_of[r]
            gain[r] = rate * volume
            for c in range(COMPS):
                spectral = w_own * one[c, r] + weight * other[c, r]
                out[c, r] = one[c, r] - rate * (along[c] + part[c, r] + volume * spectral)


def across_kernel(
    weight_ref, vrows_ref, rows_ref, sibling_ref, own_ref, own_gain_ref, sibling_next_ref,
    sibling_gain_ref, raw_ref, halo_ref,
    next_ref, term_ref, across_ref, lacking_ref, gain_ref,
    near_ref, lower_ref, half_ref, part_ref, rate_ref
):
    omega, w_own, w_across, w_near, w_far = coefficients(weight_ref)
    rows_from(raw_ref, half_ref, across_ref)
    load = lambda c, r: across_ref[c, r]
    pitchwise(load, vrows_ref, omega, part_ref, rate_ref, near_ref, lower_ref)
    rows = Rows(row_loader(load, halo_ref))
    for r in range(8):
        along, volume, rate = rows.along(r), vrows_ref[r], rate_ref[r]
        own_gain, sibling_gain, gain = own_gain_ref[r], sibling_gain_ref[r], rate * volume
        gain_ref[r] = (
            (w_own * w_far) * own_gain + (w_near * w_across) * sibling_gain + (w_across * w_near) * gain
        )
        lacking_ref[r] = w_far * own_gain
        for c in range(COMPS):
            q = across_ref[c, r]
            spectral = w_own * q + w_across * rows_ref[c, r] + w_far * sibling_ref[c, r]
            new = q - rate * (along[c] + part_ref[c, r] + volume * spectral)
            mine = own_ref[c, r] - (w_across * own_gain) * q
            sibling = sibling_next_ref[c, r] - (w_near * sibling_gain) * q
            next_ref[c, r] = mine
            term_ref[c, r] = w_own * mine + w_near * sibling + w_across * new


def far_pitchwise_kernel(
    weight_ref, vrows_ref, raw_ref, rows_ref, part_ref, rate_ref, near_ref, lower_ref, half_ref
):
    rows_from(raw_ref, half_ref, rows_ref)
    load = lambda c, r: rows_ref[c, r]
    pitchwise(load, vrows_ref, weight_ref[0], part_ref, rate_ref, near_ref, lower_ref)


def far_kernel(
    weight_ref, vrows_ref, rows_ref, sibling_ref, across_ref, own_ref, partial_ref,
    lacking_ref, lacking_term_ref, far_ref, part_ref, rate_ref, *more
):
    halos, (next_ref, term_ref, halo_ref) = more[:-3], more[-3:]
    omega, w_own, w_across, w_near, w_far = coefficients(weight_ref)
    join_halos(halos, halo_ref)
    rows = Rows(row_loader(lambda c, r: far_ref[c, r], halo_ref))
    for r in range(8):
        along, volume, rate = rows.along(r), vrows_ref[r], rate_ref[r]
        lacking, lacking_term = lacking_ref[r], lacking_term_ref[r]
        for c in range(COMPS):
            q = far_ref[c, r]
            spectral = (
                w_own * q + w_across * sibling_ref[c, r] + w_near * rows_ref[c, r]
                + w_far * across_ref[c, r]
            )
            new = q - rate * (along[c] + part_ref[c, r] + volume * spectral)
            next_ref[c, r] = own_ref[c, r] - lacking * q
            term_ref[c, r] = partial_ref[c, r] - lacking_term * q + w_far * new


def join_halos(parts, halo_ref):
    size = COMPS // len(parts)
    for n, part in enumerate(parts):
        for c in range(size):
            for l in range(2):
                halo_ref[n * size + c, l] = part[c, l]


def last_kernel(
    space_total, cap, table_ref, rows_ref, vrows_ref, halo_ref, part_ref, rate_ref, term_ref,
    new_ref, residual_ref, new_half_ref, residual_half_ref, inverse_ref, left
):
    own = Rows(row_loader(lambda c, r: rows_ref[c, r], halo_ref))
    live_slots = table_ref[3 * FACES + (space_total - 1) * cap]
    live = (lax.broadcasted_iota(jnp.int32, vrows_ref.shape[1:], 0) // 2) < live_slots
    for r in range(8):
        inverse_ref[r] = 1.0 / vrows_ref[r]
    copies = []
    for c in range(COMPS):
        for r in range(8):
            residual = part_ref[c, r] + own.along_one(c, r) + vrows_ref[r] * term_ref[c, r]
            new = jnp.where(live, own.q(r)[c] - rate_ref[r] * residual, 0.0)
            scaled = jnp.where(live, residual * inverse_ref[r], 0.0)
            for h in range(2):
                lanes = slice(128 * h, 128 * h + 128)
                new_half_ref[c, h, pl.ds(r, 8, stride=8), :] = new[:, lanes]
                residual_half_ref[c, h, pl.ds(r, 8, stride=8), :] = scaled[:, lanes]
        for n, (half_ref, out_ref) in enumerate(
            [(new_half_ref, new_ref), (residual_half_ref, residual_ref)]
        ):
            for h in range(2):
                copy = pltpu.make_async_copy(
                    half_ref.at[c, h], out_ref.at[c, :, pl.ds(128 * h, 128)], left.at[len(copies)]
                )
                copy.start()
                copies.append(copy)
    for copy in copies:
        copy.wait()


def after_kernel(value_ref, *more):
    pass


def four_instances(
    flow_state, cell_volume, frequency, block_count, block_place, face_links, face_offset, face_flip
):
    _, comps, row_count, width = flow_state.shape
    space_total = lax.axis_size("space")
    block_total = block_place.shape[0]
    cap = pair_cap(space_total, block_total)
    state = flow_state[0]

    def over_inst(x, flip):
        return lax.ppermute(x, "inst", [(i, i ^ flip) for i in range(4)])

    def over_space(parts):
        arrived = {
            k: lax.ppermute(
                parts[k - 1], "space", [(i, partner(i, k, space_total)) for i in range(space_total)]
            )
            for k in exchanges(space_total)
        }
        return [arrived[k] for k in exchanges(space_total)]

    full = (comps, 8, 8, width)
    outer = (comps, 2, 8, width)
    plane = (8, 8, width)
    pooled = (POOLED, 2, 8, width)
    entries = 3 * FACES + (space_total - 1) * cap + 1
    on_chip = lambda shape, dtype=F32: pltpu.VMEM(shape, dtype)
    sends_shape = lambda n: [on_chip((n * 2 * cap, width)) for _ in range(space_total - 1)]
    shifts = [pltpu.VMEM((3,) + full, F32), pltpu.VMEM(full, F32)]

    def call(kernel, out, specs, args, scratch=(), micros=0.3, out_specs=None, aliases={}):
        args = [
            pltpu.with_memory_space_constraint(x, spec.memory_space) for spec, x in zip(specs, args)
        ]
        return pl.pallas_call(
            kernel,
            out_shape=out,
            in_specs=specs,
            out_specs=out_specs or jax.tree.map(lambda _: VMEM, out),
            scratch_shapes=list(scratch),
            input_output_aliases=aliases,
            compiler_params=pltpu.CompilerParams(vmem_limit_bytes=12 << 20),
            cost_estimate=pl.CostEstimate(
                flops=0, bytes_accessed=int(micros * 3.69e6), transcendentals=0
            ),
        )(*args)

    packed = call(
        functools.partial(pack_kernel, space_total, block_total, cap),
        [
            on_chip(full), on_chip(plane), on_chip(outer),
            pltpu.SMEM((entries,), jnp.int32),
            on_chip((FACES, width), jnp.int32), *sends_shape(comps),
        ],
        [HBM] * 7,
        (state, cell_volume, block_count, block_place, face_links.T, face_offset.T, face_flip.T),
        scratch=[
            pltpu.VMEM((2, comps + 1, row_count, 128), F32),
            pltpu.SemaphoreType.DMA((9,)),
            pltpu.SMEM((space_total,), jnp.int32),
            pltpu.SMEM((block_total,), jnp.int32),
            pltpu.SMEM((space_total,), jnp.int32),
            pltpu.SMEM((block_total,), jnp.int32),
            *[pltpu.SMEM((2, block_total), jnp.int32)] * 3,
        ],
        micros=2.0,
        out_specs=[VMEM] * 3 + [SMEM] + [VMEM] * space_total,
    )
    rows, vrows, outer_rows, table, index = packed[:5]
    sends = packed[5:]
    weights = pl.pallas_call(
        weight_kernel, out_shape=pltpu.SMEM((8,), F32), in_specs=[SMEM], out_specs=SMEM
    )(frequency)
    halves = [pltpu.VMEM((comps, 2, row_count, 128), F32), pltpu.VMEM(full, F32)]
    pool = [
        pltpu.VMEM(((space_total - 1) * POOLED * 2 * cap + POOLED * 2 * FACES, width), F32),
        pltpu.VMEM(pooled, F32),
    ]

    def pitch(x, *first):
        return call(
            pitchwise_kernel,
            [on_chip(full), on_chip(plane)],
            [SMEM] + [VMEM] * (2 + len(first)),
            (weights, x, vrows, *first),
            scratch=shifts,
            micros=0.5,
        )

    across = over_inst(state, 2)
    sibling_halves = [over_inst(rows[n * 3 : n * 3 + 3], 1) for n in range(2)]
    received = over_space(sends)
    part, rate = pitch(rows)
    sibling, sibling_part, sibling_rate = call(
        sibling_pitchwise_kernel,
        [on_chip(full)] * 2 + [on_chip(plane)],
        [SMEM] + [VMEM] * 3,
        (weights, vrows, *sibling_halves),
        scratch=shifts,
        micros=0.5,
    )
    halo = call(
        functools.partial(halo_kernel, space_total, cap),
        on_chip(outer),
        [SMEM] + [VMEM] * (3 + space_total),
        (table, index, outer_rows, rate, sibling_rate, *received),
        scratch=pool,
    )
    across_halo = over_inst(halo, 2)
    sibling_halo = over_inst(halo, 1)
    next_outer, *next_sends = call(
        functools.partial(outer_kernel, cap),
        [on_chip(pooled), *sends_shape(POOLED)],
        [SMEM, SMEM] + [VMEM] * 6,
        (table, weights, rows, vrows, part, rate, halo, sibling),
        micros=0.3,
    )
    next_received = over_space(next_sends)
    def after(x, *first):
        return call(
            after_kernel, on_chip(x.shape), [VMEM] * (1 + len(first)), (x, *first), aliases={0: 0}, micros=0.05
        )

    far = over_inst(after(across, next_outer), 1)
    pieces = 2
    size = comps // pieces
    hx = across_halo
    far_halo = [over_inst(hx[n * size : n * size + size], 1) for n in range(pieces)]
    far_rows, far_part, far_rate = call(
        far_pitchwise_kernel,
        [on_chip(full)] * 2 + [on_chip(plane)],
        [SMEM] + [VMEM] * 2,
        (weights, vrows, far),
        scratch=shifts + halves[:1],
        micros=0.6,
    )
    own, sibling_next, own_gain, sibling_gain = call(
        near_kernel,
        [on_chip(full)] * 2 + [on_chip(plane)] * 2,
        [SMEM] + [VMEM] * 10,
        (weights, vrows, rows, part, rate, halo, sibling, sibling_part, sibling_rate, sibling_halo,
         far_rate),
        micros=0.7,
    )
    own, partial, across_rows, lacking, lacking_term = call(
        across_kernel,
        [on_chip(full)] * 3 + [on_chip(plane)] * 2,
        [SMEM] + [VMEM] * 9,
        (weights, vrows, rows, sibling, own, own_gain, sibling_next, sibling_gain, across, across_halo),
        scratch=shifts + halves[:1] + [halves[1], pltpu.VMEM(plane, F32)],
        micros=1.0,
    )
    next_rows, term = call(
        far_kernel,
        [on_chip(full)] * 2,
        [SMEM] + [VMEM] * (11 + len(far_halo)),
        (weights, vrows, rows, sibling, across_rows, own, partial, lacking, lacking_term,
         far_rows, far_part, far_rate, *far_halo),
        scratch=[pltpu.VMEM(outer, F32)],
        micros=0.5,
    )
    next_part, next_rate = pitch(next_rows)
    next_halo = call(
        functools.partial(next_halo_kernel, space_total, cap),
        on_chip(outer),
        [SMEM, VMEM, SMEM] + [VMEM] * (2 + space_total + len(far_halo)),
        (table, index, weights, next_outer, across_halo, next_rate, *next_received, *far_halo),
        scratch=pool + [pltpu.VMEM(outer, F32)],
    )
    new, residual = call(
        functools.partial(last_kernel, space_total, cap),
        [jax.ShapeDtypeStruct(state.shape, F32)] * 2,
        [SMEM] + [VMEM] * 6,
        (table, next_rows, vrows, next_halo, next_part, next_rate, term),
        scratch=[pltpu.VMEM((comps, 2, row_count, 128), F32)] * 2
        + [pltpu.VMEM(plane, F32), pltpu.SemaphoreType.DMA((4 * comps,))],
        micros=1.5,
        out_specs=[HBM] * 2,
    )
    return new[None], residual[None]


def spectral_matrix(instance_total, omega_value):
    position = jnp.arange(instance_total, dtype=jnp.int32)
    distance = (position[:, None] - position[None, :]) % instance_total
    parity = (1 - 2 * (distance % 2)).astype(jnp.float32)
    phase_angle = jnp.pi * distance.astype(jnp.float32) / instance_total
    safe_angle = jnp.where(distance == 0, 0.5 * jnp.pi, phase_angle)
    first_derivative = jnp.where(
        distance == 0, 0.0, 0.5 * parity * jnp.cos(safe_angle) / jnp.sin(safe_angle)
    )
    second_derivative = jnp.where(
        distance == 0,
        -(instance_total * instance_total + 2) / 12.0,
        -parity / (2.0 * jnp.sin(safe_angle) ** 2),
    )
    return omega_value * (first_derivative - TIME_VISCOSITY * second_derivative)


def block_tables(
    block_count, block_place, face_links, face_offset, face_flip, targets, slot_count, width
):
    block_total = block_place.shape[0]
    first_position = jnp.cumsum(block_count) - block_count
    block_at_position = (
        jnp.zeros((block_total,), jnp.int32)
        .at[block_place]
        .set(jnp.arange(block_total, dtype=jnp.int32))
    )
    owner_device = jnp.sum(
        (block_place[:, None] >= first_position[None, 1:]).astype(jnp.int32), axis=1
    )
    flat_slot = owner_device * slot_count + block_place - first_position[owner_device]
    target_device = targets // slot_count
    target_slot = targets % slot_count
    is_live = target_slot < block_count[target_device]
    block_index = block_at_position[
        jnp.clip(first_position[target_device] + target_slot, 0, block_total - 1)
    ]
    neighbour = face_links[block_index]
    source_slot = jnp.where(neighbour >= 0, flat_slot[jnp.clip(neighbour, 0, block_total - 1)], -1)
    column = jnp.arange(width, dtype=jnp.int32)
    flipped = face_flip[block_index][:, :, None]
    ordered = jnp.where(flipped == 1, width - 1 - column, column)
    column_index = (face_offset[block_index][:, :, None] + ordered) % width
    return (is_live, source_slot, column_index)


def attach_halos(blocks, lower, upper, source_slot):
    cells_i = blocks.shape[2]
    lower = jnp.where(
        (source_slot[:, 0] >= 0)[None, :, None, None],
        lower,
        jnp.repeat(blocks[:, :, 0:1], 2, axis=2),
    )
    upper = jnp.where(
        (source_slot[:, 1] >= 0)[None, :, None, None],
        upper,
        jnp.repeat(blocks[:, :, cells_i - 1 : cells_i], 2, axis=2),
    )
    return jnp.concatenate([lower, blocks, upper], axis=2)


def fluxes(conserved):
    inverse_rho = 1.0 / conserved[0]
    velocity_i = conserved[1] * inverse_rho
    velocity_j = conserved[2] * inverse_rho
    pressure = (HEAT_RATIO - 1.0) * (
        conserved[4]
        - 0.5
        * (conserved[1] * conserved[1] + conserved[2] * conserved[2] + conserved[3] * conserved[3])
        * inverse_rho
    )
    flux_i = jnp.stack(
        [
            conserved[1],
            conserved[1] * velocity_i + pressure,
            conserved[2] * velocity_i,
            conserved[3] * velocity_i,
            (conserved[4] + pressure) * velocity_i,
            conserved[5] * velocity_i,
        ]
    )
    flux_j = jnp.stack(
        [
            conserved[2],
            conserved[1] * velocity_j,
            conserved[2] * velocity_j + pressure,
            conserved[3] * velocity_j,
            (conserved[4] + pressure) * velocity_j,
            conserved[5] * velocity_j,
        ]
    )
    return (flux_i, flux_j, jnp.abs(velocity_i), jnp.abs(velocity_j))


def advance(extended, volumes, spectral, omega_value, instance_total):
    cells_i = extended.shape[2] - 4
    flux_i, flux_j, speed_i, speed_j = fluxes(extended)
    left_cell = extended[:, :, 1 : cells_i + 2]
    right_cell = extended[:, :, 2 : cells_i + 3]
    back_cell = extended[:, :, 0 : cells_i + 1]
    ahead_cell = extended[:, :, 3 : cells_i + 4]
    radius_i = 0.5 * (speed_i[:, 1 : cells_i + 2] + speed_i[:, 2 : cells_i + 3]) + SOUND_SPEED
    face_i = 0.5 * (flux_i[:, :, 1 : cells_i + 2] + flux_i[:, :, 2 : cells_i + 3]) - radius_i * (
        SECOND_DISSIPATION * (right_cell - left_cell)
        - FOURTH_DISSIPATION * (ahead_cell - 3.0 * right_cell + 3.0 * left_cell - back_cell)
    )
    centre = extended[:, :, 2 : cells_i + 2]
    centre_flux = flux_j[:, :, 2 : cells_i + 2]
    centre_speed = speed_j[:, 2 : cells_i + 2]
    next_cell = jnp.roll(centre, -1, axis=-1)
    prior_cell = jnp.roll(centre, 1, axis=-1)
    far_cell = jnp.roll(centre, -2, axis=-1)
    radius_j = 0.5 * (centre_speed + jnp.roll(centre_speed, -1, axis=-1)) + SOUND_SPEED
    face_j = 0.5 * (centre_flux + jnp.roll(centre_flux, -1, axis=-1)) - radius_j * (
        SECOND_DISSIPATION * (next_cell - centre)
        - FOURTH_DISSIPATION * (far_cell - 3.0 * next_cell + 3.0 * centre - prior_cell)
    )
    residual_sum = (
        face_i[:, :, 1:]
        - face_i[:, :, :-1]
        + (face_j - jnp.roll(face_j, 1, axis=-1))
        + volumes * spectral
    )
    step_rate = COURANT / (
        speed_i[:, 2 : cells_i + 2]
        + centre_speed
        + 2.0 * SOUND_SPEED
        + volumes * omega_value * 0.5 * instance_total
    )
    return (centre - step_rate * residual_sum, residual_sum / volumes)


def select_faces(selector, slabs):
    return jnp.einsum("tf,lcfxw->lctxw", selector, slabs, precision=lax.Precision.HIGHEST)


def orient_faces(slabs, permuter):
    return jnp.einsum("lctxw,tvw->lctxv", slabs, permuter, precision=lax.Precision.HIGHEST)


def on_device(
    flow_state, cell_volume, frequency, block_count, block_place, face_links, face_offset, face_flip
):
    local_count, comps, row_count, width = flow_state.shape
    slot_count = BLOCKS_MAX
    cells_i = row_count // slot_count
    space_total = lax.axis_size("space")
    space_index = lax.axis_index("space")
    targets = space_index * slot_count + jnp.arange(slot_count, dtype=jnp.int32)
    is_live, source_slot, column_index = block_tables(
        block_count, block_place, face_links, face_offset, face_flip, targets, slot_count, width
    )
    column = jnp.arange(width, dtype=jnp.int32)
    permuter = (
        column_index.reshape(slot_count * 2, width)[:, :, None] == column[None, None, :]
    ).astype(jnp.float32)
    side_index = jnp.arange(2, dtype=jnp.int32)[None, :]
    volumes = cell_volume.reshape(slot_count, cells_i, width)
    instance_total = local_count * lax.axis_size("inst")
    matrix = spectral_matrix(instance_total, frequency[0])
    row_offset = lax.axis_index("inst") * local_count
    own_rows = lax.dynamic_slice_in_dim(matrix, row_offset, local_count, 0)
    wanted_face = (source_slot * 2 + (1 - side_index)).reshape(-1)
    face_range = jnp.arange(space_total * slot_count * 2, dtype=jnp.int32)
    selector = (
        (wanted_face[:, None] == face_range[None, :]) & (source_slot.reshape(-1)[:, None] >= 0)
    ).astype(jnp.float32)
    current = flow_state
    last_residual = jnp.zeros_like(flow_state)
    for iteration in range(PSEUDO_STEPS):
        spectral_all = jnp.einsum(
            "nm,mcrb->ncrb",
            own_rows,
            lax.all_gather(current, "inst", axis=0, tiled=True),
            precision=lax.Precision.HIGHEST,
        )
        blocks = current.reshape(local_count, comps, slot_count, cells_i, width)
        faces = jnp.stack([blocks[:, :, :, 0:2], blocks[:, :, :, cells_i - 2 : cells_i]], axis=3)
        gathered = lax.all_gather(faces, "space", axis=2, tiled=True)
        gathered = gathered.reshape(local_count, comps, space_total * slot_count * 2, 2, width)
        arrived = select_faces(selector, gathered)
        oriented = orient_faces(arrived, permuter).reshape(
            local_count, comps, slot_count, 2, 2, width
        )

        def one_instance(own_blocks, slabs, spectral):
            extended = attach_halos(own_blocks, slabs[:, :, 0], slabs[:, :, 1], source_slot)
            return advance(
                extended,
                volumes,
                spectral.reshape(comps, slot_count, cells_i, width),
                frequency[0],
                instance_total,
            )

        updated, residual_now = jax.vmap(one_instance)(blocks, oriented, spectral_all)
        current = updated.reshape(flow_state.shape)
        last_residual = residual_now.reshape(flow_state.shape)
    row_live = jnp.repeat(is_live, cells_i)[None, None, :, None]
    return (jnp.where(row_live, current, 0.0), jnp.where(row_live, last_residual, 0.0))


def solution(mesh):
    return jax.shard_map(
        four_instances if mesh.shape["inst"] == 4 else on_device,
        mesh=mesh,
        in_specs=(
            P(("groups", "inst"), None, "space", None),
            P(("groups", "space"), None),
            P(),
            P("groups"),
            P("groups"),
            P("groups", None),
            P("groups", None),
            P("groups", None),
        ),
        out_specs=(
            P(("groups", "inst"), None, "space", None),
            P(("groups", "inst"), None, "space", None),
        ),
        check_vma=False,
    )
```

```python
import functools
import math

import jax
import jax.numpy as jnp
from jax import lax
from jax.experimental import pallas as pl
from jax.experimental.pallas import tpu as pltpu
from jax.sharding import PartitionSpec as P

BLOCKS_MAX = 4
PSEUDO_STEPS = 2


HEAT_RATIO = 1.4
SECOND_DISSIPATION = 0.05
FOURTH_DISSIPATION = 0.02
SOUND_SPEED = 1.0
COURANT = 0.5
TIME_VISCOSITY = 0.25

COMPS = 6
FACES = 2 * BLOCKS_MAX
POOLED = COMPS + 1
F32 = jnp.float32
VMEM = pl.BlockSpec(memory_space=pltpu.VMEM)
SMEM = pl.BlockSpec(memory_space=pltpu.SMEM)
HBM = pl.BlockSpec(memory_space=pltpu.HBM)


def spectral_weights(total):
    weights = [TIME_VISCOSITY * (total * total + 2) / 12.0]
    for k in range(1, total):
        sign = 1.0 - 2.0 * (k % 2)
        angle = math.pi * k / total
        first = 0.5 * sign * math.cos(angle) / math.sin(angle)
        second = -sign / (2.0 * math.sin(angle) ** 2)
        weights.append(first - TIME_VISCOSITY * second)
    return weights


def exchanges(total):
    return [2, 3, 1] if total == 4 else list(range(1, total))


def partner(device, k, total):
    return device ^ k if total & (total - 1) == 0 else (device + k) % total


def apart(device, source, total):
    return device ^ source if total & (total - 1) == 0 else (device - source + total) % total


def pair_cap(space_total, block_total):
    second_most = min(BLOCKS_MAX, block_total - BLOCKS_MAX - (space_total - 2))
    return 2 * max(1, second_most)


def primitives(q):
    inverse = 1.0 / q[0]
    u = q[1] * inverse
    v = q[2] * inverse
    p = (HEAT_RATIO - 1.0) * (
        q[4] - 0.5 * (q[1] * q[1] + q[2] * q[2] + q[3] * q[3]) * inverse
    )
    return u, v, p


def flux_along_i(q, u, p, c):
    if c == 0:
        return q[1]
    if c == 1:
        return q[1] * u + p
    return ((q[4] + p) if c == 4 else q[c]) * u


def flux_along_j(q, v, p):
    return [q[2], q[1] * v, q[2] * v + p, q[3] * v, (q[4] + p) * v, q[5] * v]


def ahead(x):
    return pltpu.roll(x, x.shape[1] - 1, axis=1)


def behind(x):
    return pltpu.roll(x, 1, axis=1)


DIFF_ONE = SECOND_DISSIPATION + 2.0 * FOURTH_DISSIPATION


def turn(x, shift):
    return pltpu.roll(x, shift % x.shape[1], axis=1)


def pitchwise_shifts(load, near_ref):
    for c in range(COMPS):
        for r in range(8):
            q = load(c, r)
            near_ref[0, c, r] = turn(q, -1)
            near_ref[1, c, r] = turn(q, -2)
            near_ref[2, c, r] = turn(q, 1)


def pitchwise_faces(q, v, p, near_ref, r):
    after = [near_ref[0, c, r] for c in range(COMPS)]
    _, v_after, p_after = primitives(after)
    radius = 0.5 * (jnp.abs(v) + jnp.abs(v_after)) + SOUND_SPEED
    here, there = flux_along_j(q, v, p), flux_along_j(after, v_after, p_after)
    upper, lower = [], []
    for c in range(COMPS):
        step = after[c] - q[c]
        others = (near_ref[1, c, r] - after[c]) + (q[c] - near_ref[2, c, r])
        damping = radius * (DIFF_ONE * step - FOURTH_DISSIPATION * others)
        upper.append(0.5 * there[c] - damping)
        lower.append(0.5 * here[c] - damping)
    return upper, lower


class Rows:
    def __init__(self, load):
        self.load = load
        self.state, self.prim, self.flux = {}, {}, {}
        self.steps, self.radii, self.faces = {}, {}, {}

    def q(self, r):
        if r not in self.state:
            self.state[r] = self.load(r)
        return self.state[r]

    def uvp(self, r):
        if r not in self.prim:
            self.prim[r] = primitives(self.q(r))
        return self.prim[r]

    def f(self, c, r):
        if (c, r) not in self.flux:
            u, _, p = self.uvp(r)
            self.flux[c, r] = flux_along_i(self.q(r), u, p, c)
        return self.flux[c, r]

    def step(self, c, r):
        if (c, r) not in self.steps:
            self.steps[c, r] = self.q(r + 1)[c] - self.q(r)[c]
        return self.steps[c, r]

    def radius(self, r):
        if r not in self.radii:
            speeds = jnp.abs(self.uvp(r)[0]) + jnp.abs(self.uvp(r + 1)[0])
            self.radii[r] = 0.5 * speeds + SOUND_SPEED
        return self.radii[r]

    def face(self, c, r):
        if (c, r) not in self.faces:
            damping = DIFF_ONE * self.step(c, r) - FOURTH_DISSIPATION * (
                self.step(c, r + 1) + self.step(c, r - 1)
            )
            average = 0.5 * (self.f(c, r) + self.f(c, r + 1))
            self.faces[c, r] = average - self.radius(r) * damping
        return self.faces[c, r]

    def along_one(self, c, r):
        return self.face(c, r) - self.face(c, r - 1)

    def along(self, r):
        return [self.along_one(c, r) for c in range(COMPS)]


def even_tiles(shape):
    return lax.broadcasted_iota(jnp.int32, shape, 0) % 2 == 0


def row_loader(load, halo_ref):
    def extended(r):
        out = []
        for c in range(COMPS):
            if r < 0:
                inner = pltpu.roll(load(c, r + 8), 1, axis=0)
                out.append(jnp.where(even_tiles(inner.shape), halo_ref[c, r + 2], inner))
            elif r > 7:
                inner = pltpu.roll(load(c, r - 8), 7, axis=0)
                out.append(jnp.where(even_tiles(inner.shape), inner, halo_ref[c, r - 8]))
            else:
                out.append(load(c, r))
        return out

    return extended


def rows_from(raw_ref, half_ref, rows_ref):
    for c in range(COMPS):
        for h in range(2):
            half_ref[c, h] = raw_ref[c, :, pl.ds(128 * h, 128)]
    for c in range(COMPS):
        for r in range(8):
            for h in range(2):
                rows_ref[c, r, :, pl.ds(128 * h, 128)] = half_ref[c, h, pl.ds(r, 8, stride=8), :]


def weight_kernel(frequency_ref, weight_ref):
    weights = spectral_weights(4)
    omega = frequency_ref[0]
    even = lax.axis_index("inst") % 2 == 0
    weight_ref[0] = omega
    weight_ref[1] = omega * F32(weights[0])
    weight_ref[2] = omega * F32(weights[2])
    weight_ref[3] = omega * jnp.where(even, F32(weights[3]), F32(weights[1]))
    weight_ref[4] = omega * jnp.where(even, F32(weights[1]), F32(weights[3]))


def coefficients(weight_ref):
    return [weight_ref[k] for k in range(5)]


def own_instance_rate(speeds, volume, omega):
    return COURANT / (speeds + 2.0 * SOUND_SPEED + volume * (omega * (0.5 * 4)))


def get_tables(space_total, block_total, sources, targets, arrival, more=()):
    moves = list(zip(sources, targets)) + list(more)
    copies = [
        pltpu.make_async_copy(source, target, arrival.at[n])
        for n, (source, target) in enumerate(moves)
    ]
    for copy in copies:
        copy.start()
    for copy in copies[: len(sources)]:
        copy.wait()
    counts_ref, place_ref, links_ref, first_ref, inverse_ref = targets[:3] + targets[-2:]
    total = jnp.int32(0)
    firsts = []
    for d in range(space_total):
        firsts.append(total)
        first_ref[d] = total
        total = total + counts_ref[d]
    for b in range(block_total):
        inverse_ref[place_ref[b]] = jnp.int32(b)

    def block_in(device, slot):
        return inverse_ref[jnp.minimum(first_ref[device] + slot, block_total - 1)]

    def source_of(block, side):
        link = links_ref[side, block]
        place = place_ref[jnp.maximum(link, 0)]
        owner = jnp.int32(0)
        first = jnp.int32(0)
        for d in range(1, space_total):
            past = place >= firsts[d]
            owner = jnp.where(past, d, owner)
            first = jnp.where(past, firsts[d], first)
        return link, owner, 2 * (place - first) + (1 - side)

    return block_in, source_of, copies[len(sources) :]


def pack_kernel(
    space_total, block_total, cap,
    state_ref, volume_ref, counts_in, place_in, links_in,
    half_ref, volume_half_ref, outer_ref, table_ref, *more
):
    sends = more[: space_total - 1]
    arrival, *small = more[space_total - 1 :]
    moves = []
    for c in range(COMPS + 1):
        for h in range(2):
            lanes = pl.ds(128 * h, 128)
            if c < COMPS:
                moves.append((state_ref.at[c, :, lanes], half_ref.at[h, c]))
            else:
                moves.append((volume_ref.at[:, lanes], volume_half_ref.at[h]))
    block_in, source_of, copies = get_tables(
        space_total, block_total, (counts_in, place_in, links_in), small, arrival, moves
    )
    me = lax.axis_index("space")
    few = 2 * small[0][me] <= cap
    for k in range(1, space_total):
        target = partner(me, k, space_total)
        for i in range(cap):
            _, owner, source = source_of(block_in(target, i // 2), i % 2)
            wanted = jnp.where(owner == me, source, 0)
            table_ref[(k - 1) * cap + i] = jnp.where(few, i, wanted)
    even = even_tiles((8, 128))
    for c in range(COMPS):
        copies[2 * c].wait()
        copies[2 * c + 1].wait()
        for l in range(2):
            for h in range(2):
                low = half_ref[h, c, pl.ds(l, 8, stride=8), :]
                high = half_ref[h, c, pl.ds(6 + l, 8, stride=8), :]
                outer_ref[c, l, :, pl.ds(128 * h, 128)] = jnp.where(even, low, high)
        pack_sends(cap, outer_ref, table_ref, sends, (c,))
    for copy in copies[2 * COMPS :]:
        copy.wait()


def rows_kernel(
    space_total, block_total, cap,
    half_ref, volume_half_ref, counts_in, place_in, links_in, offset_in, flip_in,
    rows_ref, vrows_ref, table_ref, index_ref, arrival, *small
):
    block_in, source_of, _ = get_tables(
        space_total, block_total, (counts_in, place_in, links_in, offset_in, flip_in), small, arrival
    )
    counts_ref, _, _, offset_ref, flip_ref = small[:5]
    width = index_ref.shape[1]
    for h in range(2):
        for r in range(8):
            rows = pl.ds(r, 8, stride=8)
            lanes = pl.ds(128 * h, 128)
            vrows_ref[r, :, lanes] = volume_half_ref[h, rows, :]
            for c in range(COMPS):
                rows_ref[c, r, :, lanes] = half_ref[h, c, rows, :]
    me = lax.axis_index("space")
    own_base = (space_total - 1) * POOLED * 2 * cap
    table_ref[3 * FACES] = counts_ref[me]
    tile = lax.broadcasted_iota(jnp.int32, (FACES, width), 0)
    start = jnp.zeros((FACES, width), jnp.int32)
    turned = jnp.zeros((FACES, width), jnp.int32)
    for f in range(FACES):
        slot, side = f // 2, f % 2
        block = block_in(me, slot)
        link, owner, source = source_of(block, side)
        shift = apart(me, owner, space_total)
        listed = 2 * counts_ref[owner] <= cap
        place = jnp.where(listed, jnp.minimum(source, cap - 1), min(f, cap - 1))
        outside = link < 0
        mine = owner == me
        base = jnp.where(mine, own_base + source, (shift - 1) * (POOLED * 2 * cap) + place)
        base = jnp.where(outside, own_base + 8 * side + f, base)
        table_ref[f] = base
        table_ref[FACES + f] = jnp.where(outside | mine, 2 * FACES, 2 * cap)
        table_ref[2 * FACES + f] = jnp.where(outside, 0, jnp.where(mine, FACES, cap))
        start = jnp.where(tile == f, jnp.where(outside, 0, offset_ref[side, block]), start)
        turned = jnp.where(tile == f, jnp.where(outside, 0, flip_ref[side, block]), turned)
    column = lax.broadcasted_iota(jnp.int32, (FACES, width), 1)
    index_ref[...] = (start + jnp.where(turned == 1, width - 1 - column, column)) % width


def pack_sends(cap, outer_ref, table_ref, sends, comps):
    for k, send_ref in enumerate(sends):
        for i in range(cap):
            f = table_ref[k * cap + i]
            for c in comps:
                for l in range(2):
                    send_ref[pl.ds((2 * c + l) * cap + i, 1), :] = outer_ref[c, l, pl.ds(f, 1), :]


def permuted_halos(space_total, cap, table_ref, index_ref, outer_ref, received, pool_ref, raw_ref):
    comps = outer_ref.shape[0]
    for k, part in zip(exchanges(len(received) + 1), received):
        pool_ref[pl.ds((k - 1) * POOLED * 2 * cap, comps * 2 * cap), :] = part[...]
    own_base = (space_total - 1) * POOLED * 2 * cap
    for c in range(comps):
        for l in range(2):
            pool_ref[pl.ds(own_base + (2 * c + l) * FACES, FACES), :] = outer_ref[c, l]
    for f in range(FACES):
        base, per_comp, per_layer = table_ref[f], table_ref[FACES + f], table_ref[2 * FACES + f]
        for c in range(comps):
            for l in range(2):
                row = base + c * per_comp + l * per_layer
                raw_ref[c, l, pl.ds(f, 1), :] = pool_ref[pl.ds(row, 1), :]
    masks, lanes = [], []
    for h in range(2):
        index = index_ref[:, pl.ds(128 * h, 128)]
        lanes.append(index & 127)
        masks.append(index < 128)
    for c in reversed(range(comps)):
        for l in range(2):
            low, high = raw_ref[c, l, :, pl.ds(0, 128)], raw_ref[c, l, :, pl.ds(128, 128)]
            for h in range(2):
                a = jnp.take_along_axis(low, lanes[h], axis=1)
                b = jnp.take_along_axis(high, lanes[h], axis=1)
                yield c, l, h, jnp.where(masks[h], a, b)


def halo_kernel(space_total, cap, table_ref, index_ref, outer_ref, _, __, *more):
    received, (halo_ref, pool_ref, raw_ref) = more[: space_total - 1], more[space_total - 1 :]
    for c, l, h, halo in permuted_halos(
        space_total, cap, table_ref, index_ref, outer_ref, received, pool_ref, raw_ref
    ):
        halo_ref[c, l, :, pl.ds(128 * h, 128)] = halo


def next_halo_kernel(
    space_total, cap, table_ref, index_ref, weight_ref, outer_ref, across_ref, _, *more
):
    received, halos = more[: space_total - 1], more[space_total - 1 : -4]
    halo_ref, pool_ref, raw_ref, far_ref = more[-4:]
    join_halos(halos, far_ref)
    omega, w_own, w_across, w_near, w_far = coefficients(weight_ref)
    gain = {}
    for c, l, h, halo in permuted_halos(
        space_total, cap, table_ref, index_ref, outer_ref, received, pool_ref, raw_ref
    ):
        if c == COMPS:
            gain[l, h] = halo
            continue
        lanes = pl.ds(128 * h, 128)
        lacking = w_across * across_ref[c, l, :, lanes] + w_far * far_ref[c, l, :, lanes]
        halo_ref[c, l, :, lanes] = halo - gain[l, h] * lacking


def pitchwise_kernel(weight_ref, rows_ref, vrows_ref, *more):
    part_ref, rate_ref, near_ref, lower_ref = more[-4:]
    pitchwise(lambda c, r: rows_ref[c, r], vrows_ref, weight_ref[0], part_ref, rate_ref, near_ref, lower_ref)


def cells_pitchwise_kernel(
    weight_ref, vrows_ref, raw_ref, rows_ref, part_ref, rate_ref, near_ref, lower_ref, half_ref
):
    rows_from(raw_ref, half_ref, rows_ref)
    load = lambda c, r: rows_ref[c, r]
    pitchwise(load, vrows_ref, weight_ref[0], part_ref, rate_ref, near_ref, lower_ref)


def pitchwise(load, vrows_ref, omega, part_ref, rate_ref, near_ref, lower_ref):
    pitchwise_shifts(load, near_ref)
    for r in range(8):
        q = [load(c, r) for c in range(COMPS)]
        u, v, p = primitives(q)
        upper, lower = pitchwise_faces(q, v, p, near_ref, r)
        rate_ref[r] = own_instance_rate(jnp.abs(u) + jnp.abs(v), vrows_ref[r], omega)
        for c in range(COMPS):
            part_ref[c, r] = upper[c]
            lower_ref[c, r] = lower[c]
    for r in range(8):
        for c in range(COMPS):
            part_ref[c, r] = part_ref[c, r] - turn(lower_ref[c, r], 1)


def outer_kernel(
    cap, table_ref, weight_ref, rows_ref, vrows_ref, part_ref, rate_ref, halo_ref, sibling_ref,
    outer_ref, *sends
):
    omega, w_own, w_across, w_near, w_far = coefficients(weight_ref)
    load = row_loader(lambda c, r: rows_ref[c, r], halo_ref)
    even = even_tiles(vrows_ref.shape[1:])
    low = {r: load(r) for r in range(-2, 4)}
    high = {r: load(r) for r in range(4, 10)}
    picked = {
        k: [jnp.where(even, a, b) for a, b in zip(low[k - 2], high[k + 4])] for k in range(6)
    }
    rows = Rows(lambda k: picked[k])
    for l in range(2):
        along = rows.along(l + 2)
        volume = jnp.where(even, vrows_ref[l], vrows_ref[l + 6])
        rate = jnp.where(even, rate_ref[l], rate_ref[l + 6])
        outer_ref[COMPS, l] = rate * volume
        for c in range(COMPS):
            q = picked[l + 2][c]
            part = jnp.where(even, part_ref[c, l], part_ref[c, l + 6])
            sibling = jnp.where(even, sibling_ref[c, l], sibling_ref[c, l + 6])
            spectral = w_own * q + w_near * sibling
            outer_ref[c, l] = q - rate * (along[c] + part + volume * spectral)
    pack_sends(cap, outer_ref, table_ref, sends, range(POOLED))


def near_rows(weight_ref, vrows_ref, of, rows):
    omega, w_own, w_across, w_near, w_far = coefficients(weight_ref)
    for weight, (one, part, rate_of, halo, out, gain), other in (
        (w_near, of[0], of[1][0]), (w_far, of[1], of[0][0])
    ):
        load = lambda c, r: one[c, r]
        if halo is None:
            line = Rows(lambda r: [one[c, r] for c in range(COMPS)])
        else:
            line = Rows(row_loader(load, halo))
        for r in rows:
            along, volume, rate = line.along(r), vrows_ref[r], rate_of[r]
            for c in range(COMPS):
                spectral = w_own * one[c, r] + weight * other[c, r]
                out[c, r] = one[c, r] - rate * (along[c] + part[c, r] + volume * spectral)
        if halo is None:
            for r in range(8):
                gain[r] = rate_of[r] * vrows_ref[r]


def near_inner_kernel(
    weight_ref, vrows_ref, rows_ref, part_ref, rate_ref,
    sibling_ref, sibling_part_ref, sibling_rate_ref,
    next_ref, sibling_next_ref, gain_ref, sibling_gain_ref
):
    near_rows(weight_ref, vrows_ref, (
        (rows_ref, part_ref, rate_ref, None, next_ref, gain_ref),
        (sibling_ref, sibling_part_ref, sibling_rate_ref, None, sibling_next_ref, sibling_gain_ref),
    ), range(2, 6))


def near_outer_kernel(
    weight_ref, vrows_ref, rows_ref, part_ref, rate_ref, halo_ref,
    sibling_ref, sibling_part_ref, sibling_rate_ref, sibling_halo_ref, _, __, ___,
    next_ref, sibling_next_ref
):
    near_rows(weight_ref, vrows_ref, (
        (rows_ref, part_ref, rate_ref, halo_ref, next_ref, None),
        (sibling_ref, sibling_part_ref, sibling_rate_ref, sibling_halo_ref, sibling_next_ref, None),
    ), (0, 1, 6, 7))


def across_kernel(
    weight_ref, vrows_ref, rows_ref, sibling_ref, own_ref, own_gain_ref, sibling_next_ref,
    sibling_gain_ref, raw_ref, halo_ref,
    next_ref, term_ref, across_ref, lacking_ref, gain_ref,
    near_ref, lower_ref, half_ref, part_ref, rate_ref
):
    omega, w_own, w_across, w_near, w_far = coefficients(weight_ref)
    rows_from(raw_ref, half_ref, across_ref)
    load = lambda c, r: across_ref[c, r]
    pitchwise(load, vrows_ref, omega, part_ref, rate_ref, near_ref, lower_ref)
    rows = Rows(row_loader(load, halo_ref))
    for r in range(8):
        along, volume, rate = rows.along(r), vrows_ref[r], rate_ref[r]
        own_gain, sibling_gain, gain = own_gain_ref[r], sibling_gain_ref[r], rate * volume
        gain_ref[r] = (
            (w_own * w_far) * own_gain + (w_near * w_across) * sibling_gain + (w_across * w_near) * gain
        )
        lacking_ref[r] = w_far * own_gain
        for c in range(COMPS):
            q = across_ref[c, r]
            spectral = w_own * q + w_across * rows_ref[c, r] + w_far * sibling_ref[c, r]
            new = q - rate * (along[c] + part_ref[c, r] + volume * spectral)
            mine = own_ref[c, r] - (w_across * own_gain) * q
            sibling = sibling_next_ref[c, r] - (w_near * sibling_gain) * q
            next_ref[c, r] = mine
            term_ref[c, r] = w_own * mine + w_near * sibling + w_across * new


def far_kernel(
    weight_ref, vrows_ref, rows_ref, sibling_ref, across_ref, own_ref, partial_ref,
    lacking_ref, lacking_term_ref, far_ref, part_ref, rate_ref, *more
):
    halos, (next_ref, term_ref, halo_ref) = more[:-3], more[-3:]
    omega, w_own, w_across, w_near, w_far = coefficients(weight_ref)
    join_halos(halos, halo_ref)
    rows = Rows(row_loader(lambda c, r: far_ref[c, r], halo_ref))
    for r in range(8):
        along, volume, rate = rows.along(r), vrows_ref[r], rate_ref[r]
        lacking, lacking_term = lacking_ref[r], lacking_term_ref[r]
        for c in range(COMPS):
            q = far_ref[c, r]
            spectral = (
                w_own * q + w_across * sibling_ref[c, r] + w_near * rows_ref[c, r]
                + w_far * across_ref[c, r]
            )
            new = q - rate * (along[c] + part_ref[c, r] + volume * spectral)
            next_ref[c, r] = own_ref[c, r] - lacking * q
            term_ref[c, r] = partial_ref[c, r] - lacking_term * q + w_far * new


def join_halos(parts, halo_ref):
    size = COMPS // len(parts)
    for n, part in enumerate(parts):
        for c in range(size):
            for l in range(2):
                halo_ref[n * size + c, l] = part[c, l]


def last_kernel(
    space_total, cap, table_ref, rows_ref, vrows_ref, halo_ref, part_ref, rate_ref, term_ref,
    new_ref, residual_ref, new_half_ref, residual_half_ref, inverse_ref, left
):
    own = Rows(row_loader(lambda c, r: rows_ref[c, r], halo_ref))
    live_slots = table_ref[3 * FACES]
    live = (lax.broadcasted_iota(jnp.int32, vrows_ref.shape[1:], 0) // 2) < live_slots
    for r in range(8):
        inverse_ref[r] = 1.0 / vrows_ref[r]
    copies = []
    for c in range(COMPS):
        for r in range(8):
            residual = part_ref[c, r] + own.along_one(c, r) + vrows_ref[r] * term_ref[c, r]
            new = jnp.where(live, own.q(r)[c] - rate_ref[r] * residual, 0.0)
            scaled = jnp.where(live, residual * inverse_ref[r], 0.0)
            for h in range(2):
                lanes = slice(128 * h, 128 * h + 128)
                new_half_ref[c, h, pl.ds(r, 8, stride=8), :] = new[:, lanes]
                residual_half_ref[c, h, pl.ds(r, 8, stride=8), :] = scaled[:, lanes]
        for n, (half_ref, out_ref) in enumerate(
            [(new_half_ref, new_ref), (residual_half_ref, residual_ref)]
        ):
            for h in range(2):
                copy = pltpu.make_async_copy(
                    half_ref.at[c, h], out_ref.at[c, :, pl.ds(128 * h, 128)], left.at[len(copies)]
                )
                copy.start()
                copies.append(copy)
    for copy in copies:
        copy.wait()


def after_kernel(value_ref, *more):
    pass


def four_instances(
    flow_state, cell_volume, frequency, block_count, block_place, face_links, face_offset, face_flip
):
    _, comps, row_count, width = flow_state.shape
    space_total = lax.axis_size("space")
    block_total = block_place.shape[0]
    cap = pair_cap(space_total, block_total)
    state = flow_state[0]

    def over_inst(x, flip):
        return lax.ppermute(x, "inst", [(i, i ^ flip) for i in range(4)])

    def over_space(parts):
        arrived = {
            k: lax.ppermute(
                parts[k - 1], "space", [(i, partner(i, k, space_total)) for i in range(space_total)]
            )
            for k in exchanges(space_total)
        }
        return [arrived[k] for k in exchanges(space_total)]

    full = (comps, 8, 8, width)
    outer = (comps, 2, 8, width)
    plane = (8, 8, width)
    pooled = (POOLED, 2, 8, width)
    on_chip = lambda shape, dtype=F32: pltpu.VMEM(shape, dtype)
    sends_shape = lambda n: [on_chip((n * 2 * cap, width)) for _ in range(space_total - 1)]
    shifts = [pltpu.VMEM((3,) + full, F32), pltpu.VMEM(full, F32)]

    def call(kernel, out, specs, args, scratch=(), micros=0.3, out_specs=None, aliases={}):
        args = [
            pltpu.with_memory_space_constraint(x, spec.memory_space) for spec, x in zip(specs, args)
        ]
        return pl.pallas_call(
            kernel,
            out_shape=out,
            in_specs=specs,
            out_specs=out_specs or jax.tree.map(lambda _: VMEM, out),
            scratch_shapes=list(scratch),
            input_output_aliases=aliases,
            compiler_params=pltpu.CompilerParams(vmem_limit_bytes=12 << 20),
            cost_estimate=pl.CostEstimate(
                flops=0, bytes_accessed=int(micros * 3.69e6), transcendentals=0
            ),
        )(*args)

    tables = (block_count, block_place, face_links.T, face_offset.T, face_flip.T)
    in_smem = lambda *shape: pltpu.SMEM(shape, jnp.int32)
    small = [in_smem(space_total), in_smem(block_total)] + [in_smem(2, block_total)] * 3
    derived = [in_smem(space_total), in_smem(block_total)]
    half, volume_half, outer_rows, send_table, *sends = call(
        functools.partial(pack_kernel, space_total, block_total, cap),
        [
            on_chip((2, comps, row_count, 128)), on_chip((2, row_count, 128)), on_chip(outer),
            in_smem((space_total - 1) * cap), *sends_shape(comps),
        ],
        [HBM] * 5,
        (state, cell_volume, *tables[:3]),
        scratch=[pltpu.SemaphoreType.DMA((5 + 2 * comps,)), *small[:3], *derived],
        micros=1.0,
        out_specs=[VMEM] * 3 + [SMEM] + [VMEM] * (space_total - 1),
    )
    rows, vrows, table, index = call(
        functools.partial(rows_kernel, space_total, block_total, cap),
        [on_chip(full), on_chip(plane), in_smem(3 * FACES + 1), on_chip((FACES, width), jnp.int32)],
        [VMEM] * 2 + [HBM] * 5,
        (half, volume_half, *tables),
        scratch=[pltpu.SemaphoreType.DMA((5,)), *small, *derived],
        micros=1.0,
        out_specs=[VMEM] * 2 + [SMEM, VMEM],
    )
    weights = pl.pallas_call(
        weight_kernel, out_shape=pltpu.SMEM((8,), F32), in_specs=[SMEM], out_specs=SMEM
    )(frequency)
    halves = [pltpu.VMEM((comps, 2, row_count, 128), F32), pltpu.VMEM(full, F32)]
    pool = [
        pltpu.VMEM(((space_total - 1) * POOLED * 2 * cap + POOLED * 2 * FACES, width), F32),
        pltpu.VMEM(pooled, F32),
    ]

    def pitch(x, *first):
        return call(
            pitchwise_kernel,
            [on_chip(full), on_chip(plane)],
            [SMEM] + [VMEM] * (2 + len(first)),
            (weights, x, vrows, *first),
            scratch=shifts,
            micros=0.5,
        )

    across = over_inst(state, 2)
    sibling_raw = over_inst(state, 1)
    received = over_space(sends)
    part, rate = pitch(rows)
    sibling, sibling_part, sibling_rate = call(
        cells_pitchwise_kernel,
        [on_chip(full)] * 2 + [on_chip(plane)],
        [SMEM] + [VMEM] * 2,
        (weights, vrows, sibling_raw),
        scratch=shifts + halves[:1],
        micros=0.5,
    )
    own, sibling_next, own_gain, sibling_gain = call(
        near_inner_kernel,
        [on_chip(full)] * 2 + [on_chip(plane)] * 2,
        [SMEM] + [VMEM] * 7,
        (weights, vrows, rows, part, rate, sibling, sibling_part, sibling_rate),
        micros=0.3,
    )
    halo = call(
        functools.partial(halo_kernel, space_total, cap),
        on_chip(outer),
        [SMEM] + [VMEM] * (3 + space_total),
        (table, index, outer_rows, own_gain, sibling_gain, *received),
        scratch=pool,
    )
    across_halo = over_inst(halo, 2)
    sibling_halo = over_inst(halo, 1)
    next_outer, *next_sends = call(
        functools.partial(outer_kernel, cap),
        [on_chip(pooled), *sends_shape(POOLED)],
        [SMEM, SMEM] + [VMEM] * 6,
        (send_table, weights, rows, vrows, part, rate, halo, sibling),
        micros=0.3,
    )
    next_received = over_space(next_sends)
    def after(x, *first):
        return call(
            after_kernel, on_chip(x.shape), [VMEM] * (1 + len(first)), (x, *first), aliases={0: 0}, micros=0.05
        )

    far = over_inst(after(across, next_outer), 1)
    pieces = 2
    size = comps // pieces
    hx = across_halo
    far_halo = [over_inst(hx[n * size : n * size + size], 1) for n in range(pieces)]
    far_rows, far_part, far_rate = call(
        cells_pitchwise_kernel,
        [on_chip(full)] * 2 + [on_chip(plane)],
        [SMEM] + [VMEM] * 2,
        (weights, vrows, far),
        scratch=shifts + halves[:1],
        micros=0.6,
    )
    own, sibling_next = call(
        near_outer_kernel,
        [on_chip(full)] * 2,
        [SMEM] + [VMEM] * 12,
        (weights, vrows, rows, part, rate, halo, sibling, sibling_part, sibling_rate, sibling_halo,
         far_rate, own, sibling_next),
        micros=0.4,
        aliases={11: 0, 12: 1},
    )
    own, partial, across_rows, lacking, lacking_term = call(
        across_kernel,
        [on_chip(full)] * 3 + [on_chip(plane)] * 2,
        [SMEM] + [VMEM] * 9,
        (weights, vrows, rows, sibling, own, own_gain, sibling_next, sibling_gain, across, across_halo),
        scratch=shifts + halves[:1] + [halves[1], pltpu.VMEM(plane, F32)],
        micros=1.0,
    )
    next_rows, term = call(
        far_kernel,
        [on_chip(full)] * 2,
        [SMEM] + [VMEM] * (11 + len(far_halo)),
        (weights, vrows, rows, sibling, across_rows, own, partial, lacking, lacking_term,
         far_rows, far_part, far_rate, *far_halo),
        scratch=[pltpu.VMEM(outer, F32)],
        micros=0.5,
    )
    next_part, next_rate = pitch(next_rows)
    next_halo = call(
        functools.partial(next_halo_kernel, space_total, cap),
        on_chip(outer),
        [SMEM, VMEM, SMEM] + [VMEM] * (2 + space_total + len(far_halo)),
        (table, index, weights, next_outer, across_halo, next_rate, *next_received, *far_halo),
        scratch=pool + [pltpu.VMEM(outer, F32)],
    )
    new, residual = call(
        functools.partial(last_kernel, space_total, cap),
        [jax.ShapeDtypeStruct(state.shape, F32)] * 2,
        [SMEM] + [VMEM] * 6,
        (table, next_rows, vrows, next_halo, next_part, next_rate, term),
        scratch=[pltpu.VMEM((comps, 2, row_count, 128), F32)] * 2
        + [pltpu.VMEM(plane, F32), pltpu.SemaphoreType.DMA((4 * comps,))],
        micros=1.5,
        out_specs=[HBM] * 2,
    )
    return new[None], residual[None]


def spectral_matrix(instance_total, omega_value):
    position = jnp.arange(instance_total, dtype=jnp.int32)
    distance = (position[:, None] - position[None, :]) % instance_total
    parity = (1 - 2 * (distance % 2)).astype(jnp.float32)
    phase_angle = jnp.pi * distance.astype(jnp.float32) / instance_total
    safe_angle = jnp.where(distance == 0, 0.5 * jnp.pi, phase_angle)
    first_derivative = jnp.where(
        distance == 0, 0.0, 0.5 * parity * jnp.cos(safe_angle) / jnp.sin(safe_angle)
    )
    second_derivative = jnp.where(
        distance == 0,
        -(instance_total * instance_total + 2) / 12.0,
        -parity / (2.0 * jnp.sin(safe_angle) ** 2),
    )
    return omega_value * (first_derivative - TIME_VISCOSITY * second_derivative)


def block_tables(
    block_count, block_place, face_links, face_offset, face_flip, targets, slot_count, width
):
    block_total = block_place.shape[0]
    first_position = jnp.cumsum(block_count) - block_count
    block_at_position = (
        jnp.zeros((block_total,), jnp.int32)
        .at[block_place]
        .set(jnp.arange(block_total, dtype=jnp.int32))
    )
    owner_device = jnp.sum(
        (block_place[:, None] >= first_position[None, 1:]).astype(jnp.int32), axis=1
    )
    flat_slot = owner_device * slot_count + block_place - first_position[owner_device]
    target_device = targets // slot_count
    target_slot = targets % slot_count
    is_live = target_slot < block_count[target_device]
    block_index = block_at_position[
        jnp.clip(first_position[target_device] + target_slot, 0, block_total - 1)
    ]
    neighbour = face_links[block_index]
    source_slot = jnp.where(neighbour >= 0, flat_slot[jnp.clip(neighbour, 0, block_total - 1)], -1)
    column = jnp.arange(width, dtype=jnp.int32)
    flipped = face_flip[block_index][:, :, None]
    ordered = jnp.where(flipped == 1, width - 1 - column, column)
    column_index = (face_offset[block_index][:, :, None] + ordered) % width
    return (is_live, source_slot, column_index)


def attach_halos(blocks, lower, upper, source_slot):
    cells_i = blocks.shape[2]
    lower = jnp.where(
        (source_slot[:, 0] >= 0)[None, :, None, None],
        lower,
        jnp.repeat(blocks[:, :, 0:1], 2, axis=2),
    )
    upper = jnp.where(
        (source_slot[:, 1] >= 0)[None, :, None, None],
        upper,
        jnp.repeat(blocks[:, :, cells_i - 1 : cells_i], 2, axis=2),
    )
    return jnp.concatenate([lower, blocks, upper], axis=2)


def fluxes(conserved):
    inverse_rho = 1.0 / conserved[0]
    velocity_i = conserved[1] * inverse_rho
    velocity_j = conserved[2] * inverse_rho
    pressure = (HEAT_RATIO - 1.0) * (
        conserved[4]
        - 0.5
        * (conserved[1] * conserved[1] + conserved[2] * conserved[2] + conserved[3] * conserved[3])
        * inverse_rho
    )
    flux_i = jnp.stack(
        [
            conserved[1],
            conserved[1] * velocity_i + pressure,
            conserved[2] * velocity_i,
            conserved[3] * velocity_i,
            (conserved[4] + pressure) * velocity_i,
            conserved[5] * velocity_i,
        ]
    )
    flux_j = jnp.stack(
        [
            conserved[2],
            conserved[1] * velocity_j,
            conserved[2] * velocity_j + pressure,
            conserved[3] * velocity_j,
            (conserved[4] + pressure) * velocity_j,
            conserved[5] * velocity_j,
        ]
    )
    return (flux_i, flux_j, jnp.abs(velocity_i), jnp.abs(velocity_j))


def advance(extended, volumes, spectral, omega_value, instance_total):
    cells_i = extended.shape[2] - 4
    flux_i, flux_j, speed_i, speed_j = fluxes(extended)
    left_cell = extended[:, :, 1 : cells_i + 2]
    right_cell = extended[:, :, 2 : cells_i + 3]
    back_cell = extended[:, :, 0 : cells_i + 1]
    ahead_cell = extended[:, :, 3 : cells_i + 4]
    radius_i = 0.5 * (speed_i[:, 1 : cells_i + 2] + speed_i[:, 2 : cells_i + 3]) + SOUND_SPEED
    face_i = 0.5 * (flux_i[:, :, 1 : cells_i + 2] + flux_i[:, :, 2 : cells_i + 3]) - radius_i * (
        SECOND_DISSIPATION * (right_cell - left_cell)
        - FOURTH_DISSIPATION * (ahead_cell - 3.0 * right_cell + 3.0 * left_cell - back_cell)
    )
    centre = extended[:, :, 2 : cells_i + 2]
    centre_flux = flux_j[:, :, 2 : cells_i + 2]
    centre_speed = speed_j[:, 2 : cells_i + 2]
    next_cell = jnp.roll(centre, -1, axis=-1)
    prior_cell = jnp.roll(centre, 1, axis=-1)
    far_cell = jnp.roll(centre, -2, axis=-1)
    radius_j = 0.5 * (centre_speed + jnp.roll(centre_speed, -1, axis=-1)) + SOUND_SPEED
    face_j = 0.5 * (centre_flux + jnp.roll(centre_flux, -1, axis=-1)) - radius_j * (
        SECOND_DISSIPATION * (next_cell - centre)
        - FOURTH_DISSIPATION * (far_cell - 3.0 * next_cell + 3.0 * centre - prior_cell)
    )
    residual_sum = (
        face_i[:, :, 1:]
        - face_i[:, :, :-1]
        + (face_j - jnp.roll(face_j, 1, axis=-1))
        + volumes * spectral
    )
    step_rate = COURANT / (
        speed_i[:, 2 : cells_i + 2]
        + centre_speed
        + 2.0 * SOUND_SPEED
        + volumes * omega_value * 0.5 * instance_total
    )
    return (centre - step_rate * residual_sum, residual_sum / volumes)


def select_faces(selector, slabs):
    return jnp.einsum("tf,lcfxw->lctxw", selector, slabs, precision=lax.Precision.HIGHEST)


def orient_faces(slabs, permuter):
    return jnp.einsum("lctxw,tvw->lctxv", slabs, permuter, precision=lax.Precision.HIGHEST)


def on_device(
    flow_state, cell_volume, frequency, block_count, block_place, face_links, face_offset, face_flip
):
    local_count, comps, row_count, width = flow_state.shape
    slot_count = BLOCKS_MAX
    cells_i = row_count // slot_count
    space_total = lax.axis_size("space")
    space_index = lax.axis_index("space")
    targets = space_index * slot_count + jnp.arange(slot_count, dtype=jnp.int32)
    is_live, source_slot, column_index = block_tables(
        block_count, block_place, face_links, face_offset, face_flip, targets, slot_count, width
    )
    column = jnp.arange(width, dtype=jnp.int32)
    permuter = (
        column_index.reshape(slot_count * 2, width)[:, :, None] == column[None, None, :]
    ).astype(jnp.float32)
    side_index = jnp.arange(2, dtype=jnp.int32)[None, :]
    volumes = cell_volume.reshape(slot_count, cells_i, width)
    instance_total = local_count * lax.axis_size("inst")
    matrix = spectral_matrix(instance_total, frequency[0])
    row_offset = lax.axis_index("inst") * local_count
    own_rows = lax.dynamic_slice_in_dim(matrix, row_offset, local_count, 0)
    wanted_face = (source_slot * 2 + (1 - side_index)).reshape(-1)
    face_range = jnp.arange(space_total * slot_count * 2, dtype=jnp.int32)
    selector = (
        (wanted_face[:, None] == face_range[None, :]) & (source_slot.reshape(-1)[:, None] >= 0)
    ).astype(jnp.float32)
    current = flow_state
    last_residual = jnp.zeros_like(flow_state)
    for iteration in range(PSEUDO_STEPS):
        spectral_all = jnp.einsum(
            "nm,mcrb->ncrb",
            own_rows,
            lax.all_gather(current, "inst", axis=0, tiled=True),
            precision=lax.Precision.HIGHEST,
        )
        blocks = current.reshape(local_count, comps, slot_count, cells_i, width)
        faces = jnp.stack([blocks[:, :, :, 0:2], blocks[:, :, :, cells_i - 2 : cells_i]], axis=3)
        gathered = lax.all_gather(faces, "space", axis=2, tiled=True)
        gathered = gathered.reshape(local_count, comps, space_total * slot_count * 2, 2, width)
        arrived = select_faces(selector, gathered)
        oriented = orient_faces(arrived, permuter).reshape(
            local_count, comps, slot_count, 2, 2, width
        )

        def one_instance(own_blocks, slabs, spectral):
            extended = attach_halos(own_blocks, slabs[:, :, 0], slabs[:, :, 1], source_slot)
            return advance(
                extended,
                volumes,
                spectral.reshape(comps, slot_count, cells_i, width),
                frequency[0],
                instance_total,
            )

        updated, residual_now = jax.vmap(one_instance)(blocks, oriented, spectral_all)
        current = updated.reshape(flow_state.shape)
        last_residual = residual_now.reshape(flow_state.shape)
    row_live = jnp.repeat(is_live, cells_i)[None, None, :, None]
    return (jnp.where(row_live, current, 0.0), jnp.where(row_live, last_residual, 0.0))


def solution(mesh):
    return jax.shard_map(
        four_instances if mesh.shape["inst"] == 4 else on_device,
        mesh=mesh,
        in_specs=(
            P(("groups", "inst"), None, "space", None),
            P(("groups", "space"), None),
            P(),
            P("groups"),
            P("groups"),
            P("groups", None),
            P("groups", None),
            P("groups", None),
        ),
        out_specs=(
            P(("groups", "inst"), None, "space", None),
            P(("groups", "inst"), None, "space", None),
        ),
        check_vma=False,
    )
```

```python
import functools
import math

import jax
import jax.numpy as jnp
from jax import lax
from jax.experimental import pallas as pl
from jax.experimental.pallas import tpu as pltpu
from jax.sharding import PartitionSpec as P

BLOCKS_MAX = 4
PSEUDO_STEPS = 2


HEAT_RATIO = 1.4
SECOND_DISSIPATION = 0.05
FOURTH_DISSIPATION = 0.02
SOUND_SPEED = 1.0
COURANT = 0.5
TIME_VISCOSITY = 0.25

COMPS = 6
FACES = 2 * BLOCKS_MAX
POOLED = COMPS + 1
F32 = jnp.float32
VMEM = pl.BlockSpec(memory_space=pltpu.VMEM)
SMEM = pl.BlockSpec(memory_space=pltpu.SMEM)
HBM = pl.BlockSpec(memory_space=pltpu.HBM)


def spectral_weights(total):
    weights = [TIME_VISCOSITY * (total * total + 2) / 12.0]
    for k in range(1, total):
        sign = 1.0 - 2.0 * (k % 2)
        angle = math.pi * k / total
        first = 0.5 * sign * math.cos(angle) / math.sin(angle)
        second = -sign / (2.0 * math.sin(angle) ** 2)
        weights.append(first - TIME_VISCOSITY * second)
    return weights


def exchanges(total):
    return [2, 3, 1] if total == 4 else list(range(1, total))


def partner(device, k, total):
    return device ^ k if total & (total - 1) == 0 else (device + k) % total


def apart(device, source, total):
    return device ^ source if total & (total - 1) == 0 else (device - source + total) % total


def pair_cap(space_total, block_total):
    second_most = min(BLOCKS_MAX, block_total - BLOCKS_MAX - (space_total - 2))
    return 2 * max(1, second_most)


def primitives(q):
    inverse = 1.0 / q[0]
    u = q[1] * inverse
    v = q[2] * inverse
    p = (HEAT_RATIO - 1.0) * (
        q[4] - 0.5 * (q[1] * q[1] + q[2] * q[2] + q[3] * q[3]) * inverse
    )
    return u, v, p


def flux_along_i(q, u, p, c):
    if c == 0:
        return q[1]
    if c == 1:
        return q[1] * u + p
    return ((q[4] + p) if c == 4 else q[c]) * u


def flux_along_j(q, v, p):
    return [q[2], q[1] * v, q[2] * v + p, q[3] * v, (q[4] + p) * v, q[5] * v]


def ahead(x):
    return pltpu.roll(x, x.shape[1] - 1, axis=1)


def behind(x):
    return pltpu.roll(x, 1, axis=1)


DIFF_ONE = SECOND_DISSIPATION + 2.0 * FOURTH_DISSIPATION


def turn(x, shift):
    return pltpu.roll(x, shift % x.shape[1], axis=1)


def pitchwise_shifts(load, near_ref):
    for c in range(COMPS):
        for r in range(8):
            q = load(c, r)
            near_ref[0, c, r] = turn(q, -1)
            near_ref[1, c, r] = turn(q, -2)
            near_ref[2, c, r] = turn(q, 1)


def pitchwise_faces(q, v, p, near_ref, r):
    after = [near_ref[0, c, r] for c in range(COMPS)]
    _, v_after, p_after = primitives(after)
    radius = 0.5 * (jnp.abs(v) + jnp.abs(v_after)) + SOUND_SPEED
    here, there = flux_along_j(q, v, p), flux_along_j(after, v_after, p_after)
    upper, lower = [], []
    for c in range(COMPS):
        step = after[c] - q[c]
        others = (near_ref[1, c, r] - after[c]) + (q[c] - near_ref[2, c, r])
        damping = radius * (DIFF_ONE * step - FOURTH_DISSIPATION * others)
        upper.append(0.5 * there[c] - damping)
        lower.append(0.5 * here[c] - damping)
    return upper, lower


class Rows:
    def __init__(self, load):
        self.load = load
        self.state, self.prim, self.flux = {}, {}, {}
        self.steps, self.radii, self.faces = {}, {}, {}

    def q(self, r):
        if r not in self.state:
            self.state[r] = self.load(r)
        return self.state[r]

    def uvp(self, r):
        if r not in self.prim:
            self.prim[r] = primitives(self.q(r))
        return self.prim[r]

    def f(self, c, r):
        if (c, r) not in self.flux:
            u, _, p = self.uvp(r)
            self.flux[c, r] = flux_along_i(self.q(r), u, p, c)
        return self.flux[c, r]

    def step(self, c, r):
        if (c, r) not in self.steps:
            self.steps[c, r] = self.q(r + 1)[c] - self.q(r)[c]
        return self.steps[c, r]

    def radius(self, r):
        if r not in self.radii:
            speeds = jnp.abs(self.uvp(r)[0]) + jnp.abs(self.uvp(r + 1)[0])
            self.radii[r] = 0.5 * speeds + SOUND_SPEED
        return self.radii[r]

    def face(self, c, r):
        if (c, r) not in self.faces:
            damping = DIFF_ONE * self.step(c, r) - FOURTH_DISSIPATION * (
                self.step(c, r + 1) + self.step(c, r - 1)
            )
            average = 0.5 * (self.f(c, r) + self.f(c, r + 1))
            self.faces[c, r] = average - self.radius(r) * damping
        return self.faces[c, r]

    def along_one(self, c, r):
        return self.face(c, r) - self.face(c, r - 1)

    def along(self, r):
        return [self.along_one(c, r) for c in range(COMPS)]


def even_tiles(shape):
    return lax.broadcasted_iota(jnp.int32, shape, 0) % 2 == 0


def row_loader(load, halo_ref):
    def extended(r):
        out = []
        for c in range(COMPS):
            if r < 0:
                inner = pltpu.roll(load(c, r + 8), 1, axis=0)
                out.append(jnp.where(even_tiles(inner.shape), halo_ref[c, r + 2], inner))
            elif r > 7:
                inner = pltpu.roll(load(c, r - 8), 7, axis=0)
                out.append(jnp.where(even_tiles(inner.shape), inner, halo_ref[c, r - 8]))
            else:
                out.append(load(c, r))
        return out

    return extended


def rows_from(raw_ref, half_ref, rows_ref):
    for c in range(COMPS):
        for h in range(2):
            half_ref[c, h] = raw_ref[c, :, pl.ds(128 * h, 128)]
    for c in range(COMPS):
        for r in range(8):
            for h in range(2):
                rows_ref[c, r, :, pl.ds(128 * h, 128)] = half_ref[c, h, pl.ds(r, 8, stride=8), :]


def weight_kernel(frequency_ref, weight_ref):
    weights = spectral_weights(4)
    omega = frequency_ref[0]
    even = lax.axis_index("inst") % 2 == 0
    weight_ref[0] = omega
    weight_ref[1] = omega * F32(weights[0])
    weight_ref[2] = omega * F32(weights[2])
    weight_ref[3] = omega * jnp.where(even, F32(weights[3]), F32(weights[1]))
    weight_ref[4] = omega * jnp.where(even, F32(weights[1]), F32(weights[3]))


def coefficients(weight_ref):
    return [weight_ref[k] for k in range(5)]


def own_instance_rate(speeds, volume, omega):
    return COURANT / (speeds + 2.0 * SOUND_SPEED + volume * (omega * (0.5 * 4)))


def get_tables(space_total, block_total, sources, targets, arrival, more=()):
    moves = list(zip(sources, targets)) + list(more)
    copies = [
        pltpu.make_async_copy(source, target, arrival.at[n])
        for n, (source, target) in enumerate(moves)
    ]
    for copy in copies:
        copy.start()
    for copy in copies[: len(sources)]:
        copy.wait()
    counts_ref, place_ref, links_ref, first_ref, inverse_ref = targets[:3] + targets[-2:]
    total = jnp.int32(0)
    firsts = []
    for d in range(space_total):
        firsts.append(total)
        first_ref[d] = total
        total = total + counts_ref[d]
    for b in range(block_total):
        inverse_ref[place_ref[b]] = jnp.int32(b)

    def block_in(device, slot):
        return inverse_ref[jnp.minimum(first_ref[device] + slot, block_total - 1)]

    def source_of(block, side):
        link = links_ref[side, block]
        place = place_ref[jnp.maximum(link, 0)]
        owner = jnp.int32(0)
        first = jnp.int32(0)
        for d in range(1, space_total):
            past = place >= firsts[d]
            owner = jnp.where(past, d, owner)
            first = jnp.where(past, firsts[d], first)
        return link, owner, 2 * (place - first) + (1 - side)

    return block_in, source_of, copies[len(sources) :]


def pack_kernel(
    space_total, block_total, cap,
    state_ref, volume_ref, counts_in, place_in, links_in,
    half_ref, volume_half_ref, outer_ref, table_ref, *more
):
    sends = more[: space_total - 1]
    arrival, *small = more[space_total - 1 :]
    moves = []
    for c in range(COMPS + 1):
        for h in range(2):
            lanes = pl.ds(128 * h, 128)
            if c < COMPS:
                moves.append((state_ref.at[c, :, lanes], half_ref.at[h, c]))
            else:
                moves.append((volume_ref.at[:, lanes], volume_half_ref.at[h]))
    block_in, source_of, copies = get_tables(
        space_total, block_total, (counts_in, place_in, links_in), small, arrival, moves
    )
    me = lax.axis_index("space")
    few = 2 * small[0][me] <= cap
    for k in range(1, space_total):
        target = partner(me, k, space_total)
        for i in range(cap):
            _, owner, source = source_of(block_in(target, i // 2), i % 2)
            wanted = jnp.where(owner == me, source, 0)
            table_ref[(k - 1) * cap + i] = jnp.where(few, i, wanted)
    even = even_tiles((8, 128))
    for c in range(COMPS):
        copies[2 * c].wait()
        copies[2 * c + 1].wait()
        for l in range(2):
            for h in range(2):
                low = half_ref[h, c, pl.ds(l, 8, stride=8), :]
                high = half_ref[h, c, pl.ds(6 + l, 8, stride=8), :]
                outer_ref[c, l, :, pl.ds(128 * h, 128)] = jnp.where(even, low, high)
        pack_sends(cap, outer_ref, table_ref, sends, (c,))
    for copy in copies[2 * COMPS :]:
        copy.wait()


def rows_kernel(
    space_total, block_total, cap,
    half_ref, volume_half_ref, counts_in, place_in, links_in, offset_in, flip_in,
    rows_ref, vrows_ref, table_ref, index_ref, arrival, *small
):
    block_in, source_of, _ = get_tables(
        space_total, block_total, (counts_in, place_in, links_in, offset_in, flip_in), small, arrival
    )
    counts_ref, _, _, offset_ref, flip_ref = small[:5]
    width = index_ref.shape[1]
    for h in range(2):
        for r in range(8):
            rows = pl.ds(r, 8, stride=8)
            lanes = pl.ds(128 * h, 128)
            vrows_ref[r, :, lanes] = volume_half_ref[h, rows, :]
            for c in range(COMPS):
                rows_ref[c, r, :, lanes] = half_ref[h, c, rows, :]
    me = lax.axis_index("space")
    own_base = (space_total - 1) * POOLED * 2 * cap
    table_ref[3 * FACES] = counts_ref[me]
    tile = lax.broadcasted_iota(jnp.int32, (FACES, width), 0)
    start = jnp.zeros((FACES, width), jnp.int32)
    turned = jnp.zeros((FACES, width), jnp.int32)
    for f in range(FACES):
        slot, side = f // 2, f % 2
        block = block_in(me, slot)
        link, owner, source = source_of(block, side)
        shift = apart(me, owner, space_total)
        listed = 2 * counts_ref[owner] <= cap
        place = jnp.where(listed, jnp.minimum(source, cap - 1), min(f, cap - 1))
        outside = link < 0
        mine = owner == me
        base = jnp.where(mine, own_base + source, (shift - 1) * (POOLED * 2 * cap) + place)
        base = jnp.where(outside, own_base + 8 * side + f, base)
        table_ref[f] = base
        table_ref[FACES + f] = jnp.where(outside | mine, 2 * FACES, 2 * cap)
        table_ref[2 * FACES + f] = jnp.where(outside, 0, jnp.where(mine, FACES, cap))
        start = jnp.where(tile == f, jnp.where(outside, 0, offset_ref[side, block]), start)
        turned = jnp.where(tile == f, jnp.where(outside, 0, flip_ref[side, block]), turned)
    column = lax.broadcasted_iota(jnp.int32, (FACES, width), 1)
    index_ref[...] = (start + jnp.where(turned == 1, width - 1 - column, column)) % width


def pack_sends(cap, outer_ref, table_ref, sends, comps):
    for k, send_ref in enumerate(sends):
        for i in range(cap):
            f = table_ref[k * cap + i]
            for c in comps:
                for l in range(2):
                    send_ref[pl.ds((2 * c + l) * cap + i, 1), :] = outer_ref[c, l, pl.ds(f, 1), :]


def permuted_halos(space_total, cap, table_ref, index_ref, outer_ref, received, pool_ref, raw_ref):
    comps = outer_ref.shape[0]
    for k, part in zip(exchanges(len(received) + 1), received):
        pool_ref[pl.ds((k - 1) * POOLED * 2 * cap, comps * 2 * cap), :] = part[...]
    own_base = (space_total - 1) * POOLED * 2 * cap
    for c in range(comps):
        for l in range(2):
            pool_ref[pl.ds(own_base + (2 * c + l) * FACES, FACES), :] = outer_ref[c, l]
    for f in range(FACES):
        base, per_comp, per_layer = table_ref[f], table_ref[FACES + f], table_ref[2 * FACES + f]
        for c in range(comps):
            for l in range(2):
                row = base + c * per_comp + l * per_layer
                raw_ref[c, l, pl.ds(f, 1), :] = pool_ref[pl.ds(row, 1), :]
    masks, lanes = [], []
    for h in range(2):
        index = index_ref[:, pl.ds(128 * h, 128)]
        lanes.append(index & 127)
        masks.append(index < 128)
    for c in reversed(range(comps)):
        for l in range(2):
            low, high = raw_ref[c, l, :, pl.ds(0, 128)], raw_ref[c, l, :, pl.ds(128, 128)]
            for h in range(2):
                a = jnp.take_along_axis(low, lanes[h], axis=1)
                b = jnp.take_along_axis(high, lanes[h], axis=1)
                yield c, l, h, jnp.where(masks[h], a, b)


def halo_kernel(space_total, cap, table_ref, index_ref, outer_ref, _, __, *more):
    received, (halo_ref, pool_ref, raw_ref) = more[: space_total - 1], more[space_total - 1 :]
    for c, l, h, halo in permuted_halos(
        space_total, cap, table_ref, index_ref, outer_ref, received, pool_ref, raw_ref
    ):
        halo_ref[c, l, :, pl.ds(128 * h, 128)] = halo


def next_halo_kernel(
    space_total, cap, table_ref, index_ref, weight_ref, outer_ref, across_ref, _, *more
):
    received, halos = more[: space_total - 1], more[space_total - 1 : -4]
    halo_ref, pool_ref, raw_ref, far_ref = more[-4:]
    join_halos(halos, far_ref)
    omega, w_own, w_across, w_near, w_far = coefficients(weight_ref)
    gain = {}
    for c, l, h, halo in permuted_halos(
        space_total, cap, table_ref, index_ref, outer_ref, received, pool_ref, raw_ref
    ):
        if c == COMPS:
            gain[l, h] = halo
            continue
        lanes = pl.ds(128 * h, 128)
        lacking = w_across * across_ref[c, l, :, lanes] + w_far * far_ref[c, l, :, lanes]
        halo_ref[c, l, :, lanes] = halo - gain[l, h] * lacking


def pitchwise_kernel(weight_ref, rows_ref, vrows_ref, *more):
    part_ref, rate_ref, near_ref, lower_ref = more[-4:]
    pitchwise(lambda c, r: rows_ref[c, r], vrows_ref, weight_ref[0], part_ref, rate_ref, near_ref, lower_ref)


def halves_pitchwise_kernel(
    weight_ref, vrows_ref, low_ref, high_ref, rows_ref, part_ref, rate_ref, near_ref, lower_ref
):
    for h, half_ref in enumerate((low_ref, high_ref)):
        for c in range(COMPS):
            for r in range(8):
                rows_ref[c, r, :, pl.ds(128 * h, 128)] = half_ref[c, pl.ds(r, 8, stride=8), :]
    load = lambda c, r: rows_ref[c, r]
    pitchwise(load, vrows_ref, weight_ref[0], part_ref, rate_ref, near_ref, lower_ref)


def cells_pitchwise_kernel(
    weight_ref, vrows_ref, raw_ref, rows_ref, part_ref, rate_ref, near_ref, lower_ref, half_ref
):
    rows_from(raw_ref, half_ref, rows_ref)
    load = lambda c, r: rows_ref[c, r]
    pitchwise(load, vrows_ref, weight_ref[0], part_ref, rate_ref, near_ref, lower_ref)


def pitchwise(load, vrows_ref, omega, part_ref, rate_ref, near_ref, lower_ref):
    pitchwise_shifts(load, near_ref)
    for r in range(8):
        q = [load(c, r) for c in range(COMPS)]
        u, v, p = primitives(q)
        upper, lower = pitchwise_faces(q, v, p, near_ref, r)
        rate_ref[r] = own_instance_rate(jnp.abs(u) + jnp.abs(v), vrows_ref[r], omega)
        for c in range(COMPS):
            part_ref[c, r] = upper[c]
            lower_ref[c, r] = lower[c]
    for r in range(8):
        for c in range(COMPS):
            part_ref[c, r] = part_ref[c, r] - turn(lower_ref[c, r], 1)


def outer_kernel(
    cap, table_ref, weight_ref, rows_ref, vrows_ref, part_ref, rate_ref, halo_ref, sibling_ref,
    outer_ref, *sends
):
    omega, w_own, w_across, w_near, w_far = coefficients(weight_ref)
    load = row_loader(lambda c, r: rows_ref[c, r], halo_ref)
    even = even_tiles(vrows_ref.shape[1:])
    low = {r: load(r) for r in range(-2, 4)}
    high = {r: load(r) for r in range(4, 10)}
    picked = {
        k: [jnp.where(even, a, b) for a, b in zip(low[k - 2], high[k + 4])] for k in range(6)
    }
    rows = Rows(lambda k: picked[k])
    for l in range(2):
        along = rows.along(l + 2)
        volume = jnp.where(even, vrows_ref[l], vrows_ref[l + 6])
        rate = jnp.where(even, rate_ref[l], rate_ref[l + 6])
        outer_ref[COMPS, l] = rate * volume
        for c in range(COMPS):
            q = picked[l + 2][c]
            part = jnp.where(even, part_ref[c, l], part_ref[c, l + 6])
            sibling = jnp.where(even, sibling_ref[c, l], sibling_ref[c, l + 6])
            spectral = w_own * q + w_near * sibling
            outer_ref[c, l] = q - rate * (along[c] + part + volume * spectral)
    pack_sends(cap, outer_ref, table_ref, sends, range(POOLED))


def near_rows(weight_ref, vrows_ref, of, rows):
    omega, w_own, w_across, w_near, w_far = coefficients(weight_ref)
    for weight, (one, part, rate_of, halo, out, gain), other in (
        (w_near, of[0], of[1][0]), (w_far, of[1], of[0][0])
    ):
        load = lambda c, r: one[c, r]
        if halo is None:
            line = Rows(lambda r: [one[c, r] for c in range(COMPS)])
        else:
            line = Rows(row_loader(load, halo))
        for r in rows:
            along, volume, rate = line.along(r), vrows_ref[r], rate_of[r]
            for c in range(COMPS):
                spectral = w_own * one[c, r] + weight * other[c, r]
                out[c, r] = one[c, r] - rate * (along[c] + part[c, r] + volume * spectral)
        if halo is None:
            for r in range(8):
                gain[r] = rate_of[r] * vrows_ref[r]


def near_inner_kernel(
    weight_ref, vrows_ref, rows_ref, part_ref, rate_ref,
    sibling_ref, sibling_part_ref, sibling_rate_ref,
    next_ref, sibling_next_ref, gain_ref, sibling_gain_ref
):
    near_rows(weight_ref, vrows_ref, (
        (rows_ref, part_ref, rate_ref, None, next_ref, gain_ref),
        (sibling_ref, sibling_part_ref, sibling_rate_ref, None, sibling_next_ref, sibling_gain_ref),
    ), range(2, 6))


def near_outer_kernel(
    weight_ref, vrows_ref, rows_ref, part_ref, rate_ref, halo_ref,
    sibling_ref, sibling_part_ref, sibling_rate_ref, sibling_halo_ref, _, __, ___,
    next_ref, sibling_next_ref
):
    near_rows(weight_ref, vrows_ref, (
        (rows_ref, part_ref, rate_ref, halo_ref, next_ref, None),
        (sibling_ref, sibling_part_ref, sibling_rate_ref, sibling_halo_ref, sibling_next_ref, None),
    ), (0, 1, 6, 7))


def across_kernel(
    weight_ref, vrows_ref, rows_ref, sibling_ref, own_ref, own_gain_ref, sibling_next_ref,
    sibling_gain_ref, raw_ref, halo_ref,
    next_ref, term_ref, across_ref, lacking_ref, gain_ref,
    near_ref, lower_ref, half_ref, part_ref, rate_ref
):
    omega, w_own, w_across, w_near, w_far = coefficients(weight_ref)
    rows_from(raw_ref, half_ref, across_ref)
    load = lambda c, r: across_ref[c, r]
    pitchwise(load, vrows_ref, omega, part_ref, rate_ref, near_ref, lower_ref)
    rows = Rows(row_loader(load, halo_ref))
    for r in range(8):
        along, volume, rate = rows.along(r), vrows_ref[r], rate_ref[r]
        own_gain, sibling_gain, gain = own_gain_ref[r], sibling_gain_ref[r], rate * volume
        gain_ref[r] = (
            (w_own * w_far) * own_gain + (w_near * w_across) * sibling_gain + (w_across * w_near) * gain
        )
        lacking_ref[r] = w_far * own_gain
        for c in range(COMPS):
            q = across_ref[c, r]
            spectral = w_own * q + w_across * rows_ref[c, r] + w_far * sibling_ref[c, r]
            new = q - rate * (along[c] + part_ref[c, r] + volume * spectral)
            mine = own_ref[c, r] - (w_across * own_gain) * q
            sibling = sibling_next_ref[c, r] - (w_near * sibling_gain) * q
            next_ref[c, r] = mine
            term_ref[c, r] = w_own * mine + w_near * sibling + w_across * new


def far_kernel(
    weight_ref, vrows_ref, rows_ref, sibling_ref, across_ref, own_ref, partial_ref,
    lacking_ref, lacking_term_ref, far_ref, part_ref, rate_ref, *more
):
    halos, (next_ref, term_ref, halo_ref) = more[:-3], more[-3:]
    omega, w_own, w_across, w_near, w_far = coefficients(weight_ref)
    join_halos(halos, halo_ref)
    rows = Rows(row_loader(lambda c, r: far_ref[c, r], halo_ref))
    for r in range(8):
        along, volume, rate = rows.along(r), vrows_ref[r], rate_ref[r]
        lacking, lacking_term = lacking_ref[r], lacking_term_ref[r]
        for c in range(COMPS):
            q = far_ref[c, r]
            spectral = (
                w_own * q + w_across * sibling_ref[c, r] + w_near * rows_ref[c, r]
                + w_far * across_ref[c, r]
            )
            new = q - rate * (along[c] + part_ref[c, r] + volume * spectral)
            next_ref[c, r] = own_ref[c, r] - lacking * q
            term_ref[c, r] = partial_ref[c, r] - lacking_term * q + w_far * new


def join_halos(parts, halo_ref):
    tiles = [part[pl.ds(row, 8), :] for part in parts for row in range(0, part.shape[0], 8)]
    for n, tile in enumerate(tiles):
        halo_ref[n // 2, n % 2] = tile


def last_kernel(
    space_total, cap, table_ref, rows_ref, vrows_ref, halo_ref, part_ref, rate_ref, term_ref,
    new_ref, residual_ref, new_half_ref, residual_half_ref, inverse_ref, left
):
    own = Rows(row_loader(lambda c, r: rows_ref[c, r], halo_ref))
    live_slots = table_ref[3 * FACES]
    live = (lax.broadcasted_iota(jnp.int32, vrows_ref.shape[1:], 0) // 2) < live_slots
    for r in range(8):
        inverse_ref[r] = 1.0 / vrows_ref[r]
    copies = []
    for c in range(COMPS):
        for r in range(8):
            residual = part_ref[c, r] + own.along_one(c, r) + vrows_ref[r] * term_ref[c, r]
            new = jnp.where(live, own.q(r)[c] - rate_ref[r] * residual, 0.0)
            scaled = jnp.where(live, residual * inverse_ref[r], 0.0)
            for h in range(2):
                lanes = slice(128 * h, 128 * h + 128)
                new_half_ref[c, h, pl.ds(r, 8, stride=8), :] = new[:, lanes]
                residual_half_ref[c, h, pl.ds(r, 8, stride=8), :] = scaled[:, lanes]
        for n, (half_ref, out_ref) in enumerate(
            [(new_half_ref, new_ref), (residual_half_ref, residual_ref)]
        ):
            for h in range(2):
                copy = pltpu.make_async_copy(
                    half_ref.at[c, h], out_ref.at[c, :, pl.ds(128 * h, 128)], left.at[len(copies)]
                )
                copy.start()
                copies.append(copy)
    for copy in copies:
        copy.wait()


def after_kernel(value_ref, *more):
    pass


def four_instances(
    flow_state, cell_volume, frequency, block_count, block_place, face_links, face_offset, face_flip
):
    _, comps, row_count, width = flow_state.shape
    space_total = lax.axis_size("space")
    block_total = block_place.shape[0]
    cap = pair_cap(space_total, block_total)
    state = flow_state[0]

    def over_inst(x, flip):
        return lax.ppermute(x, "inst", [(i, i ^ flip) for i in range(4)])

    def over_space(parts):
        arrived = {
            k: lax.ppermute(
                parts[k - 1], "space", [(i, partner(i, k, space_total)) for i in range(space_total)]
            )
            for k in exchanges(space_total)
        }
        return [arrived[k] for k in exchanges(space_total)]

    full = (comps, 8, 8, width)
    outer = (comps, 2, 8, width)
    plane = (8, 8, width)
    pooled = (POOLED, 2, 8, width)
    on_chip = lambda shape, dtype=F32: pltpu.VMEM(shape, dtype)
    sends_shape = lambda n: [on_chip((n * 2 * cap, width)) for _ in range(space_total - 1)]
    shifts = [pltpu.VMEM((3,) + full, F32), pltpu.VMEM(full, F32)]

    def call(kernel, out, specs, args, scratch=(), micros=0.3, out_specs=None, aliases={}):
        args = [
            pltpu.with_memory_space_constraint(x, spec.memory_space) for spec, x in zip(specs, args)
        ]
        return pl.pallas_call(
            kernel,
            out_shape=out,
            in_specs=specs,
            out_specs=out_specs or jax.tree.map(lambda _: VMEM, out),
            scratch_shapes=list(scratch),
            input_output_aliases=aliases,
            compiler_params=pltpu.CompilerParams(vmem_limit_bytes=12 << 20),
            cost_estimate=pl.CostEstimate(
                flops=0, bytes_accessed=int(micros * 3.69e6), transcendentals=0
            ),
        )(*args)

    tables = (block_count, block_place, face_links.T, face_offset.T, face_flip.T)
    in_smem = lambda *shape: pltpu.SMEM(shape, jnp.int32)
    small = [in_smem(space_total), in_smem(block_total)] + [in_smem(2, block_total)] * 3
    derived = [in_smem(space_total), in_smem(block_total)]
    half, volume_half, outer_rows, send_table, *sends = call(
        functools.partial(pack_kernel, space_total, block_total, cap),
        [
            on_chip((2, comps, row_count, 128)), on_chip((2, row_count, 128)), on_chip(outer),
            in_smem((space_total - 1) * cap), *sends_shape(comps),
        ],
        [HBM] * 5,
        (state, cell_volume, *tables[:3]),
        scratch=[pltpu.SemaphoreType.DMA((5 + 2 * comps,)), *small[:3], *derived],
        micros=1.0,
        out_specs=[VMEM] * 3 + [SMEM] + [VMEM] * (space_total - 1),
    )
    rows, vrows, table, index = call(
        functools.partial(rows_kernel, space_total, block_total, cap),
        [on_chip(full), on_chip(plane), in_smem(3 * FACES + 1), on_chip((FACES, width), jnp.int32)],
        [VMEM] * 2 + [HBM] * 5,
        (half, volume_half, *tables),
        scratch=[pltpu.SemaphoreType.DMA((5,)), *small, *derived],
        micros=1.0,
        out_specs=[VMEM] * 2 + [SMEM, VMEM],
    )
    weights = pl.pallas_call(
        weight_kernel, out_shape=pltpu.SMEM((8,), F32), in_specs=[SMEM], out_specs=SMEM
    )(frequency)
    halves = [pltpu.VMEM((comps, 2, row_count, 128), F32), pltpu.VMEM(full, F32)]
    pool = [
        pltpu.VMEM(((space_total - 1) * POOLED * 2 * cap + POOLED * 2 * FACES, width), F32),
        pltpu.VMEM(pooled, F32),
    ]

    def pitch(x, *first):
        return call(
            pitchwise_kernel,
            [on_chip(full), on_chip(plane)],
            [SMEM] + [VMEM] * (2 + len(first)),
            (weights, x, vrows, *first),
            scratch=shifts,
            micros=0.5,
        )

    across = over_inst(state, 2)
    sibling_halves = [over_inst(half[h], 1) for h in range(2)]
    received = over_space(sends)
    part, rate = pitch(rows)
    sibling, sibling_part, sibling_rate = call(
        halves_pitchwise_kernel,
        [on_chip(full)] * 2 + [on_chip(plane)],
        [SMEM] + [VMEM] * 3,
        (weights, vrows, *sibling_halves),
        scratch=shifts,
        micros=0.5,
    )
    own, sibling_next, own_gain, sibling_gain = call(
        near_inner_kernel,
        [on_chip(full)] * 2 + [on_chip(plane)] * 2,
        [SMEM] + [VMEM] * 7,
        (weights, vrows, rows, part, rate, sibling, sibling_part, sibling_rate),
        micros=0.3,
    )
    halo = call(
        functools.partial(halo_kernel, space_total, cap),
        on_chip(outer),
        [SMEM] + [VMEM] * (3 + space_total),
        (table, index, outer_rows, own_gain, sibling_gain, *received),
        scratch=pool,
    )
    across_halo = over_inst(halo, 2)
    sibling_halo = over_inst(halo, 1)
    next_outer, *next_sends = call(
        functools.partial(outer_kernel, cap),
        [on_chip(pooled), *sends_shape(POOLED)],
        [SMEM, SMEM] + [VMEM] * 6,
        (send_table, weights, rows, vrows, part, rate, halo, sibling),
        micros=0.3,
    )
    next_received = over_space(next_sends)
    def after(x, *first):
        return call(
            after_kernel, on_chip(x.shape), [VMEM] * (1 + len(first)), (x, *first), aliases={0: 0}, micros=0.05
        )

    far = over_inst(after(across, next_outer), 1)
    stacked = across_halo.reshape(comps * 2 * 8, width)
    far_halo = [over_inst(x, 1) for x in (stacked[:48], stacked[48:])]
    far_rows, far_part, far_rate = call(
        cells_pitchwise_kernel,
        [on_chip(full)] * 2 + [on_chip(plane)],
        [SMEM] + [VMEM] * 2,
        (weights, vrows, far),
        scratch=shifts + halves[:1],
        micros=0.6,
    )
    own, sibling_next = call(
        near_outer_kernel,
        [on_chip(full)] * 2,
        [SMEM] + [VMEM] * 12,
        (weights, vrows, rows, part, rate, halo, sibling, sibling_part, sibling_rate, sibling_halo,
         far_rate, own, sibling_next),
        micros=0.4,
        aliases={11: 0, 12: 1},
    )
    own, partial, across_rows, lacking, lacking_term = call(
        across_kernel,
        [on_chip(full)] * 3 + [on_chip(plane)] * 2,
        [SMEM] + [VMEM] * 9,
        (weights, vrows, rows, sibling, own, own_gain, sibling_next, sibling_gain, across, across_halo),
        scratch=shifts + halves[:1] + [halves[1], pltpu.VMEM(plane, F32)],
        micros=1.0,
    )
    next_rows, term = call(
        far_kernel,
        [on_chip(full)] * 2,
        [SMEM] + [VMEM] * (11 + len(far_halo)),
        (weights, vrows, rows, sibling, across_rows, own, partial, lacking, lacking_term,
         far_rows, far_part, far_rate, *far_halo),
        scratch=[pltpu.VMEM(outer, F32)],
        micros=0.5,
    )
    next_part, next_rate = pitch(next_rows)
    next_halo = call(
        functools.partial(next_halo_kernel, space_total, cap),
        on_chip(outer),
        [SMEM, VMEM, SMEM] + [VMEM] * (2 + space_total + len(far_halo)),
        (table, index, weights, next_outer, across_halo, next_rate, *next_received, *far_halo),
        scratch=pool + [pltpu.VMEM(outer, F32)],
    )
    new, residual = call(
        functools.partial(last_kernel, space_total, cap),
        [jax.ShapeDtypeStruct(state.shape, F32)] * 2,
        [SMEM] + [VMEM] * 6,
        (table, next_rows, vrows, next_halo, next_part, next_rate, term),
        scratch=[pltpu.VMEM((comps, 2, row_count, 128), F32)] * 2
        + [pltpu.VMEM(plane, F32), pltpu.SemaphoreType.DMA((4 * comps,))],
        micros=1.5,
        out_specs=[HBM] * 2,
    )
    return new[None], residual[None]


def spectral_matrix(instance_total, omega_value):
    position = jnp.arange(instance_total, dtype=jnp.int32)
    distance = (position[:, None] - position[None, :]) % instance_total
    parity = (1 - 2 * (distance % 2)).astype(jnp.float32)
    phase_angle = jnp.pi * distance.astype(jnp.float32) / instance_total
    safe_angle = jnp.where(distance == 0, 0.5 * jnp.pi, phase_angle)
    first_derivative = jnp.where(
        distance == 0, 0.0, 0.5 * parity * jnp.cos(safe_angle) / jnp.sin(safe_angle)
    )
    second_derivative = jnp.where(
        distance == 0,
        -(instance_total * instance_total + 2) / 12.0,
        -parity / (2.0 * jnp.sin(safe_angle) ** 2),
    )
    return omega_value * (first_derivative - TIME_VISCOSITY * second_derivative)


def block_tables(
    block_count, block_place, face_links, face_offset, face_flip, targets, slot_count, width
):
    block_total = block_place.shape[0]
    first_position = jnp.cumsum(block_count) - block_count
    block_at_position = (
        jnp.zeros((block_total,), jnp.int32)
        .at[block_place]
        .set(jnp.arange(block_total, dtype=jnp.int32))
    )
    owner_device = jnp.sum(
        (block_place[:, None] >= first_position[None, 1:]).astype(jnp.int32), axis=1
    )
    flat_slot = owner_device * slot_count + block_place - first_position[owner_device]
    target_device = targets // slot_count
    target_slot = targets % slot_count
    is_live = target_slot < block_count[target_device]
    block_index = block_at_position[
        jnp.clip(first_position[target_device] + target_slot, 0, block_total - 1)
    ]
    neighbour = face_links[block_index]
    source_slot = jnp.where(neighbour >= 0, flat_slot[jnp.clip(neighbour, 0, block_total - 1)], -1)
    column = jnp.arange(width, dtype=jnp.int32)
    flipped = face_flip[block_index][:, :, None]
    ordered = jnp.where(flipped == 1, width - 1 - column, column)
    column_index = (face_offset[block_index][:, :, None] + ordered) % width
    return (is_live, source_slot, column_index)


def attach_halos(blocks, lower, upper, source_slot):
    cells_i = blocks.shape[2]
    lower = jnp.where(
        (source_slot[:, 0] >= 0)[None, :, None, None],
        lower,
        jnp.repeat(blocks[:, :, 0:1], 2, axis=2),
    )
    upper = jnp.where(
        (source_slot[:, 1] >= 0)[None, :, None, None],
        upper,
        jnp.repeat(blocks[:, :, cells_i - 1 : cells_i], 2, axis=2),
    )
    return jnp.concatenate([lower, blocks, upper], axis=2)


def fluxes(conserved):
    inverse_rho = 1.0 / conserved[0]
    velocity_i = conserved[1] * inverse_rho
    velocity_j = conserved[2] * inverse_rho
    pressure = (HEAT_RATIO - 1.0) * (
        conserved[4]
        - 0.5
        * (conserved[1] * conserved[1] + conserved[2] * conserved[2] + conserved[3] * conserved[3])
        * inverse_rho
    )
    flux_i = jnp.stack(
        [
            conserved[1],
            conserved[1] * velocity_i + pressure,
            conserved[2] * velocity_i,
            conserved[3] * velocity_i,
            (conserved[4] + pressure) * velocity_i,
            conserved[5] * velocity_i,
        ]
    )
    flux_j = jnp.stack(
        [
            conserved[2],
            conserved[1] * velocity_j,
            conserved[2] * velocity_j + pressure,
            conserved[3] * velocity_j,
            (conserved[4] + pressure) * velocity_j,
            conserved[5] * velocity_j,
        ]
    )
    return (flux_i, flux_j, jnp.abs(velocity_i), jnp.abs(velocity_j))


def advance(extended, volumes, spectral, omega_value, instance_total):
    cells_i = extended.shape[2] - 4
    flux_i, flux_j, speed_i, speed_j = fluxes(extended)
    left_cell = extended[:, :, 1 : cells_i + 2]
    right_cell = extended[:, :, 2 : cells_i + 3]
    back_cell = extended[:, :, 0 : cells_i + 1]
    ahead_cell = extended[:, :, 3 : cells_i + 4]
    radius_i = 0.5 * (speed_i[:, 1 : cells_i + 2] + speed_i[:, 2 : cells_i + 3]) + SOUND_SPEED
    face_i = 0.5 * (flux_i[:, :, 1 : cells_i + 2] + flux_i[:, :, 2 : cells_i + 3]) - radius_i * (
        SECOND_DISSIPATION * (right_cell - left_cell)
        - FOURTH_DISSIPATION * (ahead_cell - 3.0 * right_cell + 3.0 * left_cell - back_cell)
    )
    centre = extended[:, :, 2 : cells_i + 2]
    centre_flux = flux_j[:, :, 2 : cells_i + 2]
    centre_speed = speed_j[:, 2 : cells_i + 2]
    next_cell = jnp.roll(centre, -1, axis=-1)
    prior_cell = jnp.roll(centre, 1, axis=-1)
    far_cell = jnp.roll(centre, -2, axis=-1)
    radius_j = 0.5 * (centre_speed + jnp.roll(centre_speed, -1, axis=-1)) + SOUND_SPEED
    face_j = 0.5 * (centre_flux + jnp.roll(centre_flux, -1, axis=-1)) - radius_j * (
        SECOND_DISSIPATION * (next_cell - centre)
        - FOURTH_DISSIPATION * (far_cell - 3.0 * next_cell + 3.0 * centre - prior_cell)
    )
    residual_sum = (
        face_i[:, :, 1:]
        - face_i[:, :, :-1]
        + (face_j - jnp.roll(face_j, 1, axis=-1))
        + volumes * spectral
    )
    step_rate = COURANT / (
        speed_i[:, 2 : cells_i + 2]
        + centre_speed
        + 2.0 * SOUND_SPEED
        + volumes * omega_value * 0.5 * instance_total
    )
    return (centre - step_rate * residual_sum, residual_sum / volumes)


def select_faces(selector, slabs):
    return jnp.einsum("tf,lcfxw->lctxw", selector, slabs, precision=lax.Precision.HIGHEST)


def orient_faces(slabs, permuter):
    return jnp.einsum("lctxw,tvw->lctxv", slabs, permuter, precision=lax.Precision.HIGHEST)


def on_device(
    flow_state, cell_volume, frequency, block_count, block_place, face_links, face_offset, face_flip
):
    local_count, comps, row_count, width = flow_state.shape
    slot_count = BLOCKS_MAX
    cells_i = row_count // slot_count
    space_total = lax.axis_size("space")
    space_index = lax.axis_index("space")
    targets = space_index * slot_count + jnp.arange(slot_count, dtype=jnp.int32)
    is_live, source_slot, column_index = block_tables(
        block_count, block_place, face_links, face_offset, face_flip, targets, slot_count, width
    )
    column = jnp.arange(width, dtype=jnp.int32)
    permuter = (
        column_index.reshape(slot_count * 2, width)[:, :, None] == column[None, None, :]
    ).astype(jnp.float32)
    side_index = jnp.arange(2, dtype=jnp.int32)[None, :]
    volumes = cell_volume.reshape(slot_count, cells_i, width)
    instance_total = local_count * lax.axis_size("inst")
    matrix = spectral_matrix(instance_total, frequency[0])
    row_offset = lax.axis_index("inst") * local_count
    own_rows = lax.dynamic_slice_in_dim(matrix, row_offset, local_count, 0)
    wanted_face = (source_slot * 2 + (1 - side_index)).reshape(-1)
    face_range = jnp.arange(space_total * slot_count * 2, dtype=jnp.int32)
    selector = (
        (wanted_face[:, None] == face_range[None, :]) & (source_slot.reshape(-1)[:, None] >= 0)
    ).astype(jnp.float32)
    current = flow_state
    last_residual = jnp.zeros_like(flow_state)
    for iteration in range(PSEUDO_STEPS):
        spectral_all = jnp.einsum(
            "nm,mcrb->ncrb",
            own_rows,
            lax.all_gather(current, "inst", axis=0, tiled=True),
            precision=lax.Precision.HIGHEST,
        )
        blocks = current.reshape(local_count, comps, slot_count, cells_i, width)
        faces = jnp.stack([blocks[:, :, :, 0:2], blocks[:, :, :, cells_i - 2 : cells_i]], axis=3)
        gathered = lax.all_gather(faces, "space", axis=2, tiled=True)
        gathered = gathered.reshape(local_count, comps, space_total * slot_count * 2, 2, width)
        arrived = select_faces(selector, gathered)
        oriented = orient_faces(arrived, permuter).reshape(
            local_count, comps, slot_count, 2, 2, width
        )

        def one_instance(own_blocks, slabs, spectral):
            extended = attach_halos(own_blocks, slabs[:, :, 0], slabs[:, :, 1], source_slot)
            return advance(
                extended,
                volumes,
                spectral.reshape(comps, slot_count, cells_i, width),
                frequency[0],
                instance_total,
            )

        updated, residual_now = jax.vmap(one_instance)(blocks, oriented, spectral_all)
        current = updated.reshape(flow_state.shape)
        last_residual = residual_now.reshape(flow_state.shape)
    row_live = jnp.repeat(is_live, cells_i)[None, None, :, None]
    return (jnp.where(row_live, current, 0.0), jnp.where(row_live, last_residual, 0.0))


def solution(mesh):
    return jax.shard_map(
        four_instances if mesh.shape["inst"] == 4 else on_device,
        mesh=mesh,
        in_specs=(
            P(("groups", "inst"), None, "space", None),
            P(("groups", "space"), None),
            P(),
            P("groups"),
            P("groups"),
            P("groups", None),
            P("groups", None),
            P("groups", None),
        ),
        out_specs=(
            P(("groups", "inst"), None, "space", None),
            P(("groups", "inst"), None, "space", None),
        ),
        check_vma=False,
    )
```

```python
import functools
import math

import jax
import jax.numpy as jnp
from jax import lax
from jax.experimental import pallas as pl
from jax.experimental.pallas import tpu as pltpu
from jax.sharding import PartitionSpec as P

BLOCKS_MAX = 4
PSEUDO_STEPS = 2


HEAT_RATIO = 1.4
SECOND_DISSIPATION = 0.05
FOURTH_DISSIPATION = 0.02
SOUND_SPEED = 1.0
COURANT = 0.5
TIME_VISCOSITY = 0.25

COMPS = 6
FACES = 2 * BLOCKS_MAX
POOLED = COMPS + 1
F32 = jnp.float32
VMEM = pl.BlockSpec(memory_space=pltpu.VMEM)
SMEM = pl.BlockSpec(memory_space=pltpu.SMEM)
HBM = pl.BlockSpec(memory_space=pltpu.HBM)


def spectral_weights(total):
    weights = [TIME_VISCOSITY * (total * total + 2) / 12.0]
    for k in range(1, total):
        sign = 1.0 - 2.0 * (k % 2)
        angle = math.pi * k / total
        first = 0.5 * sign * math.cos(angle) / math.sin(angle)
        second = -sign / (2.0 * math.sin(angle) ** 2)
        weights.append(first - TIME_VISCOSITY * second)
    return weights


def exchanges(total):
    return [2, 3, 1] if total == 4 else list(range(1, total))


def partner(device, k, total):
    return device ^ k if total & (total - 1) == 0 else (device + k) % total


def apart(device, source, total):
    return device ^ source if total & (total - 1) == 0 else (device - source + total) % total


def pair_cap(space_total, block_total):
    second_most = min(BLOCKS_MAX, block_total - BLOCKS_MAX - (space_total - 2))
    return 2 * max(1, second_most)


def primitives(q):
    inverse = 1.0 / q[0]
    u = q[1] * inverse
    v = q[2] * inverse
    p = (HEAT_RATIO - 1.0) * (
        q[4] - 0.5 * (q[1] * q[1] + q[2] * q[2] + q[3] * q[3]) * inverse
    )
    return u, v, p


def flux_along_i(q, u, p, c):
    if c == 0:
        return q[1]
    if c == 1:
        return q[1] * u + p
    return ((q[4] + p) if c == 4 else q[c]) * u


def flux_along_j(q, v, p):
    return [q[2], q[1] * v, q[2] * v + p, q[3] * v, (q[4] + p) * v, q[5] * v]


def ahead(x):
    return pltpu.roll(x, x.shape[1] - 1, axis=1)


def behind(x):
    return pltpu.roll(x, 1, axis=1)


DIFF_ONE = SECOND_DISSIPATION + 2.0 * FOURTH_DISSIPATION


def turn(x, shift):
    return pltpu.roll(x, shift % x.shape[1], axis=1)


def pitchwise_shifts(load, near_ref):
    for c in range(COMPS):
        for r in range(8):
            q = load(c, r)
            near_ref[0, c, r] = turn(q, -1)
            near_ref[1, c, r] = turn(q, -2)
            near_ref[2, c, r] = turn(q, 1)


def pitchwise_faces(q, v, p, near_ref, r):
    after = [near_ref[0, c, r] for c in range(COMPS)]
    _, v_after, p_after = primitives(after)
    radius = 0.5 * (jnp.abs(v) + jnp.abs(v_after)) + SOUND_SPEED
    here, there = flux_along_j(q, v, p), flux_along_j(after, v_after, p_after)
    upper, lower = [], []
    for c in range(COMPS):
        step = after[c] - q[c]
        others = (near_ref[1, c, r] - after[c]) + (q[c] - near_ref[2, c, r])
        damping = radius * (DIFF_ONE * step - FOURTH_DISSIPATION * others)
        upper.append(0.5 * there[c] - damping)
        lower.append(0.5 * here[c] - damping)
    return upper, lower


class Rows:
    def __init__(self, load):
        self.load = load
        self.state, self.prim, self.flux = {}, {}, {}
        self.steps, self.radii, self.faces = {}, {}, {}

    def q(self, r):
        if r not in self.state:
            self.state[r] = self.load(r)
        return self.state[r]

    def uvp(self, r):
        if r not in self.prim:
            self.prim[r] = primitives(self.q(r))
        return self.prim[r]

    def f(self, c, r):
        if (c, r) not in self.flux:
            u, _, p = self.uvp(r)
            self.flux[c, r] = flux_along_i(self.q(r), u, p, c)
        return self.flux[c, r]

    def step(self, c, r):
        if (c, r) not in self.steps:
            self.steps[c, r] = self.q(r + 1)[c] - self.q(r)[c]
        return self.steps[c, r]

    def radius(self, r):
        if r not in self.radii:
            speeds = jnp.abs(self.uvp(r)[0]) + jnp.abs(self.uvp(r + 1)[0])
            self.radii[r] = 0.5 * speeds + SOUND_SPEED
        return self.radii[r]

    def face(self, c, r):
        if (c, r) not in self.faces:
            damping = DIFF_ONE * self.step(c, r) - FOURTH_DISSIPATION * (
                self.step(c, r + 1) + self.step(c, r - 1)
            )
            average = 0.5 * (self.f(c, r) + self.f(c, r + 1))
            self.faces[c, r] = average - self.radius(r) * damping
        return self.faces[c, r]

    def along_one(self, c, r):
        return self.face(c, r) - self.face(c, r - 1)

    def along(self, r):
        return [self.along_one(c, r) for c in range(COMPS)]


def even_tiles(shape):
    return lax.broadcasted_iota(jnp.int32, shape, 0) % 2 == 0


def row_loader(load, halo_ref):
    def extended(r):
        out = []
        for c in range(COMPS):
            if r < 0:
                inner = pltpu.roll(load(c, r + 8), 1, axis=0)
                out.append(jnp.where(even_tiles(inner.shape), halo_ref[c, r + 2], inner))
            elif r > 7:
                inner = pltpu.roll(load(c, r - 8), 7, axis=0)
                out.append(jnp.where(even_tiles(inner.shape), inner, halo_ref[c, r - 8]))
            else:
                out.append(load(c, r))
        return out

    return extended


def rows_from(raw_ref, half_ref, rows_ref):
    for c in range(COMPS):
        for h in range(2):
            half_ref[c, h] = raw_ref[c, :, pl.ds(128 * h, 128)]
    for c in range(COMPS):
        for r in range(8):
            for h in range(2):
                rows_ref[c, r, :, pl.ds(128 * h, 128)] = half_ref[c, h, pl.ds(r, 8, stride=8), :]


def weight_kernel(frequency_ref, weight_ref):
    weights = spectral_weights(4)
    omega = frequency_ref[0]
    even = lax.axis_index("inst") % 2 == 0
    weight_ref[0] = omega
    weight_ref[1] = omega * F32(weights[0])
    weight_ref[2] = omega * F32(weights[2])
    weight_ref[3] = omega * jnp.where(even, F32(weights[3]), F32(weights[1]))
    weight_ref[4] = omega * jnp.where(even, F32(weights[1]), F32(weights[3]))


def coefficients(weight_ref):
    return [weight_ref[k] for k in range(5)]


def own_instance_rate(speeds, volume, omega):
    return COURANT / (speeds + 2.0 * SOUND_SPEED + volume * (omega * (0.5 * 4)))


def get_tables(space_total, block_total, sources, targets, arrival, more=()):
    moves = list(zip(sources, targets)) + list(more)
    copies = [
        pltpu.make_async_copy(source, target, arrival.at[n])
        for n, (source, target) in enumerate(moves)
    ]
    for copy in copies:
        copy.start()
    for copy in copies[: len(sources)]:
        copy.wait()
    counts_ref, place_ref, links_ref, first_ref, inverse_ref = targets[:3] + targets[-2:]
    total = jnp.int32(0)
    firsts = []
    for d in range(space_total):
        firsts.append(total)
        first_ref[d] = total
        total = total + counts_ref[d]
    for b in range(block_total):
        inverse_ref[place_ref[b]] = jnp.int32(b)

    def block_in(device, slot):
        return inverse_ref[jnp.minimum(first_ref[device] + slot, block_total - 1)]

    def source_of(block, side):
        link = links_ref[side, block]
        place = place_ref[jnp.maximum(link, 0)]
        owner = jnp.int32(0)
        first = jnp.int32(0)
        for d in range(1, space_total):
            past = place >= firsts[d]
            owner = jnp.where(past, d, owner)
            first = jnp.where(past, firsts[d], first)
        return link, owner, 2 * (place - first) + (1 - side)

    return block_in, source_of, copies[len(sources) :]


def pack_kernel(
    space_total, block_total, cap,
    state_ref, volume_ref, counts_in, place_in, links_in,
    half_ref, volume_half_ref, outer_ref, table_ref, *more
):
    sends = more[: space_total - 1]
    arrival, *small = more[space_total - 1 :]
    moves = []
    for c in range(COMPS + 1):
        for h in range(2):
            lanes = pl.ds(128 * h, 128)
            if c < COMPS:
                moves.append((state_ref.at[c, :, lanes], half_ref.at[h, c]))
            else:
                moves.append((volume_ref.at[:, lanes], volume_half_ref.at[h]))
    block_in, source_of, copies = get_tables(
        space_total, block_total, (counts_in, place_in, links_in), small, arrival, moves
    )
    me = lax.axis_index("space")
    few = 2 * small[0][me] <= cap
    for k in range(1, space_total):
        target = partner(me, k, space_total)
        for i in range(cap):
            _, owner, source = source_of(block_in(target, i // 2), i % 2)
            wanted = jnp.where(owner == me, source, 0)
            table_ref[(k - 1) * cap + i] = jnp.where(few, i, wanted)
    even = even_tiles((8, 128))
    for c in range(COMPS):
        copies[2 * c].wait()
        copies[2 * c + 1].wait()
        for l in range(2):
            for h in range(2):
                low = half_ref[h, c, pl.ds(l, 8, stride=8), :]
                high = half_ref[h, c, pl.ds(6 + l, 8, stride=8), :]
                outer_ref[c, l, :, pl.ds(128 * h, 128)] = jnp.where(even, low, high)
        pack_sends(cap, outer_ref, table_ref, sends, (c,))
    for copy in copies[2 * COMPS :]:
        copy.wait()


def rows_kernel(
    space_total, block_total, cap,
    half_ref, volume_half_ref, counts_in, place_in, links_in, offset_in, flip_in,
    rows_ref, vrows_ref, table_ref, index_ref, arrival, *small
):
    block_in, source_of, _ = get_tables(
        space_total, block_total, (counts_in, place_in, links_in, offset_in, flip_in), small, arrival
    )
    counts_ref, _, _, offset_ref, flip_ref = small[:5]
    width = index_ref.shape[1]
    for h in range(2):
        for r in range(8):
            rows = pl.ds(r, 8, stride=8)
            lanes = pl.ds(128 * h, 128)
            vrows_ref[r, :, lanes] = volume_half_ref[h, rows, :]
            for c in range(COMPS):
                rows_ref[c, r, :, lanes] = half_ref[h, c, rows, :]
    me = lax.axis_index("space")
    own_base = (space_total - 1) * POOLED * 2 * cap
    table_ref[3 * FACES] = counts_ref[me]
    tile = lax.broadcasted_iota(jnp.int32, (FACES, width), 0)
    start = jnp.zeros((FACES, width), jnp.int32)
    turned = jnp.zeros((FACES, width), jnp.int32)
    for f in range(FACES):
        slot, side = f // 2, f % 2
        block = block_in(me, slot)
        link, owner, source = source_of(block, side)
        shift = apart(me, owner, space_total)
        listed = 2 * counts_ref[owner] <= cap
        place = jnp.where(listed, jnp.minimum(source, cap - 1), min(f, cap - 1))
        outside = link < 0
        mine = owner == me
        base = jnp.where(mine, own_base + source, (shift - 1) * (POOLED * 2 * cap) + place)
        base = jnp.where(outside, own_base + 8 * side + f, base)
        table_ref[f] = base
        table_ref[FACES + f] = jnp.where(outside | mine, 2 * FACES, 2 * cap)
        table_ref[2 * FACES + f] = jnp.where(outside, 0, jnp.where(mine, FACES, cap))
        start = jnp.where(tile == f, jnp.where(outside, 0, offset_ref[side, block]), start)
        turned = jnp.where(tile == f, jnp.where(outside, 0, flip_ref[side, block]), turned)
    column = lax.broadcasted_iota(jnp.int32, (FACES, width), 1)
    index_ref[...] = (start + jnp.where(turned == 1, width - 1 - column, column)) % width


def pack_sends(cap, outer_ref, table_ref, sends, comps):
    for k, send_ref in enumerate(sends):
        for i in range(cap):
            f = table_ref[k * cap + i]
            for c in comps:
                for l in range(2):
                    send_ref[pl.ds((2 * c + l) * cap + i, 1), :] = outer_ref[c, l, pl.ds(f, 1), :]


def permuted_halos(space_total, cap, table_ref, index_ref, outer_ref, received, pool_ref, raw_ref):
    comps = outer_ref.shape[0]
    for k, part in zip(exchanges(len(received) + 1), received):
        pool_ref[pl.ds((k - 1) * POOLED * 2 * cap, comps * 2 * cap), :] = part[...]
    own_base = (space_total - 1) * POOLED * 2 * cap
    for c in range(comps):
        for l in range(2):
            pool_ref[pl.ds(own_base + (2 * c + l) * FACES, FACES), :] = outer_ref[c, l]
    for f in range(FACES):
        base, per_comp, per_layer = table_ref[f], table_ref[FACES + f], table_ref[2 * FACES + f]
        for c in range(comps):
            for l in range(2):
                row = base + c * per_comp + l * per_layer
                raw_ref[c, l, pl.ds(f, 1), :] = pool_ref[pl.ds(row, 1), :]
    masks, lanes = [], []
    for h in range(2):
        index = index_ref[:, pl.ds(128 * h, 128)]
        lanes.append(index & 127)
        masks.append(index < 128)
    for c in reversed(range(comps)):
        for l in range(2):
            low, high = raw_ref[c, l, :, pl.ds(0, 128)], raw_ref[c, l, :, pl.ds(128, 128)]
            for h in range(2):
                a = jnp.take_along_axis(low, lanes[h], axis=1)
                b = jnp.take_along_axis(high, lanes[h], axis=1)
                yield c, l, h, jnp.where(masks[h], a, b)


def halo_kernel(space_total, cap, table_ref, index_ref, outer_ref, _, __, *more):
    received, (halo_ref, pool_ref, raw_ref) = more[: space_total - 1], more[space_total - 1 :]
    for c, l, h, halo in permuted_halos(
        space_total, cap, table_ref, index_ref, outer_ref, received, pool_ref, raw_ref
    ):
        halo_ref[c, l, :, pl.ds(128 * h, 128)] = halo


def next_halo_kernel(
    space_total, cap, table_ref, index_ref, weight_ref, outer_ref, across_ref, _, *more
):
    received, halos = more[: space_total - 1], more[space_total - 1 : -4]
    halo_ref, pool_ref, raw_ref, far_ref = more[-4:]
    join_halos(halos, far_ref)
    omega, w_own, w_across, w_near, w_far = coefficients(weight_ref)
    gain = {}
    for c, l, h, halo in permuted_halos(
        space_total, cap, table_ref, index_ref, outer_ref, received, pool_ref, raw_ref
    ):
        if c == COMPS:
            gain[l, h] = halo
            continue
        lanes = pl.ds(128 * h, 128)
        lacking = w_across * across_ref[c, l, :, lanes] + w_far * far_ref[c, l, :, lanes]
        halo_ref[c, l, :, lanes] = halo - gain[l, h] * lacking


def pitchwise_kernel(weight_ref, rows_ref, vrows_ref, *more):
    part_ref, rate_ref, near_ref, lower_ref = more[-4:]
    pitchwise(lambda c, r: rows_ref[c, r], vrows_ref, weight_ref[0], part_ref, rate_ref, near_ref, lower_ref)


def halves_pitchwise_kernel(
    weight_ref, vrows_ref, low_ref, high_ref, rows_ref, part_ref, rate_ref, near_ref, lower_ref
):
    for h, half_ref in enumerate((low_ref, high_ref)):
        for c in range(COMPS):
            for r in range(8):
                rows_ref[c, r, :, pl.ds(128 * h, 128)] = half_ref[c, pl.ds(r, 8, stride=8), :]
    load = lambda c, r: rows_ref[c, r]
    pitchwise(load, vrows_ref, weight_ref[0], part_ref, rate_ref, near_ref, lower_ref)


def cells_pitchwise_kernel(
    weight_ref, vrows_ref, raw_ref, rows_ref, part_ref, rate_ref, near_ref, lower_ref, half_ref
):
    rows_from(raw_ref, half_ref, rows_ref)
    load = lambda c, r: rows_ref[c, r]
    pitchwise(load, vrows_ref, weight_ref[0], part_ref, rate_ref, near_ref, lower_ref)


def pitchwise(load, vrows_ref, omega, part_ref, rate_ref, near_ref, lower_ref):
    pitchwise_shifts(load, near_ref)
    for r in range(8):
        q = [load(c, r) for c in range(COMPS)]
        u, v, p = primitives(q)
        upper, lower = pitchwise_faces(q, v, p, near_ref, r)
        rate_ref[r] = own_instance_rate(jnp.abs(u) + jnp.abs(v), vrows_ref[r], omega)
        for c in range(COMPS):
            part_ref[c, r] = upper[c]
            lower_ref[c, r] = lower[c]
    for r in range(8):
        for c in range(COMPS):
            part_ref[c, r] = part_ref[c, r] - turn(lower_ref[c, r], 1)


def outer_kernel(
    cap, table_ref, weight_ref, rows_ref, vrows_ref, part_ref, rate_ref, halo_ref, sibling_ref,
    outer_ref, *sends
):
    omega, w_own, w_across, w_near, w_far = coefficients(weight_ref)
    load = row_loader(lambda c, r: rows_ref[c, r], halo_ref)
    even = even_tiles(vrows_ref.shape[1:])
    low = {r: load(r) for r in range(-2, 4)}
    high = {r: load(r) for r in range(4, 10)}
    picked = {
        k: [jnp.where(even, a, b) for a, b in zip(low[k - 2], high[k + 4])] for k in range(6)
    }
    rows = Rows(lambda k: picked[k])
    for l in range(2):
        along = rows.along(l + 2)
        volume = jnp.where(even, vrows_ref[l], vrows_ref[l + 6])
        rate = jnp.where(even, rate_ref[l], rate_ref[l + 6])
        outer_ref[COMPS, l] = rate * volume
        for c in range(COMPS):
            q = picked[l + 2][c]
            part = jnp.where(even, part_ref[c, l], part_ref[c, l + 6])
            sibling = jnp.where(even, sibling_ref[c, l], sibling_ref[c, l + 6])
            spectral = w_own * q + w_near * sibling
            outer_ref[c, l] = q - rate * (along[c] + part + volume * spectral)
    pack_sends(cap, outer_ref, table_ref, sends, range(POOLED))


def near_rows(weight_ref, vrows_ref, of, rows):
    omega, w_own, w_across, w_near, w_far = coefficients(weight_ref)
    for weight, (one, part, rate_of, halo, out, gain), other in (
        (w_near, of[0], of[1][0]), (w_far, of[1], of[0][0])
    ):
        load = lambda c, r: one[c, r]
        if halo is None:
            line = Rows(lambda r: [one[c, r] for c in range(COMPS)])
        else:
            line = Rows(row_loader(load, halo))
        for r in rows:
            along, volume, rate = line.along(r), vrows_ref[r], rate_of[r]
            for c in range(COMPS):
                spectral = w_own * one[c, r] + weight * other[c, r]
                out[c, r] = one[c, r] - rate * (along[c] + part[c, r] + volume * spectral)
        if halo is None:
            for r in range(8):
                gain[r] = rate_of[r] * vrows_ref[r]


def near_inner_kernel(
    weight_ref, vrows_ref, rows_ref, part_ref, rate_ref,
    sibling_ref, sibling_part_ref, sibling_rate_ref,
    next_ref, sibling_next_ref, gain_ref, sibling_gain_ref
):
    near_rows(weight_ref, vrows_ref, (
        (rows_ref, part_ref, rate_ref, None, next_ref, gain_ref),
        (sibling_ref, sibling_part_ref, sibling_rate_ref, None, sibling_next_ref, sibling_gain_ref),
    ), range(2, 6))


def near_outer_kernel(
    weight_ref, vrows_ref, rows_ref, part_ref, rate_ref, halo_ref,
    sibling_ref, sibling_part_ref, sibling_rate_ref, sibling_halo_ref, _, __, ___,
    next_ref, sibling_next_ref
):
    near_rows(weight_ref, vrows_ref, (
        (rows_ref, part_ref, rate_ref, halo_ref, next_ref, None),
        (sibling_ref, sibling_part_ref, sibling_rate_ref, sibling_halo_ref, sibling_next_ref, None),
    ), (0, 1, 6, 7))


def across_kernel(
    weight_ref, vrows_ref, rows_ref, sibling_ref, own_ref, own_gain_ref, sibling_next_ref,
    sibling_gain_ref, raw_ref, halo_ref,
    next_ref, term_ref, across_ref, lacking_ref, gain_ref,
    near_ref, lower_ref, half_ref, part_ref, rate_ref
):
    omega, w_own, w_across, w_near, w_far = coefficients(weight_ref)
    rows_from(raw_ref, half_ref, across_ref)
    load = lambda c, r: across_ref[c, r]
    pitchwise(load, vrows_ref, omega, part_ref, rate_ref, near_ref, lower_ref)
    rows = Rows(row_loader(load, halo_ref))
    for r in range(8):
        along, volume, rate = rows.along(r), vrows_ref[r], rate_ref[r]
        own_gain, sibling_gain, gain = own_gain_ref[r], sibling_gain_ref[r], rate * volume
        gain_ref[r] = (
            (w_own * w_far) * own_gain + (w_near * w_across) * sibling_gain + (w_across * w_near) * gain
        )
        lacking_ref[r] = w_far * own_gain
        for c in range(COMPS):
            q = across_ref[c, r]
            spectral = w_own * q + w_across * rows_ref[c, r] + w_far * sibling_ref[c, r]
            new = q - rate * (along[c] + part_ref[c, r] + volume * spectral)
            mine = own_ref[c, r] - (w_across * own_gain) * q
            sibling = sibling_next_ref[c, r] - (w_near * sibling_gain) * q
            next_ref[c, r] = mine
            term_ref[c, r] = w_own * mine + w_near * sibling + w_across * new


def far_kernel(
    weight_ref, vrows_ref, rows_ref, sibling_ref, across_ref, own_ref, partial_ref,
    lacking_ref, lacking_term_ref, far_ref, part_ref, rate_ref, *more
):
    halos, (next_ref, term_ref, halo_ref) = more[:-3], more[-3:]
    omega, w_own, w_across, w_near, w_far = coefficients(weight_ref)
    join_halos(halos, halo_ref)
    rows = Rows(row_loader(lambda c, r: far_ref[c, r], halo_ref))
    for r in range(8):
        along, volume, rate = rows.along(r), vrows_ref[r], rate_ref[r]
        lacking, lacking_term = lacking_ref[r], lacking_term_ref[r]
        for c in range(COMPS):
            q = far_ref[c, r]
            spectral = (
                w_own * q + w_across * sibling_ref[c, r] + w_near * rows_ref[c, r]
                + w_far * across_ref[c, r]
            )
            new = q - rate * (along[c] + part_ref[c, r] + volume * spectral)
            next_ref[c, r] = own_ref[c, r] - lacking * q
            term_ref[c, r] = partial_ref[c, r] - lacking_term * q + w_far * new


def join_halos(parts, halo_ref):
    tiles = [part[pl.ds(row, 8), :] for part in parts for row in range(0, part.shape[0], 8)]
    for n, tile in enumerate(tiles):
        halo_ref[n // 2, n % 2] = tile


def last_kernel(
    space_total, cap, table_ref, rows_ref, vrows_ref, halo_ref, part_ref, rate_ref, term_ref,
    new_ref, residual_ref, new_half_ref, residual_half_ref, inverse_ref, left
):
    own = Rows(row_loader(lambda c, r: rows_ref[c, r], halo_ref))
    live_slots = table_ref[3 * FACES]
    live = (lax.broadcasted_iota(jnp.int32, vrows_ref.shape[1:], 0) // 2) < live_slots
    for r in range(8):
        inverse_ref[r] = 1.0 / vrows_ref[r]
    copies = []
    for c in range(COMPS):
        for r in range(8):
            residual = part_ref[c, r] + own.along_one(c, r) + vrows_ref[r] * term_ref[c, r]
            new = jnp.where(live, own.q(r)[c] - rate_ref[r] * residual, 0.0)
            scaled = jnp.where(live, residual * inverse_ref[r], 0.0)
            for h in range(2):
                lanes = slice(128 * h, 128 * h + 128)
                new_half_ref[c, h, pl.ds(r, 8, stride=8), :] = new[:, lanes]
                residual_half_ref[c, h, pl.ds(r, 8, stride=8), :] = scaled[:, lanes]
        for n, (half_ref, out_ref) in enumerate(
            [(new_half_ref, new_ref), (residual_half_ref, residual_ref)]
        ):
            for h in range(2):
                copy = pltpu.make_async_copy(
                    half_ref.at[c, h], out_ref.at[c, :, pl.ds(128 * h, 128)], left.at[len(copies)]
                )
                copy.start()
                copies.append(copy)
    for copy in copies:
        copy.wait()


def after_kernel(value_ref, *more):
    pass


def four_instances(
    flow_state, cell_volume, frequency, block_count, block_place, face_links, face_offset, face_flip
):
    _, comps, row_count, width = flow_state.shape
    space_total = lax.axis_size("space")
    block_total = block_place.shape[0]
    cap = pair_cap(space_total, block_total)
    state = flow_state[0]

    def over_inst(x, flip):
        return lax.ppermute(x, "inst", [(i, i ^ flip) for i in range(4)])

    def over_space(parts):
        arrived = {
            k: lax.ppermute(
                parts[k - 1], "space", [(i, partner(i, k, space_total)) for i in range(space_total)]
            )
            for k in exchanges(space_total)
        }
        return [arrived[k] for k in exchanges(space_total)]

    full = (comps, 8, 8, width)
    outer = (comps, 2, 8, width)
    plane = (8, 8, width)
    pooled = (POOLED, 2, 8, width)
    on_chip = lambda shape, dtype=F32: pltpu.VMEM(shape, dtype)
    sends_shape = lambda n: [on_chip((n * 2 * cap, width)) for _ in range(space_total - 1)]
    shifts = [pltpu.VMEM((3,) + full, F32), pltpu.VMEM(full, F32)]

    def call(kernel, out, specs, args, scratch=(), micros=0.3, out_specs=None, aliases={}):
        args = [
            pltpu.with_memory_space_constraint(x, spec.memory_space) for spec, x in zip(specs, args)
        ]
        return pl.pallas_call(
            kernel,
            out_shape=out,
            in_specs=specs,
            out_specs=out_specs or jax.tree.map(lambda _: VMEM, out),
            scratch_shapes=list(scratch),
            input_output_aliases=aliases,
            compiler_params=pltpu.CompilerParams(vmem_limit_bytes=12 << 20),
            cost_estimate=pl.CostEstimate(
                flops=0, bytes_accessed=int(micros * 3.69e6), transcendentals=0
            ),
        )(*args)

    tables = (block_count, block_place, face_links.T, face_offset.T, face_flip.T)
    in_smem = lambda *shape: pltpu.SMEM(shape, jnp.int32)
    small = [in_smem(space_total), in_smem(block_total)] + [in_smem(2, block_total)] * 3
    derived = [in_smem(space_total), in_smem(block_total)]
    half, volume_half, outer_rows, send_table, *sends = call(
        functools.partial(pack_kernel, space_total, block_total, cap),
        [
            on_chip((2, comps, row_count, 128)), on_chip((2, row_count, 128)), on_chip(outer),
            in_smem((space_total - 1) * cap), *sends_shape(comps),
        ],
        [HBM] * 5,
        (state, cell_volume, *tables[:3]),
        scratch=[pltpu.SemaphoreType.DMA((5 + 2 * comps,)), *small[:3], *derived],
        micros=1.0,
        out_specs=[VMEM] * 3 + [SMEM] + [VMEM] * (space_total - 1),
    )
    rows, vrows, table, index = call(
        functools.partial(rows_kernel, space_total, block_total, cap),
        [on_chip(full), on_chip(plane), in_smem(3 * FACES + 1), on_chip((FACES, width), jnp.int32)],
        [VMEM] * 2 + [HBM] * 5,
        (half, volume_half, *tables),
        scratch=[pltpu.SemaphoreType.DMA((5,)), *small, *derived],
        micros=1.0,
        out_specs=[VMEM] * 2 + [SMEM, VMEM],
    )
    weights = pl.pallas_call(
        weight_kernel, out_shape=pltpu.SMEM((8,), F32), in_specs=[SMEM], out_specs=SMEM
    )(frequency)
    halves = [pltpu.VMEM((comps, 2, row_count, 128), F32), pltpu.VMEM(full, F32)]
    pool = [
        pltpu.VMEM(((space_total - 1) * POOLED * 2 * cap + POOLED * 2 * FACES, width), F32),
        pltpu.VMEM(pooled, F32),
    ]

    def pitch(x, *first):
        return call(
            pitchwise_kernel,
            [on_chip(full), on_chip(plane)],
            [SMEM] + [VMEM] * (2 + len(first)),
            (weights, x, vrows, *first),
            scratch=shifts,
            micros=0.5,
        )

    across = over_inst(state, 2)
    sibling_halves = [over_inst(half[h], 1) for h in range(2)]
    received = over_space(sends)
    part, rate = pitch(rows)
    sibling, sibling_part, sibling_rate = call(
        halves_pitchwise_kernel,
        [on_chip(full)] * 2 + [on_chip(plane)],
        [SMEM] + [VMEM] * 3,
        (weights, vrows, *sibling_halves),
        scratch=shifts,
        micros=0.5,
    )
    own, sibling_next, own_gain, sibling_gain = call(
        near_inner_kernel,
        [on_chip(full)] * 2 + [on_chip(plane)] * 2,
        [SMEM] + [VMEM] * 7,
        (weights, vrows, rows, part, rate, sibling, sibling_part, sibling_rate),
        micros=0.3,
    )
    halo = call(
        functools.partial(halo_kernel, space_total, cap),
        on_chip(outer),
        [SMEM] + [VMEM] * (3 + space_total),
        (table, index, outer_rows, own_gain, sibling_gain, *received),
        scratch=pool,
    )
    across_halo = over_inst(halo, 2)
    sibling_halo = over_inst(halo, 1)
    next_outer, *next_sends = call(
        functools.partial(outer_kernel, cap),
        [on_chip(pooled), *sends_shape(POOLED)],
        [SMEM, SMEM] + [VMEM] * 6,
        (send_table, weights, rows, vrows, part, rate, halo, sibling),
        micros=0.3,
    )
    next_received = over_space(next_sends)
    def after(x, *first):
        return call(
            after_kernel, on_chip(x.shape), [VMEM] * (1 + len(first)), (x, *first), aliases={0: 0}, micros=0.05
        )

    far = over_inst(after(across, next_outer), 1)
    stacked = across_halo.reshape(comps * 2 * 8, width)
    far_halo = [over_inst(x, 1) for x in (stacked[:16], stacked[16:56], stacked[56:])]
    far_rows, far_part, far_rate = call(
        cells_pitchwise_kernel,
        [on_chip(full)] * 2 + [on_chip(plane)],
        [SMEM] + [VMEM] * 2,
        (weights, vrows, far),
        scratch=shifts + halves[:1],
        micros=0.6,
    )
    own, sibling_next = call(
        near_outer_kernel,
        [on_chip(full)] * 2,
        [SMEM] + [VMEM] * 12,
        (weights, vrows, rows, part, rate, halo, sibling, sibling_part, sibling_rate, sibling_halo,
         far_rate, own, sibling_next),
        micros=0.4,
        aliases={11: 0, 12: 1},
    )
    own, partial, across_rows, lacking, lacking_term = call(
        across_kernel,
        [on_chip(full)] * 3 + [on_chip(plane)] * 2,
        [SMEM] + [VMEM] * 9,
        (weights, vrows, rows, sibling, own, own_gain, sibling_next, sibling_gain, across, across_halo),
        scratch=shifts + halves[:1] + [halves[1], pltpu.VMEM(plane, F32)],
        micros=1.0,
    )
    next_rows, term = call(
        far_kernel,
        [on_chip(full)] * 2,
        [SMEM] + [VMEM] * (11 + len(far_halo)),
        (weights, vrows, rows, sibling, across_rows, own, partial, lacking, lacking_term,
         far_rows, far_part, far_rate, *far_halo),
        scratch=[pltpu.VMEM(outer, F32)],
        micros=0.5,
    )
    next_part, next_rate = pitch(next_rows)
    next_halo = call(
        functools.partial(next_halo_kernel, space_total, cap),
        on_chip(outer),
        [SMEM, VMEM, SMEM] + [VMEM] * (2 + space_total + len(far_halo)),
        (table, index, weights, next_outer, across_halo, next_rate, *next_received, *far_halo),
        scratch=pool + [pltpu.VMEM(outer, F32)],
    )
    new, residual = call(
        functools.partial(last_kernel, space_total, cap),
        [jax.ShapeDtypeStruct(state.shape, F32)] * 2,
        [SMEM] + [VMEM] * 6,
        (table, next_rows, vrows, next_halo, next_part, next_rate, term),
        scratch=[pltpu.VMEM((comps, 2, row_count, 128), F32)] * 2
        + [pltpu.VMEM(plane, F32), pltpu.SemaphoreType.DMA((4 * comps,))],
        micros=1.5,
        out_specs=[HBM] * 2,
    )
    return new[None], residual[None]


def spectral_matrix(instance_total, omega_value):
    position = jnp.arange(instance_total, dtype=jnp.int32)
    distance = (position[:, None] - position[None, :]) % instance_total
    parity = (1 - 2 * (distance % 2)).astype(jnp.float32)
    phase_angle = jnp.pi * distance.astype(jnp.float32) / instance_total
    safe_angle = jnp.where(distance == 0, 0.5 * jnp.pi, phase_angle)
    first_derivative = jnp.where(
        distance == 0, 0.0, 0.5 * parity * jnp.cos(safe_angle) / jnp.sin(safe_angle)
    )
    second_derivative = jnp.where(
        distance == 0,
        -(instance_total * instance_total + 2) / 12.0,
        -parity / (2.0 * jnp.sin(safe_angle) ** 2),
    )
    return omega_value * (first_derivative - TIME_VISCOSITY * second_derivative)


def block_tables(
    block_count, block_place, face_links, face_offset, face_flip, targets, slot_count, width
):
    block_total = block_place.shape[0]
    first_position = jnp.cumsum(block_count) - block_count
    block_at_position = (
        jnp.zeros((block_total,), jnp.int32)
        .at[block_place]
        .set(jnp.arange(block_total, dtype=jnp.int32))
    )
    owner_device = jnp.sum(
        (block_place[:, None] >= first_position[None, 1:]).astype(jnp.int32), axis=1
    )
    flat_slot = owner_device * slot_count + block_place - first_position[owner_device]
    target_device = targets // slot_count
    target_slot = targets % slot_count
    is_live = target_slot < block_count[target_device]
    block_index = block_at_position[
        jnp.clip(first_position[target_device] + target_slot, 0, block_total - 1)
    ]
    neighbour = face_links[block_index]
    source_slot = jnp.where(neighbour >= 0, flat_slot[jnp.clip(neighbour, 0, block_total - 1)], -1)
    column = jnp.arange(width, dtype=jnp.int32)
    flipped = face_flip[block_index][:, :, None]
    ordered = jnp.where(flipped == 1, width - 1 - column, column)
    column_index = (face_offset[block_index][:, :, None] + ordered) % width
    return (is_live, source_slot, column_index)


def attach_halos(blocks, lower, upper, source_slot):
    cells_i = blocks.shape[2]
    lower = jnp.where(
        (source_slot[:, 0] >= 0)[None, :, None, None],
        lower,
        jnp.repeat(blocks[:, :, 0:1], 2, axis=2),
    )
    upper = jnp.where(
        (source_slot[:, 1] >= 0)[None, :, None, None],
        upper,
        jnp.repeat(blocks[:, :, cells_i - 1 : cells_i], 2, axis=2),
    )
    return jnp.concatenate([lower, blocks, upper], axis=2)


def fluxes(conserved):
    inverse_rho = 1.0 / conserved[0]
    velocity_i = conserved[1] * inverse_rho
    velocity_j = conserved[2] * inverse_rho
    pressure = (HEAT_RATIO - 1.0) * (
        conserved[4]
        - 0.5
        * (conserved[1] * conserved[1] + conserved[2] * conserved[2] + conserved[3] * conserved[3])
        * inverse_rho
    )
    flux_i = jnp.stack(
        [
            conserved[1],
            conserved[1] * velocity_i + pressure,
            conserved[2] * velocity_i,
            conserved[3] * velocity_i,
            (conserved[4] + pressure) * velocity_i,
            conserved[5] * velocity_i,
        ]
    )
    flux_j = jnp.stack(
        [
            conserved[2],
            conserved[1] * velocity_j,
            conserved[2] * velocity_j + pressure,
            conserved[3] * velocity_j,
            (conserved[4] + pressure) * velocity_j,
            conserved[5] * velocity_j,
        ]
    )
    return (flux_i, flux_j, jnp.abs(velocity_i), jnp.abs(velocity_j))


def advance(extended, volumes, spectral, omega_value, instance_total):
    cells_i = extended.shape[2] - 4
    flux_i, flux_j, speed_i, speed_j = fluxes(extended)
    left_cell = extended[:, :, 1 : cells_i + 2]
    right_cell = extended[:, :, 2 : cells_i + 3]
    back_cell = extended[:, :, 0 : cells_i + 1]
    ahead_cell = extended[:, :, 3 : cells_i + 4]
    radius_i = 0.5 * (speed_i[:, 1 : cells_i + 2] + speed_i[:, 2 : cells_i + 3]) + SOUND_SPEED
    face_i = 0.5 * (flux_i[:, :, 1 : cells_i + 2] + flux_i[:, :, 2 : cells_i + 3]) - radius_i * (
        SECOND_DISSIPATION * (right_cell - left_cell)
        - FOURTH_DISSIPATION * (ahead_cell - 3.0 * right_cell + 3.0 * left_cell - back_cell)
    )
    centre = extended[:, :, 2 : cells_i + 2]
    centre_flux = flux_j[:, :, 2 : cells_i + 2]
    centre_speed = speed_j[:, 2 : cells_i + 2]
    next_cell = jnp.roll(centre, -1, axis=-1)
    prior_cell = jnp.roll(centre, 1, axis=-1)
    far_cell = jnp.roll(centre, -2, axis=-1)
    radius_j = 0.5 * (centre_speed + jnp.roll(centre_speed, -1, axis=-1)) + SOUND_SPEED
    face_j = 0.5 * (centre_flux + jnp.roll(centre_flux, -1, axis=-1)) - radius_j * (
        SECOND_DISSIPATION * (next_cell - centre)
        - FOURTH_DISSIPATION * (far_cell - 3.0 * next_cell + 3.0 * centre - prior_cell)
    )
    residual_sum = (
        face_i[:, :, 1:]
        - face_i[:, :, :-1]
        + (face_j - jnp.roll(face_j, 1, axis=-1))
        + volumes * spectral
    )
    step_rate = COURANT / (
        speed_i[:, 2 : cells_i + 2]
        + centre_speed
        + 2.0 * SOUND_SPEED
        + volumes * omega_value * 0.5 * instance_total
    )
    return (centre - step_rate * residual_sum, residual_sum / volumes)


def select_faces(selector, slabs):
    return jnp.einsum("tf,lcfxw->lctxw", selector, slabs, precision=lax.Precision.HIGHEST)


def orient_faces(slabs, permuter):
    return jnp.einsum("lctxw,tvw->lctxv", slabs, permuter, precision=lax.Precision.HIGHEST)


def on_device(
    flow_state, cell_volume, frequency, block_count, block_place, face_links, face_offset, face_flip
):
    local_count, comps, row_count, width = flow_state.shape
    slot_count = BLOCKS_MAX
    cells_i = row_count // slot_count
    space_total = lax.axis_size("space")
    space_index = lax.axis_index("space")
    targets = space_index * slot_count + jnp.arange(slot_count, dtype=jnp.int32)
    is_live, source_slot, column_index = block_tables(
        block_count, block_place, face_links, face_offset, face_flip, targets, slot_count, width
    )
    column = jnp.arange(width, dtype=jnp.int32)
    permuter = (
        column_index.reshape(slot_count * 2, width)[:, :, None] == column[None, None, :]
    ).astype(jnp.float32)
    side_index = jnp.arange(2, dtype=jnp.int32)[None, :]
    volumes = cell_volume.reshape(slot_count, cells_i, width)
    instance_total = local_count * lax.axis_size("inst")
    matrix = spectral_matrix(instance_total, frequency[0])
    row_offset = lax.axis_index("inst") * local_count
    own_rows = lax.dynamic_slice_in_dim(matrix, row_offset, local_count, 0)
    wanted_face = (source_slot * 2 + (1 - side_index)).reshape(-1)
    face_range = jnp.arange(space_total * slot_count * 2, dtype=jnp.int32)
    selector = (
        (wanted_face[:, None] == face_range[None, :]) & (source_slot.reshape(-1)[:, None] >= 0)
    ).astype(jnp.float32)
    current = flow_state
    last_residual = jnp.zeros_like(flow_state)
    for iteration in range(PSEUDO_STEPS):
        spectral_all = jnp.einsum(
            "nm,mcrb->ncrb",
            own_rows,
            lax.all_gather(current, "inst", axis=0, tiled=True),
            precision=lax.Precision.HIGHEST,
        )
        blocks = current.reshape(local_count, comps, slot_count, cells_i, width)
        faces = jnp.stack([blocks[:, :, :, 0:2], blocks[:, :, :, cells_i - 2 : cells_i]], axis=3)
        gathered = lax.all_gather(faces, "space", axis=2, tiled=True)
        gathered = gathered.reshape(local_count, comps, space_total * slot_count * 2, 2, width)
        arrived = select_faces(selector, gathered)
        oriented = orient_faces(arrived, permuter).reshape(
            local_count, comps, slot_count, 2, 2, width
        )

        def one_instance(own_blocks, slabs, spectral):
            extended = attach_halos(own_blocks, slabs[:, :, 0], slabs[:, :, 1], source_slot)
            return advance(
                extended,
                volumes,
                spectral.reshape(comps, slot_count, cells_i, width),
                frequency[0],
                instance_total,
            )

        updated, residual_now = jax.vmap(one_instance)(blocks, oriented, spectral_all)
        current = updated.reshape(flow_state.shape)
        last_residual = residual_now.reshape(flow_state.shape)
    row_live = jnp.repeat(is_live, cells_i)[None, None, :, None]
    return (jnp.where(row_live, current, 0.0), jnp.where(row_live, last_residual, 0.0))


def solution(mesh):
    return jax.shard_map(
        four_instances if mesh.shape["inst"] == 4 else on_device,
        mesh=mesh,
        in_specs=(
            P(("groups", "inst"), None, "space", None),
            P(("groups", "space"), None),
            P(),
            P("groups"),
            P("groups"),
            P("groups", None),
            P("groups", None),
            P("groups", None),
        ),
        out_specs=(
            P(("groups", "inst"), None, "space", None),
            P(("groups", "inst"), None, "space", None),
        ),
        check_vma=False,
    )
```

```python
import functools
import math

import jax
import jax.numpy as jnp
from jax import lax
from jax.experimental import pallas as pl
from jax.experimental.pallas import tpu as pltpu
from jax.sharding import PartitionSpec as P

BLOCKS_MAX = 4
PSEUDO_STEPS = 2


HEAT_RATIO = 1.4
SECOND_DISSIPATION = 0.05
FOURTH_DISSIPATION = 0.02
SOUND_SPEED = 1.0
COURANT = 0.5
TIME_VISCOSITY = 0.25

COMPS = 6
FACES = 2 * BLOCKS_MAX
POOLED = COMPS + 1
F32 = jnp.float32
VMEM = pl.BlockSpec(memory_space=pltpu.VMEM)
SMEM = pl.BlockSpec(memory_space=pltpu.SMEM)
HBM = pl.BlockSpec(memory_space=pltpu.HBM)


def spectral_weights(total):
    weights = [TIME_VISCOSITY * (total * total + 2) / 12.0]
    for k in range(1, total):
        sign = 1.0 - 2.0 * (k % 2)
        angle = math.pi * k / total
        first = 0.5 * sign * math.cos(angle) / math.sin(angle)
        second = -sign / (2.0 * math.sin(angle) ** 2)
        weights.append(first - TIME_VISCOSITY * second)
    return weights


def exchanges(total):
    return [2, 3, 1] if total == 4 else list(range(1, total))


def partner(device, k, total):
    return device ^ k if total & (total - 1) == 0 else (device + k) % total


def apart(device, source, total):
    return device ^ source if total & (total - 1) == 0 else (device - source + total) % total


def pair_cap(space_total, block_total):
    second_most = min(BLOCKS_MAX, block_total - BLOCKS_MAX - (space_total - 2))
    return 2 * max(1, second_most)


def primitives(q):
    inverse = 1.0 / q[0]
    u = q[1] * inverse
    v = q[2] * inverse
    p = (HEAT_RATIO - 1.0) * (
        q[4] - 0.5 * (q[1] * q[1] + q[2] * q[2] + q[3] * q[3]) * inverse
    )
    return u, v, p


def flux_along_i(q, u, p, c):
    if c == 0:
        return q[1]
    if c == 1:
        return q[1] * u + p
    return ((q[4] + p) if c == 4 else q[c]) * u


def flux_along_j(q, v, p):
    return [q[2], q[1] * v, q[2] * v + p, q[3] * v, (q[4] + p) * v, q[5] * v]


def ahead(x):
    return pltpu.roll(x, x.shape[1] - 1, axis=1)


def behind(x):
    return pltpu.roll(x, 1, axis=1)


DIFF_ONE = SECOND_DISSIPATION + 2.0 * FOURTH_DISSIPATION


def turn(x, shift):
    return pltpu.roll(x, shift % x.shape[1], axis=1)


def pitchwise_shifts(load, near_ref):
    for c in range(COMPS):
        for r in range(8):
            q = load(c, r)
            near_ref[0, c, r] = turn(q, -1)
            near_ref[1, c, r] = turn(q, -2)
            near_ref[2, c, r] = turn(q, 1)


def pitchwise_faces(q, v, p, near_ref, r):
    after = [near_ref[0, c, r] for c in range(COMPS)]
    _, v_after, p_after = primitives(after)
    radius = 0.5 * (jnp.abs(v) + jnp.abs(v_after)) + SOUND_SPEED
    here, there = flux_along_j(q, v, p), flux_along_j(after, v_after, p_after)
    upper, lower = [], []
    for c in range(COMPS):
        step = after[c] - q[c]
        others = (near_ref[1, c, r] - after[c]) + (q[c] - near_ref[2, c, r])
        damping = radius * (DIFF_ONE * step - FOURTH_DISSIPATION * others)
        upper.append(0.5 * there[c] - damping)
        lower.append(0.5 * here[c] - damping)
    return upper, lower


class Rows:
    def __init__(self, load):
        self.load = load
        self.state, self.prim, self.flux = {}, {}, {}
        self.steps, self.radii, self.faces = {}, {}, {}

    def q(self, r):
        if r not in self.state:
            self.state[r] = self.load(r)
        return self.state[r]

    def uvp(self, r):
        if r not in self.prim:
            self.prim[r] = primitives(self.q(r))
        return self.prim[r]

    def f(self, c, r):
        if (c, r) not in self.flux:
            u, _, p = self.uvp(r)
            self.flux[c, r] = flux_along_i(self.q(r), u, p, c)
        return self.flux[c, r]

    def step(self, c, r):
        if (c, r) not in self.steps:
            self.steps[c, r] = self.q(r + 1)[c] - self.q(r)[c]
        return self.steps[c, r]

    def radius(self, r):
        if r not in self.radii:
            speeds = jnp.abs(self.uvp(r)[0]) + jnp.abs(self.uvp(r + 1)[0])
            self.radii[r] = 0.5 * speeds + SOUND_SPEED
        return self.radii[r]

    def face(self, c, r):
        if (c, r) not in self.faces:
            damping = DIFF_ONE * self.step(c, r) - FOURTH_DISSIPATION * (
                self.step(c, r + 1) + self.step(c, r - 1)
            )
            average = 0.5 * (self.f(c, r) + self.f(c, r + 1))
            self.faces[c, r] = average - self.radius(r) * damping
        return self.faces[c, r]

    def along_one(self, c, r):
        return self.face(c, r) - self.face(c, r - 1)

    def along(self, r):
        return [self.along_one(c, r) for c in range(COMPS)]


def even_tiles(shape):
    return lax.broadcasted_iota(jnp.int32, shape, 0) % 2 == 0


def row_loader(load, halo_ref):
    def extended(r):
        out = []
        for c in range(COMPS):
            if r < 0:
                inner = pltpu.roll(load(c, r + 8), 1, axis=0)
                out.append(jnp.where(even_tiles(inner.shape), halo_ref[c, r + 2], inner))
            elif r > 7:
                inner = pltpu.roll(load(c, r - 8), 7, axis=0)
                out.append(jnp.where(even_tiles(inner.shape), inner, halo_ref[c, r - 8]))
            else:
                out.append(load(c, r))
        return out

    return extended


def rows_from(raw_ref, half_ref, rows_ref):
    for c in range(COMPS):
        for h in range(2):
            half_ref[c, h] = raw_ref[c, :, pl.ds(128 * h, 128)]
    for c in range(COMPS):
        for r in range(8):
            for h in range(2):
                rows_ref[c, r, :, pl.ds(128 * h, 128)] = half_ref[c, h, pl.ds(r, 8, stride=8), :]


def weight_kernel(frequency_ref, weight_ref):
    weights = spectral_weights(4)
    omega = frequency_ref[0]
    even = lax.axis_index("inst") % 2 == 0
    weight_ref[0] = omega
    weight_ref[1] = omega * F32(weights[0])
    weight_ref[2] = omega * F32(weights[2])
    weight_ref[3] = omega * jnp.where(even, F32(weights[3]), F32(weights[1]))
    weight_ref[4] = omega * jnp.where(even, F32(weights[1]), F32(weights[3]))


def coefficients(weight_ref):
    return [weight_ref[k] for k in range(5)]


def own_instance_rate(speeds, volume, omega):
    return COURANT / (speeds + 2.0 * SOUND_SPEED + volume * (omega * (0.5 * 4)))


def get_tables(space_total, block_total, sources, targets, arrival, more=()):
    moves = list(zip(sources, targets)) + list(more)
    copies = [
        pltpu.make_async_copy(source, target, arrival.at[n])
        for n, (source, target) in enumerate(moves)
    ]
    for copy in copies:
        copy.start()
    for copy in copies[: len(sources)]:
        copy.wait()
    counts_ref, place_ref, links_ref, first_ref, inverse_ref = targets[:3] + targets[-2:]
    total = jnp.int32(0)
    firsts = []
    for d in range(space_total):
        firsts.append(total)
        first_ref[d] = total
        total = total + counts_ref[d]
    for b in range(block_total):
        inverse_ref[place_ref[b]] = jnp.int32(b)

    def block_in(device, slot):
        return inverse_ref[jnp.minimum(first_ref[device] + slot, block_total - 1)]

    def source_of(block, side):
        link = links_ref[side, block]
        place = place_ref[jnp.maximum(link, 0)]
        owner = jnp.int32(0)
        first = jnp.int32(0)
        for d in range(1, space_total):
            past = place >= firsts[d]
            owner = jnp.where(past, d, owner)
            first = jnp.where(past, firsts[d], first)
        return link, owner, 2 * (place - first) + (1 - side)

    return block_in, source_of, copies[len(sources) :]


def pack_kernel(
    space_total, block_total, cap,
    state_ref, volume_ref, counts_in, place_in, links_in,
    half_ref, volume_half_ref, outer_ref, table_ref, *more
):
    sends = more[: space_total - 1]
    arrival, *small = more[space_total - 1 :]
    moves = []
    for c in range(COMPS + 1):
        for h in range(2):
            lanes = pl.ds(128 * h, 128)
            if c < COMPS:
                moves.append((state_ref.at[c, :, lanes], half_ref.at[h, c]))
            else:
                moves.append((volume_ref.at[:, lanes], volume_half_ref.at[h]))
    block_in, source_of, copies = get_tables(
        space_total, block_total, (counts_in, place_in, links_in), small, arrival, moves
    )
    me = lax.axis_index("space")
    few = 2 * small[0][me] <= cap
    for k in range(1, space_total):
        target = partner(me, k, space_total)
        for i in range(cap):
            _, owner, source = source_of(block_in(target, i // 2), i % 2)
            wanted = jnp.where(owner == me, source, 0)
            table_ref[(k - 1) * cap + i] = jnp.where(few, i, wanted)
    even = even_tiles((8, 128))
    for c in range(COMPS):
        copies[2 * c].wait()
        copies[2 * c + 1].wait()
        for l in range(2):
            for h in range(2):
                low = half_ref[h, c, pl.ds(l, 8, stride=8), :]
                high = half_ref[h, c, pl.ds(6 + l, 8, stride=8), :]
                outer_ref[c, l, :, pl.ds(128 * h, 128)] = jnp.where(even, low, high)
        pack_sends(cap, outer_ref, table_ref, sends, (c,))
    for copy in copies[2 * COMPS :]:
        copy.wait()


def rows_kernel(
    space_total, block_total, cap,
    half_ref, volume_half_ref, counts_in, place_in, links_in, offset_in, flip_in,
    rows_ref, vrows_ref, table_ref, index_ref, arrival, *small
):
    block_in, source_of, _ = get_tables(
        space_total, block_total, (counts_in, place_in, links_in, offset_in, flip_in), small, arrival
    )
    counts_ref, _, _, offset_ref, flip_ref = small[:5]
    width = index_ref.shape[1]
    for h in range(2):
        for r in range(8):
            rows = pl.ds(r, 8, stride=8)
            lanes = pl.ds(128 * h, 128)
            vrows_ref[r, :, lanes] = volume_half_ref[h, rows, :]
            for c in range(COMPS):
                rows_ref[c, r, :, lanes] = half_ref[h, c, rows, :]
    me = lax.axis_index("space")
    own_base = (space_total - 1) * POOLED * 2 * cap
    table_ref[3 * FACES] = counts_ref[me]
    tile = lax.broadcasted_iota(jnp.int32, (FACES, width), 0)
    start = jnp.zeros((FACES, width), jnp.int32)
    turned = jnp.zeros((FACES, width), jnp.int32)
    for f in range(FACES):
        slot, side = f // 2, f % 2
        block = block_in(me, slot)
        link, owner, source = source_of(block, side)
        shift = apart(me, owner, space_total)
        listed = 2 * counts_ref[owner] <= cap
        place = jnp.where(listed, jnp.minimum(source, cap - 1), min(f, cap - 1))
        outside = link < 0
        mine = owner == me
        base = jnp.where(mine, own_base + source, (shift - 1) * (POOLED * 2 * cap) + place)
        base = jnp.where(outside, own_base + 8 * side + f, base)
        table_ref[f] = base
        table_ref[FACES + f] = jnp.where(outside | mine, 2 * FACES, 2 * cap)
        table_ref[2 * FACES + f] = jnp.where(outside, 0, jnp.where(mine, FACES, cap))
        start = jnp.where(tile == f, jnp.where(outside, 0, offset_ref[side, block]), start)
        turned = jnp.where(tile == f, jnp.where(outside, 0, flip_ref[side, block]), turned)
    column = lax.broadcasted_iota(jnp.int32, (FACES, width), 1)
    index_ref[...] = (start + jnp.where(turned == 1, width - 1 - column, column)) % width


def pack_sends(cap, outer_ref, table_ref, sends, comps):
    for k, send_ref in enumerate(sends):
        for i in range(cap):
            f = table_ref[k * cap + i]
            for c in comps:
                for l in range(2):
                    send_ref[pl.ds((2 * c + l) * cap + i, 1), :] = outer_ref[c, l, pl.ds(f, 1), :]


def permuted_halos(space_total, cap, table_ref, index_ref, outer_ref, received, pool_ref, raw_ref):
    comps = outer_ref.shape[0]
    for k, part in zip(exchanges(len(received) + 1), received):
        pool_ref[pl.ds((k - 1) * POOLED * 2 * cap, comps * 2 * cap), :] = part[...]
    own_base = (space_total - 1) * POOLED * 2 * cap
    for c in range(comps):
        for l in range(2):
            pool_ref[pl.ds(own_base + (2 * c + l) * FACES, FACES), :] = outer_ref[c, l]
    for f in range(FACES):
        base, per_comp, per_layer = table_ref[f], table_ref[FACES + f], table_ref[2 * FACES + f]
        for c in range(comps):
            for l in range(2):
                row = base + c * per_comp + l * per_layer
                raw_ref[c, l, pl.ds(f, 1), :] = pool_ref[pl.ds(row, 1), :]
    masks, lanes = [], []
    for h in range(2):
        index = index_ref[:, pl.ds(128 * h, 128)]
        lanes.append(index & 127)
        masks.append(index < 128)
    for c in reversed(range(comps)):
        for l in range(2):
            low, high = raw_ref[c, l, :, pl.ds(0, 128)], raw_ref[c, l, :, pl.ds(128, 128)]
            for h in range(2):
                a = jnp.take_along_axis(low, lanes[h], axis=1)
                b = jnp.take_along_axis(high, lanes[h], axis=1)
                yield c, l, h, jnp.where(masks[h], a, b)


def halo_kernel(space_total, cap, table_ref, index_ref, outer_ref, _, __, *more):
    received, (halo_ref, pool_ref, raw_ref) = more[: space_total - 1], more[space_total - 1 :]
    for c, l, h, halo in permuted_halos(
        space_total, cap, table_ref, index_ref, outer_ref, received, pool_ref, raw_ref
    ):
        halo_ref[c, l, :, pl.ds(128 * h, 128)] = halo


def next_halos(
    space_total, cap, table_ref, index_ref, weight_ref, outer_ref, across_ref, halos, received,
    halo_ref, pool_ref, raw_ref, far_ref
):
    join_halos(halos, far_ref)
    omega, w_own, w_across, w_near, w_far = coefficients(weight_ref)
    gain = {}
    for c, l, h, halo in permuted_halos(
        space_total, cap, table_ref, index_ref, outer_ref, received, pool_ref, raw_ref
    ):
        if c == COMPS:
            gain[l, h] = halo
            continue
        lanes = pl.ds(128 * h, 128)
        lacking = w_across * across_ref[c, l, :, lanes] + w_far * far_ref[c, l, :, lanes]
        halo_ref[c, l, :, lanes] = halo - gain[l, h] * lacking


def pitchwise_kernel(weight_ref, rows_ref, vrows_ref, *more):
    part_ref, rate_ref, near_ref, lower_ref = more[-4:]
    pitchwise(lambda c, r: rows_ref[c, r], vrows_ref, weight_ref[0], part_ref, rate_ref, near_ref, lower_ref)


def halves_pitchwise_kernel(
    weight_ref, vrows_ref, low_ref, high_ref, rows_ref, part_ref, rate_ref, near_ref, lower_ref
):
    for h, half_ref in enumerate((low_ref, high_ref)):
        for c in range(COMPS):
            for r in range(8):
                rows_ref[c, r, :, pl.ds(128 * h, 128)] = half_ref[c, pl.ds(r, 8, stride=8), :]
    load = lambda c, r: rows_ref[c, r]
    pitchwise(load, vrows_ref, weight_ref[0], part_ref, rate_ref, near_ref, lower_ref)


def cells_pitchwise_kernel(
    weight_ref, vrows_ref, raw_ref, rows_ref, part_ref, rate_ref, near_ref, lower_ref, half_ref
):
    rows_from(raw_ref, half_ref, rows_ref)
    load = lambda c, r: rows_ref[c, r]
    pitchwise(load, vrows_ref, weight_ref[0], part_ref, rate_ref, near_ref, lower_ref)


def pitchwise(load, vrows_ref, omega, part_ref, rate_ref, near_ref, lower_ref):
    pitchwise_shifts(load, near_ref)
    for r in range(8):
        q = [load(c, r) for c in range(COMPS)]
        u, v, p = primitives(q)
        upper, lower = pitchwise_faces(q, v, p, near_ref, r)
        rate_ref[r] = own_instance_rate(jnp.abs(u) + jnp.abs(v), vrows_ref[r], omega)
        for c in range(COMPS):
            part_ref[c, r] = upper[c]
            lower_ref[c, r] = lower[c]
    for r in range(8):
        for c in range(COMPS):
            part_ref[c, r] = part_ref[c, r] - turn(lower_ref[c, r], 1)


def outer_kernel(
    cap, table_ref, weight_ref, rows_ref, vrows_ref, part_ref, rate_ref, halo_ref, sibling_ref,
    outer_ref, *sends
):
    omega, w_own, w_across, w_near, w_far = coefficients(weight_ref)
    load = row_loader(lambda c, r: rows_ref[c, r], halo_ref)
    even = even_tiles(vrows_ref.shape[1:])
    low = {r: load(r) for r in range(-2, 4)}
    high = {r: load(r) for r in range(4, 10)}
    picked = {
        k: [jnp.where(even, a, b) for a, b in zip(low[k - 2], high[k + 4])] for k in range(6)
    }
    rows = Rows(lambda k: picked[k])
    for l in range(2):
        along = rows.along(l + 2)
        volume = jnp.where(even, vrows_ref[l], vrows_ref[l + 6])
        rate = jnp.where(even, rate_ref[l], rate_ref[l + 6])
        outer_ref[COMPS, l] = rate * volume
        for c in range(COMPS):
            q = picked[l + 2][c]
            part = jnp.where(even, part_ref[c, l], part_ref[c, l + 6])
            sibling = jnp.where(even, sibling_ref[c, l], sibling_ref[c, l + 6])
            spectral = w_own * q + w_near * sibling
            outer_ref[c, l] = q - rate * (along[c] + part + volume * spectral)
    pack_sends(cap, outer_ref, table_ref, sends, range(POOLED))


def near_rows(weight_ref, vrows_ref, of, rows):
    omega, w_own, w_across, w_near, w_far = coefficients(weight_ref)
    for weight, (one, part, rate_of, halo, out, gain), other in (
        (w_near, of[0], of[1][0]), (w_far, of[1], of[0][0])
    ):
        load = lambda c, r: one[c, r]
        if halo is None:
            line = Rows(lambda r: [one[c, r] for c in range(COMPS)])
        else:
            line = Rows(row_loader(load, halo))
        for r in rows:
            along, volume, rate = line.along(r), vrows_ref[r], rate_of[r]
            for c in range(COMPS):
                spectral = w_own * one[c, r] + weight * other[c, r]
                out[c, r] = one[c, r] - rate * (along[c] + part[c, r] + volume * spectral)
        if halo is None:
            for r in range(8):
                gain[r] = rate_of[r] * vrows_ref[r]


def near_inner_kernel(
    weight_ref, vrows_ref, rows_ref, part_ref, rate_ref,
    sibling_ref, sibling_part_ref, sibling_rate_ref,
    next_ref, sibling_next_ref, gain_ref, sibling_gain_ref
):
    near_rows(weight_ref, vrows_ref, (
        (rows_ref, part_ref, rate_ref, None, next_ref, gain_ref),
        (sibling_ref, sibling_part_ref, sibling_rate_ref, None, sibling_next_ref, sibling_gain_ref),
    ), range(2, 6))


def near_outer_kernel(
    weight_ref, vrows_ref, rows_ref, part_ref, rate_ref, halo_ref,
    sibling_ref, sibling_part_ref, sibling_rate_ref, sibling_halo_ref, _, __, ___,
    next_ref, sibling_next_ref
):
    near_rows(weight_ref, vrows_ref, (
        (rows_ref, part_ref, rate_ref, halo_ref, next_ref, None),
        (sibling_ref, sibling_part_ref, sibling_rate_ref, sibling_halo_ref, sibling_next_ref, None),
    ), (0, 1, 6, 7))


def across_kernel(
    weight_ref, vrows_ref, rows_ref, sibling_ref, own_ref, own_gain_ref, sibling_next_ref,
    sibling_gain_ref, raw_ref, halo_ref,
    next_ref, term_ref, across_ref, lacking_ref, gain_ref,
    near_ref, lower_ref, half_ref, part_ref, rate_ref
):
    omega, w_own, w_across, w_near, w_far = coefficients(weight_ref)
    rows_from(raw_ref, half_ref, across_ref)
    load = lambda c, r: across_ref[c, r]
    pitchwise(load, vrows_ref, omega, part_ref, rate_ref, near_ref, lower_ref)
    rows = Rows(row_loader(load, halo_ref))
    for r in range(8):
        along, volume, rate = rows.along(r), vrows_ref[r], rate_ref[r]
        own_gain, sibling_gain, gain = own_gain_ref[r], sibling_gain_ref[r], rate * volume
        gain_ref[r] = (
            (w_own * w_far) * own_gain + (w_near * w_across) * sibling_gain + (w_across * w_near) * gain
        )
        lacking_ref[r] = w_far * own_gain
        for c in range(COMPS):
            q = across_ref[c, r]
            spectral = w_own * q + w_across * rows_ref[c, r] + w_far * sibling_ref[c, r]
            new = q - rate * (along[c] + part_ref[c, r] + volume * spectral)
            mine = own_ref[c, r] - (w_across * own_gain) * q
            sibling = sibling_next_ref[c, r] - (w_near * sibling_gain) * q
            next_ref[c, r] = mine
            term_ref[c, r] = w_own * mine + w_near * sibling + w_across * new


def far_kernel(
    weight_ref, vrows_ref, rows_ref, sibling_ref, across_ref, own_ref, partial_ref,
    lacking_ref, lacking_term_ref, far_ref, part_ref, rate_ref, *more
):
    halos, (next_ref, term_ref, halo_ref) = more[:-3], more[-3:]
    omega, w_own, w_across, w_near, w_far = coefficients(weight_ref)
    join_halos(halos, halo_ref)
    rows = Rows(row_loader(lambda c, r: far_ref[c, r], halo_ref))
    for r in range(8):
        along, volume, rate = rows.along(r), vrows_ref[r], rate_ref[r]
        lacking, lacking_term = lacking_ref[r], lacking_term_ref[r]
        for c in range(COMPS):
            q = far_ref[c, r]
            spectral = (
                w_own * q + w_across * sibling_ref[c, r] + w_near * rows_ref[c, r]
                + w_far * across_ref[c, r]
            )
            new = q - rate * (along[c] + part_ref[c, r] + volume * spectral)
            next_ref[c, r] = own_ref[c, r] - lacking * q
            term_ref[c, r] = partial_ref[c, r] - lacking_term * q + w_far * new


def join_halos(parts, halo_ref):
    tiles = [part[pl.ds(row, 8), :] for part in parts for row in range(0, part.shape[0], 8)]
    for n, tile in enumerate(tiles):
        halo_ref[n // 2, n % 2] = tile


def last_kernel(
    space_total, cap, table_ref, index_ref, weight_ref, rows_ref, vrows_ref, part_ref, rate_ref,
    term_ref, outer_ref, across_ref, *more
):
    received, halos = more[: space_total - 1], more[space_total - 1 : -10]
    new_ref, residual_ref, new_half_ref, residual_half_ref, inverse_ref, left = more[-10:-4]
    halo_ref, pool_ref, raw_ref, far_ref = more[-4:]
    next_halos(
        space_total, cap, table_ref, index_ref, weight_ref, outer_ref, across_ref, halos, received,
        halo_ref, pool_ref, raw_ref, far_ref,
    )
    own = Rows(row_loader(lambda c, r: rows_ref[c, r], halo_ref))
    live_slots = table_ref[3 * FACES]
    live = (lax.broadcasted_iota(jnp.int32, vrows_ref.shape[1:], 0) // 2) < live_slots
    for r in range(8):
        inverse_ref[r] = 1.0 / vrows_ref[r]
    copies = []
    for c in range(COMPS):
        for r in range(8):
            residual = part_ref[c, r] + own.along_one(c, r) + vrows_ref[r] * term_ref[c, r]
            new = jnp.where(live, own.q(r)[c] - rate_ref[r] * residual, 0.0)
            scaled = jnp.where(live, residual * inverse_ref[r], 0.0)
            for h in range(2):
                lanes = slice(128 * h, 128 * h + 128)
                new_half_ref[c, h, pl.ds(r, 8, stride=8), :] = new[:, lanes]
                residual_half_ref[c, h, pl.ds(r, 8, stride=8), :] = scaled[:, lanes]
        for n, (half_ref, out_ref) in enumerate(
            [(new_half_ref, new_ref), (residual_half_ref, residual_ref)]
        ):
            for h in range(2):
                copy = pltpu.make_async_copy(
                    half_ref.at[c, h], out_ref.at[c, :, pl.ds(128 * h, 128)], left.at[len(copies)]
                )
                copy.start()
                copies.append(copy)
    for copy in copies:
        copy.wait()


def after_kernel(value_ref, *more):
    pass


def four_instances(
    flow_state, cell_volume, frequency, block_count, block_place, face_links, face_offset, face_flip
):
    _, comps, row_count, width = flow_state.shape
    space_total = lax.axis_size("space")
    block_total = block_place.shape[0]
    cap = pair_cap(space_total, block_total)
    state = flow_state[0]

    def over_inst(x, flip):
        return lax.ppermute(x, "inst", [(i, i ^ flip) for i in range(4)])

    def over_space(parts):
        arrived = {
            k: lax.ppermute(
                parts[k - 1], "space", [(i, partner(i, k, space_total)) for i in range(space_total)]
            )
            for k in exchanges(space_total)
        }
        return [arrived[k] for k in exchanges(space_total)]

    full = (comps, 8, 8, width)
    outer = (comps, 2, 8, width)
    plane = (8, 8, width)
    pooled = (POOLED, 2, 8, width)
    on_chip = lambda shape, dtype=F32: pltpu.VMEM(shape, dtype)
    sends_shape = lambda n: [on_chip((n * 2 * cap, width)) for _ in range(space_total - 1)]
    shifts = [pltpu.VMEM((3,) + full, F32), pltpu.VMEM(full, F32)]

    def call(kernel, out, specs, args, scratch=(), micros=0.3, out_specs=None, aliases={}):
        args = [
            pltpu.with_memory_space_constraint(x, spec.memory_space) for spec, x in zip(specs, args)
        ]
        return pl.pallas_call(
            kernel,
            out_shape=out,
            in_specs=specs,
            out_specs=out_specs or jax.tree.map(lambda _: VMEM, out),
            scratch_shapes=list(scratch),
            input_output_aliases=aliases,
            compiler_params=pltpu.CompilerParams(vmem_limit_bytes=12 << 20),
            cost_estimate=pl.CostEstimate(
                flops=0, bytes_accessed=int(micros * 3.69e6), transcendentals=0
            ),
        )(*args)

    tables = (block_count, block_place, face_links.T, face_offset.T, face_flip.T)
    in_smem = lambda *shape: pltpu.SMEM(shape, jnp.int32)
    small = [in_smem(space_total), in_smem(block_total)] + [in_smem(2, block_total)] * 3
    derived = [in_smem(space_total), in_smem(block_total)]
    half, volume_half, outer_rows, send_table, *sends = call(
        functools.partial(pack_kernel, space_total, block_total, cap),
        [
            on_chip((2, comps, row_count, 128)), on_chip((2, row_count, 128)), on_chip(outer),
            in_smem((space_total - 1) * cap), *sends_shape(comps),
        ],
        [HBM] * 5,
        (state, cell_volume, *tables[:3]),
        scratch=[pltpu.SemaphoreType.DMA((5 + 2 * comps,)), *small[:3], *derived],
        micros=1.0,
        out_specs=[VMEM] * 3 + [SMEM] + [VMEM] * (space_total - 1),
    )
    rows, vrows, table, index = call(
        functools.partial(rows_kernel, space_total, block_total, cap),
        [on_chip(full), on_chip(plane), in_smem(3 * FACES + 1), on_chip((FACES, width), jnp.int32)],
        [VMEM] * 2 + [HBM] * 5,
        (half, volume_half, *tables),
        scratch=[pltpu.SemaphoreType.DMA((5,)), *small, *derived],
        micros=1.0,
        out_specs=[VMEM] * 2 + [SMEM, VMEM],
    )
    weights = pl.pallas_call(
        weight_kernel, out_shape=pltpu.SMEM((8,), F32), in_specs=[SMEM], out_specs=SMEM
    )(frequency)
    halves = [pltpu.VMEM((comps, 2, row_count, 128), F32), pltpu.VMEM(full, F32)]
    pool = [
        pltpu.VMEM(((space_total - 1) * POOLED * 2 * cap + POOLED * 2 * FACES, width), F32),
        pltpu.VMEM(pooled, F32),
    ]

    def pitch(x, *first):
        return call(
            pitchwise_kernel,
            [on_chip(full), on_chip(plane)],
            [SMEM] + [VMEM] * (2 + len(first)),
            (weights, x, vrows, *first),
            scratch=shifts,
            micros=0.5,
        )

    across = over_inst(state, 2)
    sibling_halves = [over_inst(half[h], 1) for h in range(2)]
    received = over_space(sends)
    part, rate = pitch(rows)
    sibling, sibling_part, sibling_rate = call(
        halves_pitchwise_kernel,
        [on_chip(full)] * 2 + [on_chip(plane)],
        [SMEM] + [VMEM] * 3,
        (weights, vrows, *sibling_halves),
        scratch=shifts,
        micros=0.5,
    )
    own, sibling_next, own_gain, sibling_gain = call(
        near_inner_kernel,
        [on_chip(full)] * 2 + [on_chip(plane)] * 2,
        [SMEM] + [VMEM] * 7,
        (weights, vrows, rows, part, rate, sibling, sibling_part, sibling_rate),
        micros=0.3,
    )
    halo = call(
        functools.partial(halo_kernel, space_total, cap),
        on_chip(outer),
        [SMEM] + [VMEM] * (3 + space_total),
        (table, index, outer_rows, own_gain, sibling_gain, *received),
        scratch=pool,
    )
    across_halo = over_inst(halo, 2)
    sibling_halo = over_inst(halo, 1)
    next_outer, *next_sends = call(
        functools.partial(outer_kernel, cap),
        [on_chip(pooled), *sends_shape(POOLED)],
        [SMEM, SMEM] + [VMEM] * 6,
        (send_table, weights, rows, vrows, part, rate, halo, sibling),
        micros=0.3,
    )
    next_received = over_space(next_sends)
    def after(x, *first):
        return call(
            after_kernel, on_chip(x.shape), [VMEM] * (1 + len(first)), (x, *first), aliases={0: 0}, micros=0.05
        )

    far = over_inst(after(across, next_outer), 1)
    stacked = across_halo.reshape(comps * 2 * 8, width)
    far_halo = [over_inst(x, 1) for x in (stacked[:16], stacked[16:56], stacked[56:])]
    far_rows, far_part, far_rate = call(
        cells_pitchwise_kernel,
        [on_chip(full)] * 2 + [on_chip(plane)],
        [SMEM] + [VMEM] * 2,
        (weights, vrows, far),
        scratch=shifts + halves[:1],
        micros=0.6,
    )
    own, sibling_next = call(
        near_outer_kernel,
        [on_chip(full)] * 2,
        [SMEM] + [VMEM] * 12,
        (weights, vrows, rows, part, rate, halo, sibling, sibling_part, sibling_rate, sibling_halo,
         far_rate, own, sibling_next),
        micros=0.4,
        aliases={11: 0, 12: 1},
    )
    own, partial, across_rows, lacking, lacking_term = call(
        across_kernel,
        [on_chip(full)] * 3 + [on_chip(plane)] * 2,
        [SMEM] + [VMEM] * 9,
        (weights, vrows, rows, sibling, own, own_gain, sibling_next, sibling_gain, across, across_halo),
        scratch=shifts + halves[:1] + [halves[1], pltpu.VMEM(plane, F32)],
        micros=1.0,
    )
    next_rows, term = call(
        far_kernel,
        [on_chip(full)] * 2,
        [SMEM] + [VMEM] * (11 + len(far_halo)),
        (weights, vrows, rows, sibling, across_rows, own, partial, lacking, lacking_term,
         far_rows, far_part, far_rate, *far_halo),
        scratch=[pltpu.VMEM(outer, F32)],
        micros=0.5,
    )
    next_part, next_rate = pitch(next_rows)
    new, residual = call(
        functools.partial(last_kernel, space_total, cap),
        [jax.ShapeDtypeStruct(state.shape, F32)] * 2,
        [SMEM, VMEM, SMEM] + [VMEM] * (6 + space_total + len(far_halo)),
        (table, index, weights, next_rows, vrows, next_part, next_rate, term, next_outer,
         across_halo, *next_received, *far_halo),
        scratch=[pltpu.VMEM((comps, 2, row_count, 128), F32)] * 2
        + [pltpu.VMEM(plane, F32), pltpu.SemaphoreType.DMA((4 * comps,)), pltpu.VMEM(outer, F32)]
        + pool + [pltpu.VMEM(outer, F32)],
        micros=1.5,
        out_specs=[HBM] * 2,
    )
    return new[None], residual[None]


def spectral_matrix(instance_total, omega_value):
    position = jnp.arange(instance_total, dtype=jnp.int32)
    distance = (position[:, None] - position[None, :]) % instance_total
    parity = (1 - 2 * (distance % 2)).astype(jnp.float32)
    phase_angle = jnp.pi * distance.astype(jnp.float32) / instance_total
    safe_angle = jnp.where(distance == 0, 0.5 * jnp.pi, phase_angle)
    first_derivative = jnp.where(
        distance == 0, 0.0, 0.5 * parity * jnp.cos(safe_angle) / jnp.sin(safe_angle)
    )
    second_derivative = jnp.where(
        distance == 0,
        -(instance_total * instance_total + 2) / 12.0,
        -parity / (2.0 * jnp.sin(safe_angle) ** 2),
    )
    return omega_value * (first_derivative - TIME_VISCOSITY * second_derivative)


def block_tables(
    block_count, block_place, face_links, face_offset, face_flip, targets, slot_count, width
):
    block_total = block_place.shape[0]
    first_position = jnp.cumsum(block_count) - block_count
    block_at_position = (
        jnp.zeros((block_total,), jnp.int32)
        .at[block_place]
        .set(jnp.arange(block_total, dtype=jnp.int32))
    )
    owner_device = jnp.sum(
        (block_place[:, None] >= first_position[None, 1:]).astype(jnp.int32), axis=1
    )
    flat_slot = owner_device * slot_count + block_place - first_position[owner_device]
    target_device = targets // slot_count
    target_slot = targets % slot_count
    is_live = target_slot < block_count[target_device]
    block_index = block_at_position[
        jnp.clip(first_position[target_device] + target_slot, 0, block_total - 1)
    ]
    neighbour = face_links[block_index]
    source_slot = jnp.where(neighbour >= 0, flat_slot[jnp.clip(neighbour, 0, block_total - 1)], -1)
    column = jnp.arange(width, dtype=jnp.int32)
    flipped = face_flip[block_index][:, :, None]
    ordered = jnp.where(flipped == 1, width - 1 - column, column)
    column_index = (face_offset[block_index][:, :, None] + ordered) % width
    return (is_live, source_slot, column_index)


def attach_halos(blocks, lower, upper, source_slot):
    cells_i = blocks.shape[2]
    lower = jnp.where(
        (source_slot[:, 0] >= 0)[None, :, None, None],
        lower,
        jnp.repeat(blocks[:, :, 0:1], 2, axis=2),
    )
    upper = jnp.where(
        (source_slot[:, 1] >= 0)[None, :, None, None],
        upper,
        jnp.repeat(blocks[:, :, cells_i - 1 : cells_i], 2, axis=2),
    )
    return jnp.concatenate([lower, blocks, upper], axis=2)


def fluxes(conserved):
    inverse_rho = 1.0 / conserved[0]
    velocity_i = conserved[1] * inverse_rho
    velocity_j = conserved[2] * inverse_rho
    pressure = (HEAT_RATIO - 1.0) * (
        conserved[4]
        - 0.5
        * (conserved[1] * conserved[1] + conserved[2] * conserved[2] + conserved[3] * conserved[3])
        * inverse_rho
    )
    flux_i = jnp.stack(
        [
            conserved[1],
            conserved[1] * velocity_i + pressure,
            conserved[2] * velocity_i,
            conserved[3] * velocity_i,
            (conserved[4] + pressure) * velocity_i,
            conserved[5] * velocity_i,
        ]
    )
    flux_j = jnp.stack(
        [
            conserved[2],
            conserved[1] * velocity_j,
            conserved[2] * velocity_j + pressure,
            conserved[3] * velocity_j,
            (conserved[4] + pressure) * velocity_j,
            conserved[5] * velocity_j,
        ]
    )
    return (flux_i, flux_j, jnp.abs(velocity_i), jnp.abs(velocity_j))


def advance(extended, volumes, spectral, omega_value, instance_total):
    cells_i = extended.shape[2] - 4
    flux_i, flux_j, speed_i, speed_j = fluxes(extended)
    left_cell = extended[:, :, 1 : cells_i + 2]
    right_cell = extended[:, :, 2 : cells_i + 3]
    back_cell = extended[:, :, 0 : cells_i + 1]
    ahead_cell = extended[:, :, 3 : cells_i + 4]
    radius_i = 0.5 * (speed_i[:, 1 : cells_i + 2] + speed_i[:, 2 : cells_i + 3]) + SOUND_SPEED
    face_i = 0.5 * (flux_i[:, :, 1 : cells_i + 2] + flux_i[:, :, 2 : cells_i + 3]) - radius_i * (
        SECOND_DISSIPATION * (right_cell - left_cell)
        - FOURTH_DISSIPATION * (ahead_cell - 3.0 * right_cell + 3.0 * left_cell - back_cell)
    )
    centre = extended[:, :, 2 : cells_i + 2]
    centre_flux = flux_j[:, :, 2 : cells_i + 2]
    centre_speed = speed_j[:, 2 : cells_i + 2]
    next_cell = jnp.roll(centre, -1, axis=-1)
    prior_cell = jnp.roll(centre, 1, axis=-1)
    far_cell = jnp.roll(centre, -2, axis=-1)
    radius_j = 0.5 * (centre_speed + jnp.roll(centre_speed, -1, axis=-1)) + SOUND_SPEED
    face_j = 0.5 * (centre_flux + jnp.roll(centre_flux, -1, axis=-1)) - radius_j * (
        SECOND_DISSIPATION * (next_cell - centre)
        - FOURTH_DISSIPATION * (far_cell - 3.0 * next_cell + 3.0 * centre - prior_cell)
    )
    residual_sum = (
        face_i[:, :, 1:]
        - face_i[:, :, :-1]
        + (face_j - jnp.roll(face_j, 1, axis=-1))
        + volumes * spectral
    )
    step_rate = COURANT / (
        speed_i[:, 2 : cells_i + 2]
        + centre_speed
        + 2.0 * SOUND_SPEED
        + volumes * omega_value * 0.5 * instance_total
    )
    return (centre - step_rate * residual_sum, residual_sum / volumes)


def select_faces(selector, slabs):
    return jnp.einsum("tf,lcfxw->lctxw", selector, slabs, precision=lax.Precision.HIGHEST)


def orient_faces(slabs, permuter):
    return jnp.einsum("lctxw,tvw->lctxv", slabs, permuter, precision=lax.Precision.HIGHEST)


def on_device(
    flow_state, cell_volume, frequency, block_count, block_place, face_links, face_offset, face_flip
):
    local_count, comps, row_count, width = flow_state.shape
    slot_count = BLOCKS_MAX
    cells_i = row_count // slot_count
    space_total = lax.axis_size("space")
    space_index = lax.axis_index("space")
    targets = space_index * slot_count + jnp.arange(slot_count, dtype=jnp.int32)
    is_live, source_slot, column_index = block_tables(
        block_count, block_place, face_links, face_offset, face_flip, targets, slot_count, width
    )
    column = jnp.arange(width, dtype=jnp.int32)
    permuter = (
        column_index.reshape(slot_count * 2, width)[:, :, None] == column[None, None, :]
    ).astype(jnp.float32)
    side_index = jnp.arange(2, dtype=jnp.int32)[None, :]
    volumes = cell_volume.reshape(slot_count, cells_i, width)
    instance_total = local_count * lax.axis_size("inst")
    matrix = spectral_matrix(instance_total, frequency[0])
    row_offset = lax.axis_index("inst") * local_count
    own_rows = lax.dynamic_slice_in_dim(matrix, row_offset, local_count, 0)
    wanted_face = (source_slot * 2 + (1 - side_index)).reshape(-1)
    face_range = jnp.arange(space_total * slot_count * 2, dtype=jnp.int32)
    selector = (
        (wanted_face[:, None] == face_range[None, :]) & (source_slot.reshape(-1)[:, None] >= 0)
    ).astype(jnp.float32)
    current = flow_state
    last_residual = jnp.zeros_like(flow_state)
    for iteration in range(PSEUDO_STEPS):
        spectral_all = jnp.einsum(
            "nm,mcrb->ncrb",
            own_rows,
            lax.all_gather(current, "inst", axis=0, tiled=True),
            precision=lax.Precision.HIGHEST,
        )
        blocks = current.reshape(local_count, comps, slot_count, cells_i, width)
        faces = jnp.stack([blocks[:, :, :, 0:2], blocks[:, :, :, cells_i - 2 : cells_i]], axis=3)
        gathered = lax.all_gather(faces, "space", axis=2, tiled=True)
        gathered = gathered.reshape(local_count, comps, space_total * slot_count * 2, 2, width)
        arrived = select_faces(selector, gathered)
        oriented = orient_faces(arrived, permuter).reshape(
            local_count, comps, slot_count, 2, 2, width
        )

        def one_instance(own_blocks, slabs, spectral):
            extended = attach_halos(own_blocks, slabs[:, :, 0], slabs[:, :, 1], source_slot)
            return advance(
                extended,
                volumes,
                spectral.reshape(comps, slot_count, cells_i, width),
                frequency[0],
                instance_total,
            )

        updated, residual_now = jax.vmap(one_instance)(blocks, oriented, spectral_all)
        current = updated.reshape(flow_state.shape)
        last_residual = residual_now.reshape(flow_state.shape)
    row_live = jnp.repeat(is_live, cells_i)[None, None, :, None]
    return (jnp.where(row_live, current, 0.0), jnp.where(row_live, last_residual, 0.0))


def solution(mesh):
    return jax.shard_map(
        four_instances if mesh.shape["inst"] == 4 else on_device,
        mesh=mesh,
        in_specs=(
            P(("groups", "inst"), None, "space", None),
            P(("groups", "space"), None),
            P(),
            P("groups"),
            P("groups"),
            P("groups", None),
            P("groups", None),
            P("groups", None),
        ),
        out_specs=(
            P(("groups", "inst"), None, "space", None),
            P(("groups", "inst"), None, "space", None),
        ),
        check_vma=False,
    )
```
